32 devices in a mesh: page: 16 (over z, y, core), strip: 2 (over x).
Axes of the slice: x: 2, y: 2, z: 4, core: 2. Of those that a mesh axis runs over, the one named last changes fastest.
Arguments:
- features: bfloat16 [16, 32, 32, 512], P('page', 'strip'), may hold values from -6 to 6
- quarter_turns: int32 [16], P('page'), may hold values from 0 to 3, as said below
- heights: int32 [16], P('page'), may hold values from 8 to 32, as said below
- widths: int32 [16], P('page'), may hold values from 8 to 32, as said below
- frozen_scale: float32 [2, 512], replicated, may hold values from 0.5 to 2
- frozen_shift: float32 [2, 512], replicated, may hold values from -3 to 3
- first_kernel: bfloat16 [3, 3, 512, 512], replicated, may hold values from -0.09375 to 0.09375
- second_kernel: bfloat16 [3, 3, 512, 512], replicated, may hold values from -0.09375 to 0.09375
- project_weight: bfloat16 [512, 256], replicated, may hold values from -0.25 to 0.25
- project_bias: float32 [256], replicated, may hold values from -3 to 3
- query_weight: bfloat16 [256, 256], replicated, may hold values from -0.375 to 0.375
- query_bias: float32 [256], replicated, may hold values from -3 to 3
- key_weight: bfloat16 [256, 256], replicated, may hold values from -0.375 to 0.375
- value_weight: bfloat16 [256, 256], replicated, may hold values from -0.375 to 0.375
- value_bias: float32 [256], replicated, may hold values from -3 to 3
- output_weight: bfloat16 [256, 256], replicated, may hold values from -1.5 to 1.5
- output_bias: float32 [256], replicated, may hold values from -3 to 3
- first_gain: float32 [256], replicated, may hold values from 0.1 to 1.9
- first_shift: float32 [256], replicated, may hold values from -3 to 3
- expand_weight: bfloat16 [256, 2048], replicated, may hold values from -0.375 to 0.375
- expand_bias: float32 [2048], replicated, may hold values from -3 to 3
- shrink_weight: bfloat16 [2048, 256], replicated, may hold values from -0.125 to 0.125
- shrink_bias: float32 [256], replicated, may hold values from -3 to 3
- final_gain: float32 [256], replicated, may hold values from 0.1 to 1.9
- final_shift: float32 [256], replicated, may hold values from -3 to 3
- cotangent: bfloat16 [16, 32, 32, 256], P('page', 'strip'), may hold values from -6 to 6
Outputs:
- encoded: bfloat16 [16, 32, 32, 256], P('page', 'strip')
- features_grad: float32 [16, 32, 32, 512], P('page', 'strip')
- first_kernel_grad: float32 [3, 3, 512, 512], P(None, None, 'page', 'strip')
- second_kernel_grad: float32 [3, 3, 512, 512], P(None, None, 'page', 'strip')
- project_weight_grad: float32 [512, 256], replicated
- project_bias_grad: float32 [256], replicated
- query_weight_grad: float32 [256, 256], replicated
- query_bias_grad: float32 [256], replicated
- key_weight_grad: float32 [256, 256], replicated
- value_weight_grad: float32 [256, 256], replicated
- value_bias_grad: float32 [256], replicated
- output_weight_grad: float32 [256, 256], replicated
- output_bias_grad: float32 [256], replicated
- first_gain_grad: float32 [256], replicated
- first_shift_grad: float32 [256], replicated
- expand_weight_grad: float32 [256, 2048], replicated
- expand_bias_grad: float32 [2048], replicated
- shrink_weight_grad: float32 [2048, 256], replicated
- shrink_bias_grad: float32 [256], replicated
- final_gain_grad: float32 [256], replicated
- final_shift_grad: float32 [256], replicated
The draws below stay inside these ranges and needn't reach their ends.
Inputs may be any that keep to these rules, and one draw needn't show every extreme that they name: `quarter_turns`: in every block of 1 consecutive pages one page, drawn from the seed, has valid cells in every stored row: its height is 32 and its quarter turns are 0 or 2, or its width is 32 and its quarter turns are 1 or 3. `heights`: drawn together with quarter_turns and widths as stated there. `widths`: drawn together with quarter_turns and heights as stated there.
All inputs are finite; a program needn't handle non-finite values.
Results may differ from the reference program's by a relative error of at most 0.035.
Values may be sent and summed in bfloat16 or wider, within the bound.
A program may use at most 128 MiB of HBM per device.

```python
import math
import jax
import jax.numpy as jnp
from jax import lax

C = 512
D = 256
HEADS = 8
FF = 2048
S = 32
PAGES = 1
P_TOT = 16


def page_layout(key):
    groups = P_TOT // PAGES
    pick = jax.random.randint(jax.random.fold_in(key, 101), (groups,), 0, PAGES)
    chosen = jnp.arange(P_TOT) % PAGES == jnp.repeat(pick, PAGES, total_repeat_length=P_TOT)
    flip = jax.random.randint(jax.random.fold_in(key, 102), (P_TOT,), 0, 2)
    half_turn = jax.random.randint(jax.random.fold_in(key, 103), (P_TOT,), 0, 2)
    free_turns = jax.random.randint(jax.random.fold_in(key, 104), (P_TOT,), 0, 4)
    drawn_h = jax.random.randint(jax.random.fold_in(key, 105), (P_TOT,), S // 4, S + 1)
    drawn_w = jax.random.randint(jax.random.fold_in(key, 106), (P_TOT,), S // 4, S + 1)
    turns = jnp.where(chosen, 2 * half_turn + flip, free_turns)
    heights = jnp.where(chosen & (flip == 0), S, drawn_h)
    widths = jnp.where(chosen & (flip == 1), S, drawn_w)
    return (turns.astype(jnp.int32), heights.astype(jnp.int32), widths.astype(jnp.int32))


def draw_quarter_turns(key, part):
    return page_layout(key)[0]


def draw_heights(key, part):
    return page_layout(key)[1]


def draw_widths(key, part):
    return page_layout(key)[2]


def steps_of(stream_key, shape, shards, smallest, largest):
    def one(dim, blocks):
        steps = jax.random.uniform(jax.random.fold_in(jax.random.fold_in(stream_key, 6), dim), (blocks,), jnp.float32, smallest / len(shards), largest / len(shards))
        return jnp.repeat(jnp.exp(steps), shape[dim] // blocks).reshape((-1,) + (1,) * (len(shape) - dim - 1))

    factor_of = one(*shards[0])
    for cut in shards[1:]:
        factor_of = factor_of * one(*cut)
    return factor_of


def bell_draw(key, dims, scale, bound, cuts=(), kind=jnp.bfloat16):
    values = scale * jax.random.normal(key, dims, jnp.float32)
    if cuts:
        values = values * steps_of(key, dims, cuts, -0.22, 0.18)
    return jnp.clip(values, -bound, bound).astype(kind)


def setup_inputs(seed: int = 0) -> dict:
    streams_of = jax.random.split(jax.random.key(seed), 27)
    features = bell_draw(streams_of[0], (P_TOT, S, S, C), 1.0, 6.0, ((0, 16), (1, 2)))
    quarter_turns = draw_quarter_turns(jax.random.fold_in(streams_of[26], 71), 0)
    heights = draw_heights(jax.random.fold_in(streams_of[26], 71), 0)
    widths = draw_widths(jax.random.fold_in(streams_of[26], 71), 0)
    frozen_scale = jnp.clip(jnp.exp(jax.random.uniform(streams_of[4], (2, C), jnp.float32, math.log(0.5), math.log(2.0))), 0.5, 2.0)
    frozen_shift = bell_draw(streams_of[5], (2, C), 0.5, 3.0, (), jnp.float32)
    first_kernel = bell_draw(streams_of[6], (3, 3, C, C), (9 * C) ** -0.5, 0.09375)
    second_kernel = bell_draw(streams_of[7], (3, 3, C, C), (9 * C) ** -0.5, 0.09375)
    project_weight = bell_draw(streams_of[8], (C, D), C ** -0.5, 0.25)
    project_bias = bell_draw(streams_of[9], (D,), 0.5, 3.0, (), jnp.float32)
    query_weight = bell_draw(streams_of[10], (D, D), D ** -0.5, 0.375)
    query_bias = bell_draw(streams_of[11], (D,), 0.5, 3.0, (), jnp.float32)
    key_weight = bell_draw(streams_of[12], (D, D), D ** -0.5, 0.375)
    value_weight = bell_draw(streams_of[13], (D, D), D ** -0.5, 0.375)
    value_bias = bell_draw(streams_of[14], (D,), 0.5, 3.0, (), jnp.float32)
    output_weight = bell_draw(streams_of[15], (D, D), (D // 16) ** -0.5, 1.5)
    output_bias = bell_draw(streams_of[16], (D,), 0.5, 3.0, (), jnp.float32)
    first_gain = jnp.clip(1.0 + 0.18 * jax.random.normal(streams_of[17], (D,), jnp.float32), 0.1, 1.9)
    first_shift = bell_draw(streams_of[18], (D,), 0.5, 3.0, (), jnp.float32)
    expand_weight = bell_draw(streams_of[19], (D, FF), D ** -0.5, 0.375)
    expand_bias = bell_draw(streams_of[20], (FF,), 0.5, 3.0, (), jnp.float32)
    shrink_weight = bell_draw(streams_of[21], (FF, D), FF ** -0.5, 0.125)
    shrink_bias = bell_draw(streams_of[22], (D,), 0.5, 3.0, (), jnp.float32)
    final_gain = jnp.clip(1.0 + 0.18 * jax.random.normal(streams_of[23], (D,), jnp.float32), 0.1, 1.9)
    final_shift = bell_draw(streams_of[24], (D,), 0.5, 3.0, (), jnp.float32)
    cotangent = bell_draw(streams_of[25], (P_TOT, S, S, D), 1.0, 6.0, ((0, 16), (1, 2)))
    return {"features": features, "quarter_turns": quarter_turns, "heights": heights, "widths": widths, "frozen_scale": frozen_scale, "frozen_shift": frozen_shift, "first_kernel": first_kernel, "second_kernel": second_kernel, "project_weight": project_weight, "project_bias": project_bias, "query_weight": query_weight, "query_bias": query_bias, "key_weight": key_weight, "value_weight": value_weight, "value_bias": value_bias, "output_weight": output_weight, "output_bias": output_bias, "first_gain": first_gain, "first_shift": first_shift, "expand_weight": expand_weight, "expand_bias": expand_bias, "shrink_weight": shrink_weight, "shrink_bias": shrink_bias, "final_gain": final_gain, "final_shift": final_shift, "cotangent": cotangent}


@jax.custom_vjp
def low(v):
    return lax.optimization_barrier(v.astype(jnp.bfloat16)).astype(jnp.float32)

@jax.custom_vjp
def low_back(v):
    return v

def low_keep(v):
    return (low(v), None)

def low_pass(kept, grad):
    return (grad,)

def back_keep(v):
    return (v, None)

def back_low(kept, grad):
    return (low(grad),)
low.defvjp(low_keep, low_pass)
low_back.defvjp(back_keep, back_low)

def gelu_exact(v):
    return jax.nn.gelu(v, approximate=False)

def layer_norm(v, gain, shift):
    center = v - lax.optimization_barrier(jnp.mean(v, axis=-1, keepdims=True))
    spread = lax.optimization_barrier(jnp.mean(center * center, axis=-1, keepdims=True))
    return center * lax.rsqrt(spread + 1e-05) * gain + shift

def sine_positions(turns, heights, widths, row_start, rows, side, width):
    row = row_start + jnp.arange(rows, dtype=jnp.int32)[None, :, None]
    column = jnp.arange(side, dtype=jnp.int32)[None, None, :]
    turn = turns[:, None, None]
    upright_y = jnp.where(turn == 0, row, jnp.where(turn == 1, column, jnp.where(turn == 2, side - 1 - row, side - 1 - column)))
    upright_x = jnp.where(turn == 0, column, jnp.where(turn == 1, side - 1 - row, jnp.where(turn == 2, side - 1 - column, row)))
    valid = (upright_y < heights[:, None, None]) & (upright_x < widths[:, None, None])
    half = width // 2
    index = jnp.arange(half, dtype=jnp.int32)
    period = 10000.0 ** (2.0 * (index // 2).astype(jnp.float32) / half)
    even = index % 2 == 0
    along_y = (upright_y + 1).astype(jnp.float32) / (heights[:, None, None].astype(jnp.float32) + 1e-06) * (2.0 * math.pi)
    along_x = (upright_x + 1).astype(jnp.float32) / (widths[:, None, None].astype(jnp.float32) + 1e-06) * (2.0 * math.pi)
    phase_y = along_y[..., None] / period
    phase_x = along_x[..., None] / period
    pos_y = jnp.where(even, jnp.sin(phase_y), jnp.cos(phase_y))
    pos_x = jnp.where(even, jnp.sin(phase_x), jnp.cos(phase_x))
    return (jnp.concatenate([pos_y, pos_x], axis=-1), valid)

def conv_same(value, kernel):
    return lax.conv_general_dilated(value[None], kernel, (1, 1), 'SAME', dimension_numbers=('NHWC', 'HWIO', 'NHWC'), precision=lax.Precision.HIGHEST)[0]

def matmul(left, right):
    return jnp.dot(left, right, precision=lax.Precision.HIGHEST)

def forward_page(feat, params, position, key_bias, frozen_scale, frozen_shift):
    first_kernel, second_kernel, project_weight, project_bias, query_weight, query_bias, key_weight, value_weight, value_bias, output_weight, output_bias, first_gain, first_shift, expand_weight, expand_bias, shrink_weight, shrink_bias, final_gain, final_shift = params
    side, channels = (feat.shape[0], feat.shape[2])
    width = project_weight.shape[1]
    head_size = width // HEADS
    length = side * side
    first_out = low_back(conv_same(feat, first_kernel))
    first_pre = first_out * frozen_scale[0] + frozen_shift[0]
    hidden = low(gelu_exact(first_pre))
    second_out = low_back(conv_same(hidden, second_kernel))
    second_pre = second_out * frozen_scale[1] + frozen_shift[1] + feat
    block = low(gelu_exact(second_pre)).reshape(length, channels)
    source = low_back(matmul(block, project_weight) + project_bias)
    joint = low(source + position)
    plain = low(source)
    queries = low_back(low(matmul(joint, query_weight) + query_bias)).reshape(length, HEADS, head_size)
    keys = low_back(low(matmul(joint, key_weight))).reshape(length, HEADS, head_size)
    values = low_back(low(matmul(plain, value_weight) + value_bias)).reshape(length, HEADS, head_size)
    scores = jnp.einsum('qhd,khd->hqk', queries, keys, precision=lax.Precision.HIGHEST) * head_size ** (-0.5)
    scores = low_back(scores + key_bias[None, None, :])
    prob = jax.nn.softmax(scores, axis=-1)
    mixed = jnp.einsum('hqk,khd->qhd', low(prob), values, precision=lax.Precision.HIGHEST).reshape(length, width)
    combined = low_back(low(mixed))
    attended = low_back(matmul(combined, output_weight) + output_bias)
    normed = layer_norm(source + attended, first_gain, first_shift)
    ff_in = low(normed)
    expanded = low_back(matmul(ff_in, expand_weight) + expand_bias)
    activated = low(gelu_exact(expanded))
    shrunk = low_back(matmul(activated, shrink_weight) + shrink_bias)
    return layer_norm(normed + shrunk, final_gain, final_shift)

def reference(features, quarter_turns, heights, widths, frozen_scale, frozen_shift, first_kernel, second_kernel, project_weight, project_bias, query_weight, query_bias, key_weight, value_weight, value_bias, output_weight, output_bias, first_gain, first_shift, expand_weight, expand_bias, shrink_weight, shrink_bias, final_gain, final_shift, cotangent):
    params = (first_kernel, second_kernel, project_weight, project_bias, query_weight, query_bias, key_weight, value_weight, value_bias, output_weight, output_bias, first_gain, first_shift, expand_weight, expand_bias, shrink_weight, shrink_bias, final_gain, final_shift)
    params = tuple((p.astype(jnp.float32) for p in params))
    pages, side = (features.shape[0], features.shape[1])
    width = project_weight.shape[1]
    position, valid = sine_positions(quarter_turns, heights, widths, jnp.int32(0), side, side, width)
    position = position.reshape(pages, side * side, width).astype(jnp.float32)
    key_bias = jnp.where(valid, 0.0, -10000.0).reshape(pages, side * side).astype(jnp.float32)

    def page_step(totals, inputs):
        feat, cot, pos_page, bias_page = inputs

        def local_forward(value, weights):
            return forward_page(value, weights, pos_page, bias_page, frozen_scale, frozen_shift)
        result, pullback = jax.vjp(local_forward, feat.astype(jnp.float32), params)
        feat_grad, weight_grads = pullback(cot.astype(jnp.float32).reshape(side * side, width))
        totals = jax.tree.map(lambda a, b: a + b, totals, weight_grads)
        return (totals, (result.astype(jnp.bfloat16).reshape(side, side, width), feat_grad))
    init = jax.tree.map(jnp.zeros_like, params)
    totals, (encoded, features_grad) = lax.scan(page_step, init, (features, cotangent, position, key_bias))
    return (encoded, features_grad) + tuple(totals)
```

```python
import functools
import math

import jax
import jax.numpy as jnp
from jax import lax
from jax.experimental import pallas as pl
from jax.experimental.pallas import tpu as pltpu
from jax.sharding import PartitionSpec as P

HEADS = 8


def with_halo(block, sides, width):
    for axis, dim in sides:
        count = lax.axis_size(axis)
        forward = [(i, i + 1) for i in range(count - 1)]
        backward = [(target, source) for source, target in forward]
        low = lax.ppermute(
            lax.slice_in_dim(block, block.shape[dim] - width, None, axis=dim), axis, forward
        )
        high = lax.ppermute(lax.slice_in_dim(block, 0, width, axis=dim), axis, backward)
        block = jnp.concatenate([low, block, high], axis=dim)
    return block


def gelu_exact(value):
    return jax.nn.gelu(value, approximate=False)


def gelu_back(value, upstream):
    return jax.vjp(gelu_exact, value)[1](upstream)[0]


def layer_norm(value, gain, shift):
    center = value - jnp.mean(value, axis=-1, keepdims=True)
    spread = jnp.mean(center * center, axis=-1, keepdims=True)
    return center * lax.rsqrt(spread + 1e-05) * gain + shift


def sine_positions(turns, heights, widths, row_start, rows, side, width):
    row = row_start + jnp.arange(rows, dtype=jnp.int32)[None, :, None]
    column = jnp.arange(side, dtype=jnp.int32)[None, None, :]
    turn = turns[:, None, None]
    upright_y = jnp.where(
        turn == 0,
        row,
        jnp.where(turn == 1, column, jnp.where(turn == 2, side - 1 - row, side - 1 - column)),
    )
    upright_x = jnp.where(
        turn == 0,
        column,
        jnp.where(turn == 1, side - 1 - row, jnp.where(turn == 2, side - 1 - column, row)),
    )
    valid = (upright_y < heights[:, None, None]) & (upright_x < widths[:, None, None])
    half = width // 2
    index = jnp.arange(half, dtype=jnp.int32)
    period = 10000.0 ** (2.0 * (index // 2).astype(jnp.float32) / half)
    even = index % 2 == 0
    along_y = (
        (upright_y + 1).astype(jnp.float32)
        / (heights[:, None, None].astype(jnp.float32) + 1e-06)
        * (2.0 * math.pi)
    )
    along_x = (
        (upright_x + 1).astype(jnp.float32)
        / (widths[:, None, None].astype(jnp.float32) + 1e-06)
        * (2.0 * math.pi)
    )
    phase_y = along_y[..., None] / period
    phase_x = along_x[..., None] / period
    pos_y = jnp.where(even, jnp.sin(phase_y), jnp.cos(phase_y))
    pos_x = jnp.where(even, jnp.sin(phase_x), jnp.cos(phase_x))
    return (jnp.concatenate([pos_y, pos_x], axis=-1), valid)


def pad_columns(value):
    return jnp.pad(value, ((0, 0), (0, 0), (1, 1), (0, 0)))


def conv_valid(padded, kernel):
    return lax.conv_general_dilated(
        padded,
        kernel,
        (1, 1),
        "VALID",
        dimension_numbers=("NHWC", "HWIO", "NHWC"),
        preferred_element_type=jnp.float32,
    )


def flipped(kernel):
    return jnp.transpose(kernel[::-1, ::-1], (0, 1, 3, 2))


def kernel_grad(padded, upstream):
    rows, side, channels = (upstream.shape[1], upstream.shape[2], upstream.shape[3])
    terms = []
    for down in range(3):
        for across in range(3):
            window = padded[:, down : down + rows, across : across + side, :]
            terms.append(
                jnp.einsum("prci,prco->io", window, upstream, preferred_element_type=jnp.float32)
            )
    return jnp.stack(terms).reshape(3, 3, padded.shape[3], channels)


def left_product(left, right):
    return jnp.einsum("ti,to->io", left, right, preferred_element_type=jnp.float32)


def right_back(upstream, weight):
    return jnp.einsum("to,io->ti", upstream, weight, preferred_element_type=jnp.float32)


def column_sum(value):
    return jnp.sum(value.astype(jnp.float32), axis=0)


def body(
    features,
    quarter_turns,
    heights,
    widths,
    frozen_scale,
    frozen_shift,
    first_kernel,
    second_kernel,
    project_weight,
    project_bias,
    query_weight,
    query_bias,
    key_weight,
    value_weight,
    value_bias,
    output_weight,
    output_bias,
    first_gain,
    first_shift,
    expand_weight,
    expand_bias,
    shrink_weight,
    shrink_bias,
    final_gain,
    final_shift,
    cotangent,
):
    pages, rows, side, channels = features.shape
    width = project_weight.shape[1]
    head_size = width // HEADS
    length = rows * side
    strips = lax.axis_size("strip")
    whole = strips * length
    row_start = lax.axis_index("strip") * rows
    factor = head_size ** (-0.5)
    padded_in = pad_columns(with_halo(features, (("strip", 1),), 1))
    first_pre = conv_valid(padded_in, first_kernel) * frozen_scale[0] + frozen_shift[0]
    hidden = gelu_exact(first_pre).astype(jnp.bfloat16)
    padded_hidden = pad_columns(with_halo(hidden, (("strip", 1),), 1))
    second_pre = (
        conv_valid(padded_hidden, second_kernel) * frozen_scale[1]
        + frozen_shift[1]
        + features.astype(jnp.float32)
    )
    block = gelu_exact(second_pre).astype(jnp.bfloat16).reshape(pages * length, channels)
    source = jnp.dot(block, project_weight, preferred_element_type=jnp.float32) + project_bias
    position, valid = sine_positions(quarter_turns, heights, widths, row_start, rows, side, width)
    joint = (source + position.reshape(pages * length, width)).astype(jnp.bfloat16)
    plain = source.astype(jnp.bfloat16)
    queries = (
        jnp.dot(joint, query_weight, preferred_element_type=jnp.float32) + query_bias
    ).astype(jnp.bfloat16)
    queries = queries.reshape(pages, length, HEADS, head_size)
    keys_local = (
        jnp.dot(joint, key_weight, preferred_element_type=jnp.float32)
        .astype(jnp.bfloat16)
        .reshape(pages, length, width)
    )
    values_local = (
        (jnp.dot(plain, value_weight, preferred_element_type=jnp.float32) + value_bias)
        .astype(jnp.bfloat16)
        .reshape(pages, length, width)
    )
    key_bias = jnp.where(valid, 0.0, -10000.0).astype(jnp.bfloat16).reshape(pages, length)
    keys_piece = lax.all_gather(keys_local, "strip", axis=1, tiled=True)
    values_piece = lax.all_gather(values_local, "strip", axis=1, tiled=True)
    bias_piece = lax.all_gather(key_bias, "strip", axis=1, tiled=True)
    count = keys_piece.shape[1]
    partial_scores = jnp.einsum(
        "pqhd,pkhd->phqk",
        queries,
        keys_piece.reshape(pages, count, HEADS, head_size),
        preferred_element_type=jnp.float32,
    )
    partial_scores = partial_scores * factor + bias_piece.astype(jnp.float32)[:, None, None, :]
    peak = jnp.max(partial_scores, axis=-1)
    expd = jnp.exp(partial_scores - peak[..., None])
    denom = jnp.sum(expd, axis=-1)
    logsum = peak + jnp.log(denom)
    low_prob = (expd / denom[..., None]).astype(jnp.bfloat16)
    mixed = jnp.einsum(
        "phqk,pkhd->pqhd",
        low_prob,
        values_piece.reshape(pages, whole, HEADS, head_size),
        preferred_element_type=jnp.float32,
    )
    combined = mixed.reshape(pages * length, width).astype(jnp.bfloat16)
    attended = jnp.dot(combined, output_weight, preferred_element_type=jnp.float32) + output_bias
    first_sum = source + attended
    normed = layer_norm(first_sum, first_gain, first_shift)
    ff_in = normed.astype(jnp.bfloat16)
    expanded = jnp.dot(ff_in, expand_weight, preferred_element_type=jnp.float32) + expand_bias
    activated = gelu_exact(expanded).astype(jnp.bfloat16)
    second_sum = (
        normed + jnp.dot(activated, shrink_weight, preferred_element_type=jnp.float32) + shrink_bias
    )
    result, final_back = jax.vjp(layer_norm, second_sum, final_gain, final_shift)
    encoded = result.astype(jnp.bfloat16).reshape(pages, rows, side, width)
    d_second, final_gain_grad, final_shift_grad = final_back(
        cotangent.astype(jnp.float32).reshape(pages * length, width)
    )
    d_shrunk = d_second.astype(jnp.bfloat16)
    shrink_bias_grad = column_sum(d_shrunk)
    shrink_weight_grad = left_product(activated, d_shrunk)
    d_expanded = gelu_back(expanded, right_back(d_shrunk, shrink_weight)).astype(jnp.bfloat16)
    expand_bias_grad = column_sum(d_expanded)
    expand_weight_grad = left_product(ff_in, d_expanded)
    d_normed = right_back(d_expanded, expand_weight) + d_second
    d_first, first_gain_grad, first_shift_grad = jax.vjp(
        layer_norm, first_sum, first_gain, first_shift
    )[1](d_normed)
    d_attended = d_first.astype(jnp.bfloat16)
    output_bias_grad = column_sum(d_attended)
    output_weight_grad = left_product(combined, d_attended)
    d_combined = (
        right_back(d_attended, output_weight)
        .astype(jnp.bfloat16)
        .reshape(pages, length, HEADS, head_size)
    )
    delta = jnp.sum(d_combined.astype(jnp.float32) * mixed, axis=-1)
    logsum_rows = jnp.transpose(logsum, (0, 2, 1))
    keys_all, values_again, bias_all = (
        lax.all_gather(keys_local, "strip", axis=1, tiled=True),
        lax.all_gather(values_local, "strip", axis=1, tiled=True),
        lax.all_gather(key_bias, "strip", axis=1, tiled=True),
    )
    keys_four = keys_all.reshape(pages, whole, HEADS, head_size)
    values_four = values_again.reshape(pages, whole, HEADS, head_size)
    part_scores = (
        jnp.einsum("pqhd,pkhd->phqk", queries, keys_four, preferred_element_type=jnp.float32)
        * factor
    )
    part_scores = part_scores + bias_all.astype(jnp.float32)[:, None, None, :]
    prob = jnp.exp(part_scores - jnp.transpose(logsum_rows, (0, 2, 1))[..., None])
    d_prob = jnp.einsum(
        "pqhd,pkhd->phqk", d_combined, values_four, preferred_element_type=jnp.float32
    )
    pair_d_scores = (prob * (d_prob - jnp.transpose(delta, (0, 2, 1))[..., None])).astype(
        jnp.bfloat16
    )
    weights_low = prob.astype(jnp.bfloat16)
    d_queries = factor * jnp.einsum(
        "phqk,pkhd->pqhd", pair_d_scores, keys_four, preferred_element_type=jnp.float32
    )
    key_part = factor * jnp.einsum(
        "phqk,pqhd->kphd", pair_d_scores, queries, preferred_element_type=jnp.float32
    )
    value_part = jnp.einsum(
        "phqk,pqhd->kphd", weights_low, d_combined, preferred_element_type=jnp.float32
    )
    summed = lax.psum_scatter(
        jnp.concatenate(
            [
                key_part.reshape(length * lax.axis_size("strip"), pages, width),
                value_part.reshape(length * lax.axis_size("strip"), pages, width),
            ],
            axis=-1,
        ).astype(jnp.bfloat16),
        "strip",
        scatter_dimension=0,
        tiled=True,
    ).astype(jnp.float32)
    d_keys = jnp.transpose(summed[:, :, :width], (1, 0, 2))
    d_values = jnp.transpose(summed[:, :, width:], (1, 0, 2))
    d_queries_low = d_queries.reshape(pages * length, width).astype(jnp.bfloat16)
    d_keys_low = d_keys.reshape(pages * length, width).astype(jnp.bfloat16)
    d_values_low = d_values.reshape(pages * length, width).astype(jnp.bfloat16)
    query_bias_grad = column_sum(d_queries_low)
    query_weight_grad = left_product(joint, d_queries_low)
    key_weight_grad = left_product(joint, d_keys_low)
    value_weight_grad = left_product(plain, d_values_low)
    value_bias_grad = column_sum(d_values_low)
    d_source = (
        d_first
        + right_back(d_queries_low, query_weight)
        + right_back(d_keys_low, key_weight)
        + right_back(d_values_low, value_weight)
    )
    d_source_low = d_source.astype(jnp.bfloat16)
    project_bias_grad = column_sum(d_source_low)
    project_weight_grad = left_product(block, d_source_low)
    d_block = right_back(d_source_low, project_weight).reshape(pages, rows, side, channels)
    d_second_pre = gelu_back(second_pre, d_block)
    d_late = (d_second_pre * frozen_scale[1]).astype(jnp.bfloat16)
    padded_late = pad_columns(with_halo(d_late, (("strip", 1),), 1))
    d_hidden = conv_valid(padded_late, flipped(second_kernel))
    second_kernel_grad = kernel_grad(padded_hidden, d_late)
    d_early = (gelu_back(first_pre, d_hidden) * frozen_scale[0]).astype(jnp.bfloat16)
    padded_early = pad_columns(with_halo(d_early, (("strip", 1),), 1))
    features_grad = conv_valid(padded_early, flipped(first_kernel)) + d_second_pre
    first_kernel_grad = kernel_grad(padded_in, d_early)
    first_part, second_part = (
        lax.psum_scatter(
            first_kernel_grad.astype(jnp.bfloat16), "page", scatter_dimension=2, tiled=True
        ).astype(jnp.float32),
        lax.psum_scatter(
            second_kernel_grad.astype(jnp.bfloat16), "page", scatter_dimension=2, tiled=True
        ).astype(jnp.float32),
    )
    first_part, second_part = (
        lax.psum_scatter(
            first_part.astype(jnp.bfloat16), "strip", scatter_dimension=3, tiled=True
        ).astype(jnp.float32),
        lax.psum_scatter(
            second_part.astype(jnp.bfloat16), "strip", scatter_dimension=3, tiled=True
        ).astype(jnp.float32),
    )
    dense = lax.psum(
        (
            project_weight_grad,
            project_bias_grad,
            query_weight_grad,
            query_bias_grad,
            key_weight_grad,
            value_weight_grad,
            value_bias_grad,
            output_weight_grad,
            output_bias_grad,
            first_gain_grad,
            first_shift_grad,
            expand_weight_grad,
            expand_bias_grad,
            shrink_weight_grad,
            shrink_bias_grad,
            final_gain_grad,
            final_shift_grad,
        ),
        ("page", "strip"),
    )
    return (encoded, features_grad, first_part, second_part) + tuple(dense)


MESH = pl.DeviceIdType.MESH
STEPS = {"core": 1, "y": 2, "z0": 4, "z1": 8}
ORDERS = (("x", "y", "z0", "z1"), ("y", "x", "z0", "z1"), ("z0", "z1", "x", "y"))


def own_bits():
    page, strip = lax.axis_index("page"), lax.axis_index("strip")
    bits = {name: (page // step) % 2 for name, step in STEPS.items()}
    peers = {name: (page + step - 2 * step * bits[name], strip) for name, step in STEPS.items()}
    bits["x"] = strip
    peers["x"] = (page, 1 - strip)
    peers["across"] = (peers["core"][0], 1 - strip)
    return bits, peers


def enter(peers):
    barrier = pltpu.get_barrier_semaphore()
    for peer in peers.values():
        pl.semaphore_signal(barrier, inc=1, device_id=peer, device_id_type=MESH)
    pl.semaphore_wait(barrier, len(peers))


def remote(source, target, sends, recvs, peer):
    return pltpu.make_async_remote_copy(
        source, target, sends, recvs, device_id=peer, device_id_type=MESH
    )


def slot_of(order, place):
    slot = 0
    for name in order:
        slot = slot * 2 + place[name]
    return slot


class Halving:
    def __init__(self, order, bits, peers, current, parts, sums, sends, recvs, whole=None):
        self.order, self.bits, self.peers = order, bits, peers
        self.current, self.parts, self.sums = current, parts, sums
        self.sends, self.recvs, self.whole = sends, recvs, whole
        self.slots = 2 ** len(order)
        self.flight = None

    def steps(self):
        return len(self.order) * (1 if self.whole is None else 2)

    def begin(self, step):
        count = len(self.order)
        if step < count:
            name = self.order[step]
            half = self.slots >> (step + 1)
            offset = self.slots - (self.slots >> step)
            source = self.current.at[pl.ds((1 - self.bits[name]) * half, half)]
            target = self.parts.at[pl.ds(offset, half)]
        else:
            level = 2 * count - 1 - step
            name = self.order[level]
            size = self.slots >> (level + 1)
            first = 0
            for depth in range(level + 1):
                first = first + self.bits[self.order[depth]] * (self.slots >> (depth + 1))
            source = self.whole.at[pl.ds(first, size)]
            target = self.whole.at[pl.ds(first, size)]
        self.flight = remote(
            source, target, self.sends.at[step], self.recvs.at[step], self.peers[name]
        )
        self.flight.start()

    def end(self, step):
        count = len(self.order)
        self.flight.wait()
        if step >= count:
            return None
        name = self.order[step]
        half = self.slots >> (step + 1)
        offset = self.slots - (self.slots >> step)
        mine = self.current[pl.ds(self.bits[name] * half, half)]
        total = mine.astype(jnp.float32) + self.parts[pl.ds(offset, half)].astype(jnp.float32)
        if step == count - 1:
            return total
        following = self.sums.at[pl.ds(offset, half)]
        following[...] = total.astype(jnp.bfloat16)
        self.current = following
        return None


def link_plan(units):
    waiting = sorted((ready, unit, 0) for unit, (ready, _) in enumerate(units))
    free, finished = {}, []
    while waiting:
        ready, unit, step = waiting.pop(0)
        link, spent = units[unit][1][step]
        begin = max(ready, free.get(link, 0.0))
        free[link] = begin + spent
        done = begin + spent + 1.5
        finished.append((done, unit, step))
        if step + 1 < len(units[unit][1]):
            waiting.append((done, unit, step + 1))
            waiting.sort()
    return sorted(finished)


def link_costs(order, size, back):
    costs = []
    for name in order:
        size = size / 2
        if name == "core":
            costs.append(("core", size / 6e5))
        else:
            costs.append((name[0], size * (4 if name == "z1" else 2) / 1e5))
    return costs + costs[::-1] if back else costs


def shifted(value):
    side = value.shape[0]
    wide = value.astype(jnp.float32)
    column = lax.broadcasted_iota(jnp.int32, wide.shape, 0)
    later = jnp.where(column < side - 1, pltpu.roll(wide, side - 1, 0), 0.0)
    earlier = jnp.where(column > 0, pltpu.roll(wide, 1, 0), 0.0)
    return later.astype(jnp.bfloat16), earlier.astype(jnp.bfloat16)


def late_kernel(
    side,
    late_ref,
    slope_ref,
    direct_ref,
    hidden_ref,
    features_ref,
    first_hbm,
    second_hbm,
    dense_ref,
    small_ref,
    fgrad_ref,
    first_out,
    second_out,
    dense_out,
    small_out,
    first_w,
    second_w,
    hidden_all,
    features_all,
    late_ext,
    late_side,
    late_pair,
    late_sib,
    early_side,
    early_pair,
    early_sib,
    grads,
    parts,
    sums,
    dense_parts,
    dense_sums,
    small_parts,
    small_sums,
    owned,
    owned_sib,
    weight_sems,
    pair_sends,
    pair_recvs,
    grad_sends,
    grad_recvs,
    dense_sends,
    dense_recvs,
    small_sends,
    small_recvs,
    owned_sends,
    owned_recvs,
):
    length, channels = late_ref.shape
    rows = length // side
    lanes = 128
    bits, peers = own_bits()
    strip, core = bits["x"], bits["core"]
    second_load = pltpu.make_async_copy(second_hbm, second_w, weight_sems.at[0])
    first_load = pltpu.make_async_copy(first_hbm, first_w, weight_sems.at[1])
    second_load.start()
    first_load.start()
    enter(peers)

    edge = 2 * side
    own_edge = (1 - strip) * (length - edge)
    halo_at = strip * (length + edge)
    copies = [
        remote(
            late_ref.at[pl.ds(pl.multiple_of(own_edge, side), edge)],
            late_ext.at[pl.ds(pl.multiple_of(halo_at, side), edge)],
            pair_sends.at[0],
            pair_recvs.at[0],
            peers["x"],
        )
    ]
    number = 1
    for part in range(2):
        chunk = pl.ds(pl.multiple_of(part * 2 * lanes + (1 - core) * lanes, lanes), lanes)
        copies.append(
            remote(
                late_ref.at[:, chunk],
                late_sib.at[pl.ds(side, length), pl.ds(part * lanes, lanes)],
                pair_sends.at[number],
                pair_recvs.at[number],
                peers["core"],
            )
        )
        copies.append(
            remote(
                late_ref.at[pl.ds(pl.multiple_of((1 - strip) * (length - side), side), side), chunk],
                late_sib.at[
                    pl.ds(pl.multiple_of(strip * (length + side), side), side),
                    pl.ds(part * lanes, lanes),
                ],
                pair_sends.at[number + 1],
                pair_recvs.at[number + 1],
                peers["across"],
            )
        )
        number += 2
    for source, target in ((hidden_ref, hidden_all), (features_ref, features_all)):
        copies.append(
            remote(
                source,
                target.at[1],
                pair_sends.at[number],
                pair_recvs.at[number],
                peers["core"],
            )
        )
        number += 1
    for copy in copies:
        copy.start()

    dense_units = dense_ref.shape[0]
    taps = 9
    reducers, costs = [], []
    for unit in range(dense_units):
        order = ("core",) + ORDERS[unit % 2]
        reducers.append(
            Halving(
                order,
                bits,
                peers,
                dense_ref.at[unit],
                dense_parts.at[unit],
                dense_sums.at[unit],
                dense_sends.at[unit],
                dense_recvs.at[unit],
                dense_out.at[unit],
            )
        )
        costs.append((1.0, link_costs(order, 262144, True)))
    for unit in range(2 * taps):
        order = ORDERS[(0, 1, 0, 1, 2, 0, 1, 0, 1)[unit % taps]]
        reducers.append(
            Halving(
                order,
                bits,
                peers,
                grads.at[unit],
                parts.at[unit],
                sums.at[unit],
                grad_sends.at[unit],
                grad_recvs.at[unit],
            )
        )
        made = 4.0 + 0.5 * unit if unit < taps else 14.0 + 0.5 * (unit - taps)
        costs.append((made, link_costs(order, 262144, False)))
    agenda = link_plan(costs)

    def advance(now):
        while agenda and agenda[0][0] <= now:
            _, unit, step = agenda.pop(0)
            reducer = reducers[unit]
            total = reducer.end(step)
            if total is not None:
                low = total.astype(jnp.bfloat16)
                if unit < dense_units:
                    place = 0
                    for name in reducer.order:
                        place = place * 2 + bits[name]
                    dense_out[unit, pl.ds(place, 1)] = low
                else:
                    tap = unit - dense_units
                    owned[tap // taps, 0, tap % taps] = low[0, : low.shape[1] // 2]
                    owned[tap // taps, 1, tap % taps] = low[0, low.shape[1] // 2 :]
            if step + 1 < reducer.steps():
                reducer.begin(step + 1)

    for unit in range(dense_units):
        reducers[unit].begin(0)

    blank = jnp.zeros((edge, channels), jnp.bfloat16)
    late_ext[pl.ds(pl.multiple_of(strip * (length + edge), side), edge)] = blank
    late_sib[pl.ds(pl.multiple_of(strip * (length + side), side), side)] = blank[
        :side, : 2 * lanes
    ]
    late_ext[pl.ds(edge, length)] = late_ref[...]
    hidden_all[0] = hidden_ref[...]
    features_all[0] = features_ref[...]
    small_now = small_ref[...]
    for step, name in enumerate(("core", "x", "y", "z0", "z1")):
        small_sums[step] = small_now
        copy = remote(
            small_sums.at[step],
            small_parts.at[step],
            small_sends.at[step],
            small_recvs.at[step],
            peers[name],
        )
        copy.start()
        copy.wait()
        small_now = small_now + small_parts[step]
    small_out[...] = small_now
    for copy in copies:
        copy.wait()

    def spread(source, target, chunk, count):
        def one(row, carry):
            at = pl.ds(pl.multiple_of(row * side, side), side)
            value = source[at] if chunk is None else source[at, chunk]
            later, earlier = shifted(value)
            if chunk is None:
                target[0, at] = later
                target[1, at] = value
                target[2, at] = earlier
            else:
                lane = chunk[1]
                target[0, at, lane] = later
                target[1, at, lane] = value
                target[2, at, lane] = earlier
            return carry

        lax.fori_loop(0, count, one, 0)

    def spread_pair(source, target, skip):
        def one(row, carry):
            at = pl.ds(pl.multiple_of(row * side, side), side)
            for part in range(2):
                chunk = pl.ds(pl.multiple_of(part * 2 * lanes + core * lanes, lanes), lanes)
                value = source[pl.ds(pl.multiple_of((row + skip) * side, side), side), chunk]
                later, earlier = shifted(value)
                lane = pl.ds(part * lanes, lanes)
                target[0, at, lane] = later
                target[1, at, lane] = value
                target[2, at, lane] = earlier
            return carry

        lax.fori_loop(0, rows + 2, one, 0)

    def kernel_grads(left, own, sibling, first_unit, clock):
        for tap in range(taps):
            down, across = tap // 3, tap % 3
            window = pl.ds(side * (2 - down), length)
            product = jnp.dot(
                left[0], own[0 + across, window], preferred_element_type=jnp.float32
            ) + jnp.dot(left[1], sibling[across, window], preferred_element_type=jnp.float32)
            low = product.astype(jnp.bfloat16)
            unit = first_unit + tap
            order = reducers[dense_units + unit].order
            block = low.shape[0] // 8
            for chip in range(8):
                for half in range(2):
                    slot = slot_of(
                        order,
                        {"x": half, "y": chip % 2, "z0": chip // 2 % 2, "z1": chip // 4},
                    )
                    grads[unit, slot] = low[
                        chip * block : (chip + 1) * block, half * lanes : (half + 1) * lanes
                    ]
            reducers[dense_units + unit].begin(0)
            advance(clock + 0.5 * tap)

    spread(late_ext, late_side, None, rows + 4)
    spread_pair(late_ext, late_pair, 1)
    spread(late_sib, early_sib, None, rows + 2)
    kernel_grads(hidden_all, late_pair, early_sib, 0, 4.0)
    second_load.wait()

    def transposed_conv(shifts, weight, count):
        total = None
        for tap in range(taps):
            down, across = tap // 3, tap % 3
            term = lax.dot_general(
                shifts[across, pl.ds(side * (2 - down), count)],
                weight[tap],
                (((1,), (1,)), ((), ())),
                preferred_element_type=jnp.float32,
            )
            total = term if total is None else total + term
        return total

    early = (transposed_conv(late_side, second_w, length + edge) * slope_ref[...]).astype(
        jnp.bfloat16
    )
    early_side[1] = early
    pair_copies = []
    for part in range(2):
        chunk = pl.ds(pl.multiple_of(part * 2 * lanes + (1 - core) * lanes, lanes), lanes)
        pair_copies.append(
            remote(
                early_side.at[1, :, chunk],
                early_pair.at[:, pl.ds(part * lanes, lanes)],
                pair_sends.at[number],
                pair_recvs.at[number],
                peers["core"],
            )
        )
        number += 1
    for copy in pair_copies:
        copy.start()
    advance(10.0)
    spread(early_side.at[1], late_side, None, rows + 2)
    spread_pair(early_side.at[1], late_pair, 0)
    for copy in pair_copies:
        copy.wait()
    spread(early_pair, early_sib, None, rows + 2)
    kernel_grads(features_all, late_pair, early_sib, taps, 14.0)
    first_load.wait()
    fgrad_ref[...] = transposed_conv(late_side, first_w, length) + direct_ref[...]
    advance(1e9)
    finals = []
    for which, out in ((1, first_out), (0, second_out)):
        copy = remote(
            owned.at[which, 1 - core],
            owned_sib.at[which],
            owned_sends.at[which],
            owned_recvs.at[which],
            peers["core"],
        )
        copy.start()
        finals.append((copy, which, out))
    for copy, which, out in finals:
        copy.wait()
        out[:, :, pl.ds(pl.multiple_of(core * lanes, lanes), lanes)] = owned[which, core].astype(
            jnp.float32
        )
        out[:, :, pl.ds(pl.multiple_of((1 - core) * lanes, lanes), lanes)] = owned_sib[
            which
        ].astype(jnp.float32)


def late_call(side, late, slope, direct, hidden, features, first, second, dense, small):
    length, channels = late.shape
    edge = 2 * side
    units = dense.shape[0]
    bf16, f32 = jnp.bfloat16, jnp.float32
    vmem = pl.BlockSpec(memory_space=pltpu.VMEM)
    hbm = pl.BlockSpec(memory_space=pl.ANY)
    sems = pltpu.SemaphoreType.DMA
    return pl.pallas_call(
        functools.partial(late_kernel, side),
        out_shape=(
            jax.ShapeDtypeStruct((length, channels), f32),
            jax.ShapeDtypeStruct((9, channels // 16, channels // 2), f32),
            jax.ShapeDtypeStruct((9, channels // 16, channels // 2), f32),
            jax.ShapeDtypeStruct(dense.shape, bf16),
            jax.ShapeDtypeStruct(small.shape, f32),
        ),
        in_specs=[vmem] * 5 + [hbm] * 2 + [vmem] * 2,
        out_specs=[vmem] * 5,
        scratch_shapes=[
            pltpu.VMEM(first.shape, bf16),
            pltpu.VMEM(second.shape, bf16),
            pltpu.VMEM((2, channels, length), bf16),
            pltpu.VMEM((2, channels, length), bf16),
            pltpu.VMEM((length + 2 * edge, channels), bf16),
            pltpu.VMEM((3, length + 2 * edge, channels), bf16),
            pltpu.VMEM((3, length + edge, channels // 2), bf16),
            pltpu.VMEM((length + edge, channels // 2), bf16),
            pltpu.VMEM((3, length + edge, channels), bf16),
            pltpu.VMEM((length + edge, channels // 2), bf16),
            pltpu.VMEM((3, length + edge, channels // 2), bf16),
            pltpu.VMEM((18, 16, channels // 8, 128), bf16),
            pltpu.VMEM((18, 16, channels // 8, 128), bf16),
            pltpu.VMEM((18, 16, channels // 8, 128), bf16),
            pltpu.VMEM(dense.shape, bf16),
            pltpu.VMEM(dense.shape, bf16),
            pltpu.VMEM((5,) + small.shape, f32),
            pltpu.VMEM((5,) + small.shape, f32),
            pltpu.VMEM((2, 2, 9, channels // 16, 128), bf16),
            pltpu.VMEM((2, 9, channels // 16, 128), bf16),
            sems((2,)),
            sems((9,)),
            sems((9,)),
            sems((18, 4)),
            sems((18, 4)),
            sems((units, 10)),
            sems((units, 10)),
            sems((5,)),
            sems((5,)),
            sems((2,)),
            sems((2,)),
        ],
        compiler_params=pltpu.CompilerParams(
            collective_id=0, has_side_effects=True, vmem_limit_bytes=62 * 1024 * 1024
        ),
        name="late_gradients",
    )(late, slope, direct, hidden, features, first, second, dense, small)


def swap(value):
    return lax.ppermute(value, "strip", [(0, 1), (1, 0)])


def gelu_both(value):
    bell = 0.5 * (1.0 + lax.erf(value * math.sqrt(0.5)))
    density = jnp.exp(-0.5 * value * value) * (1.0 / math.sqrt(2.0 * math.pi))
    return value * bell, bell + value * density


def paired_body(
    features,
    quarter_turns,
    heights,
    widths,
    frozen_scale,
    frozen_shift,
    first_kernel,
    second_kernel,
    project_weight,
    project_bias,
    query_weight,
    query_bias,
    key_weight,
    value_weight,
    value_bias,
    output_weight,
    output_bias,
    first_gain,
    first_shift,
    expand_weight,
    expand_bias,
    shrink_weight,
    shrink_bias,
    final_gain,
    final_shift,
    cotangent,
):
    pages, rows, side, channels = features.shape
    width = project_weight.shape[1]
    head_size = width // HEADS
    length = rows * side
    strip = lax.axis_index("strip")
    row_start = strip * rows
    factor = head_size ** (-0.5)

    got = swap(lax.dynamic_slice_in_dim(features, (1 - strip) * (rows - 2), 2, axis=1))
    extended = jnp.concatenate(
        [
            jnp.where(strip == 1, got, jnp.zeros_like(got)),
            features,
            jnp.where(strip == 0, got, jnp.zeros_like(got)),
        ],
        axis=1,
    )
    first_pre = (
        conv_valid(pad_columns(extended), first_kernel) * frozen_scale[0] + frozen_shift[0]
    )
    place = row_start - 1 + jnp.arange(rows + 2)
    inside = ((place >= 0) & (place < 2 * rows))[None, :, None, None]
    hidden, slope = gelu_both(first_pre)
    hidden = jnp.where(inside, hidden, 0.0).astype(jnp.bfloat16)
    slope = jnp.where(inside, slope * frozen_scale[0], 0.0)
    second_pre = (
        conv_valid(pad_columns(hidden), second_kernel) * frozen_scale[1]
        + frozen_shift[1]
        + features.astype(jnp.float32)
    )
    block, second_slope = gelu_both(second_pre.reshape(length, channels))
    block = block.astype(jnp.bfloat16)
    source = jnp.dot(block, project_weight, preferred_element_type=jnp.float32) + project_bias
    position, valid = sine_positions(quarter_turns, heights, widths, row_start, rows, side, width)
    other_valid = sine_positions(
        quarter_turns, heights, widths, (1 - strip) * rows, rows, side, width
    )[1]
    joint = (source + position.reshape(length, width)).astype(jnp.bfloat16)
    plain = source.astype(jnp.bfloat16)
    queries = (
        jnp.dot(joint, query_weight, preferred_element_type=jnp.float32) + query_bias
    ).astype(jnp.bfloat16)
    queries = queries.reshape(length, HEADS, head_size)
    keys_own = jnp.dot(joint, key_weight, preferred_element_type=jnp.float32).astype(jnp.bfloat16)
    values_own = (
        jnp.dot(plain, value_weight, preferred_element_type=jnp.float32) + value_bias
    ).astype(jnp.bfloat16)
    pair = jnp.concatenate([keys_own, values_own], axis=1)
    pair = jnp.concatenate([pair, swap(pair)], axis=0)
    keys_four = pair[:, :width].reshape(2 * length, HEADS, head_size)
    values_four = pair[:, width:].reshape(2 * length, HEADS, head_size)
    key_bias = jnp.where(
        jnp.concatenate([valid.reshape(length), other_valid.reshape(length)]), 0.0, -10000.0
    )
    scores = jnp.einsum("qhd,khd->hqk", queries, keys_four, preferred_element_type=jnp.float32)
    scores = scores * factor + key_bias
    peak = jnp.max(scores, axis=-1)
    expd = jnp.exp(scores - peak[..., None])
    denom = jnp.sum(expd, axis=-1)
    logsum = peak + jnp.log(denom)
    low_prob = (expd / denom[..., None]).astype(jnp.bfloat16)
    mixed = jnp.einsum("hqk,khd->qhd", low_prob, values_four, preferred_element_type=jnp.float32)
    combined = mixed.reshape(length, width).astype(jnp.bfloat16)
    attended = jnp.dot(combined, output_weight, preferred_element_type=jnp.float32) + output_bias
    first_sum = source + attended
    normed = layer_norm(first_sum, first_gain, first_shift)
    ff_in = normed.astype(jnp.bfloat16)
    expanded = jnp.dot(ff_in, expand_weight, preferred_element_type=jnp.float32) + expand_bias
    activated = gelu_exact(expanded).astype(jnp.bfloat16)
    second_sum = (
        normed + jnp.dot(activated, shrink_weight, preferred_element_type=jnp.float32) + shrink_bias
    )
    result, final_back = jax.vjp(layer_norm, second_sum, final_gain, final_shift)
    encoded = result.astype(jnp.bfloat16).reshape(pages, rows, side, width)
    d_second, final_gain_grad, final_shift_grad = final_back(
        cotangent.astype(jnp.float32).reshape(length, width)
    )
    d_shrunk = d_second.astype(jnp.bfloat16)
    shrink_bias_grad = column_sum(d_shrunk)
    shrink_weight_grad = left_product(activated, d_shrunk)
    d_expanded = gelu_back(expanded, right_back(d_shrunk, shrink_weight)).astype(jnp.bfloat16)
    expand_bias_grad = column_sum(d_expanded)
    expand_weight_grad = left_product(ff_in, d_expanded)
    d_normed = right_back(d_expanded, expand_weight) + d_second
    d_first, first_gain_grad, first_shift_grad = jax.vjp(
        layer_norm, first_sum, first_gain, first_shift
    )[1](d_normed)
    d_attended = d_first.astype(jnp.bfloat16)
    output_bias_grad = column_sum(d_attended)
    output_weight_grad = left_product(combined, d_attended)
    d_combined = lax.optimization_barrier(
        right_back(d_attended, output_weight).astype(jnp.bfloat16)
    ).reshape(length, HEADS, head_size)
    delta = jnp.sum(d_combined.astype(jnp.float32) * mixed, axis=-1).T
    prob = jnp.exp(scores - logsum[..., None])
    d_prob = jnp.einsum("qhd,khd->hqk", d_combined, values_four, preferred_element_type=jnp.float32)
    d_scores = (prob * (d_prob - delta[..., None])).astype(jnp.bfloat16)
    weights_low = prob.astype(jnp.bfloat16)
    d_queries = factor * jnp.einsum(
        "hqk,khd->qhd", d_scores, keys_four, preferred_element_type=jnp.float32
    )
    key_part = factor * jnp.einsum(
        "hqk,qhd->khd", d_scores, queries, preferred_element_type=jnp.float32
    )
    value_part = jnp.einsum(
        "hqk,qhd->khd", weights_low, d_combined, preferred_element_type=jnp.float32
    )
    both = jnp.concatenate(
        [key_part.reshape(2 * length, width), value_part.reshape(2 * length, width)], axis=1
    )
    summed = both[:length] + swap(both[length:].astype(jnp.bfloat16)).astype(jnp.float32)
    d_queries_low = d_queries.reshape(length, width).astype(jnp.bfloat16)
    d_keys_low = summed[:, :width].astype(jnp.bfloat16)
    d_values_low = summed[:, width:].astype(jnp.bfloat16)
    query_bias_grad = column_sum(d_queries_low)
    query_weight_grad = left_product(joint, d_queries_low)
    key_weight_grad = left_product(joint, d_keys_low)
    value_weight_grad = left_product(plain, d_values_low)
    value_bias_grad = column_sum(d_values_low)
    d_source = (
        d_first
        + right_back(d_queries_low, query_weight)
        + right_back(d_keys_low, key_weight)
        + right_back(d_values_low, value_weight)
    )
    d_source_low = d_source.astype(jnp.bfloat16)
    project_bias_grad = column_sum(d_source_low)
    project_weight_grad = left_product(block, d_source_low)
    d_second_pre = right_back(d_source_low, project_weight) * second_slope
    d_late = (d_second_pre * frozen_scale[1]).astype(jnp.bfloat16)

    hidden_units = expand_weight.shape[1]
    dense = jnp.concatenate(
        [
            shrink_weight_grad,
            jnp.transpose(
                expand_weight_grad.reshape(width, hidden_units // width, width), (1, 0, 2)
            ).reshape(hidden_units, width),
            project_weight_grad,
            query_weight_grad,
            key_weight_grad,
            value_weight_grad,
            output_weight_grad,
        ],
        axis=0,
    ).astype(jnp.bfloat16)
    count = dense.shape[0] // 512
    small_rows = [
        project_bias_grad,
        query_bias_grad,
        value_bias_grad,
        output_bias_grad,
        first_gain_grad,
        first_shift_grad,
        shrink_bias_grad,
        final_gain_grad,
        final_shift_grad,
    ]
    small = jnp.concatenate(
        [jnp.stack(small_rows), expand_bias_grad.reshape(-1, width)], axis=0
    )
    small = jnp.pad(small, ((0, -small.shape[0] % 8), (0, 0)))
    features_grad, first_part, second_part, dense, small = late_call(
        side,
        d_late,
        slope.reshape(-1, channels),
        d_second_pre,
        hidden[:, 1:-1].reshape(length, channels).T,
        features.reshape(length, channels).T,
        first_kernel.reshape(9, channels, channels),
        second_kernel.reshape(9, channels, channels),
        dense.reshape(count, 32, 16, width),
        small,
    )
    dense = dense.reshape(-1, width).astype(jnp.float32)
    at = 0
    cut = []
    for size in (hidden_units, hidden_units, channels, width, width, width, width):
        cut.append(dense[at : at + size])
        at += size
    shrink_sum, expand_sum, project_sum, query_sum, key_sum, value_sum, output_sum = cut
    expand_sum = jnp.transpose(
        expand_sum.reshape(hidden_units // width, width, width), (1, 0, 2)
    ).reshape(width, hidden_units)
    part_shape = (3, 3, channels // 16, channels // 2)
    return (
        encoded,
        features_grad.reshape(pages, rows, side, channels),
        first_part.reshape(part_shape),
        second_part.reshape(part_shape),
        project_sum,
        small[0],
        query_sum,
        small[1],
        key_sum,
        value_sum,
        small[2],
        output_sum,
        small[3],
        small[4],
        small[5],
        expand_sum,
        small[9 : 9 + hidden_units // width].reshape(hidden_units),
        shrink_sum,
        small[6],
        small[7],
        small[8],
    )


def solution(mesh):
    paired = mesh.shape["strip"] == 2 and mesh.shape["page"] == 16
    return jax.shard_map(
        paired_body if paired else body,
        mesh=mesh,
        in_specs=(
            P("page", "strip", None, None),
            P("page"),
            P("page"),
            P("page"),
            P(),
            P(),
            P(),
            P(),
            P(),
            P(),
            P(),
            P(),
            P(),
            P(),
            P(),
            P(),
            P(),
            P(),
            P(),
            P(),
            P(),
            P(),
            P(),
            P(),
            P(),
            P("page", "strip", None, None),
        ),
        out_specs=(
            P("page", "strip", None, None),
            P("page", "strip", None, None),
            P(None, None, "page", "strip"),
            P(None, None, "page", "strip"),
            P(),
            P(),
            P(),
            P(),
            P(),
            P(),
            P(),
            P(),
            P(),
            P(),
            P(),
            P(),
            P(),
            P(),
            P(),
            P(),
            P(),
        ),
        check_vma=False,
    )
```

```python
import functools
import math
from types import SimpleNamespace

import jax
import jax.numpy as jnp
from jax import lax
from jax.experimental import pallas as pl
from jax.experimental.pallas import tpu as pltpu
from jax.sharding import PartitionSpec as P

HEADS = 8


def with_halo(block, sides, width):
    for axis, dim in sides:
        count = lax.axis_size(axis)
        forward = [(i, i + 1) for i in range(count - 1)]
        backward = [(target, source) for source, target in forward]
        low = lax.ppermute(
            lax.slice_in_dim(block, block.shape[dim] - width, None, axis=dim), axis, forward
        )
        high = lax.ppermute(lax.slice_in_dim(block, 0, width, axis=dim), axis, backward)
        block = jnp.concatenate([low, block, high], axis=dim)
    return block


def gelu_exact(value):
    return jax.nn.gelu(value, approximate=False)


def gelu_back(value, upstream):
    return jax.vjp(gelu_exact, value)[1](upstream)[0]


def layer_norm(value, gain, shift):
    center = value - jnp.mean(value, axis=-1, keepdims=True)
    spread = jnp.mean(center * center, axis=-1, keepdims=True)
    return center * lax.rsqrt(spread + 1e-05) * gain + shift


def sine_positions(turns, heights, widths, row_start, rows, side, width):
    row = row_start + jnp.arange(rows, dtype=jnp.int32)[None, :, None]
    column = jnp.arange(side, dtype=jnp.int32)[None, None, :]
    turn = turns[:, None, None]
    upright_y = jnp.where(
        turn == 0,
        row,
        jnp.where(turn == 1, column, jnp.where(turn == 2, side - 1 - row, side - 1 - column)),
    )
    upright_x = jnp.where(
        turn == 0,
        column,
        jnp.where(turn == 1, side - 1 - row, jnp.where(turn == 2, side - 1 - column, row)),
    )
    valid = (upright_y < heights[:, None, None]) & (upright_x < widths[:, None, None])
    half = width // 2
    index = jnp.arange(half, dtype=jnp.int32)
    period = 10000.0 ** (2.0 * (index // 2).astype(jnp.float32) / half)
    even = index % 2 == 0
    along_y = (
        (upright_y + 1).astype(jnp.float32)
        / (heights[:, None, None].astype(jnp.float32) + 1e-06)
        * (2.0 * math.pi)
    )
    along_x = (
        (upright_x + 1).astype(jnp.float32)
        / (widths[:, None, None].astype(jnp.float32) + 1e-06)
        * (2.0 * math.pi)
    )
    phase_y = along_y[..., None] / period
    phase_x = along_x[..., None] / period
    pos_y = jnp.where(even, jnp.sin(phase_y), jnp.cos(phase_y))
    pos_x = jnp.where(even, jnp.sin(phase_x), jnp.cos(phase_x))
    return (jnp.concatenate([pos_y, pos_x], axis=-1), valid)


def pad_columns(value):
    return jnp.pad(value, ((0, 0), (0, 0), (1, 1), (0, 0)))


def conv_valid(padded, kernel):
    return lax.conv_general_dilated(
        padded,
        kernel,
        (1, 1),
        "VALID",
        dimension_numbers=("NHWC", "HWIO", "NHWC"),
        preferred_element_type=jnp.float32,
    )


def flipped(kernel):
    return jnp.transpose(kernel[::-1, ::-1], (0, 1, 3, 2))


def kernel_grad(padded, upstream):
    rows, side, channels = (upstream.shape[1], upstream.shape[2], upstream.shape[3])
    terms = []
    for down in range(3):
        for across in range(3):
            window = padded[:, down : down + rows, across : across + side, :]
            terms.append(
                jnp.einsum("prci,prco->io", window, upstream, preferred_element_type=jnp.float32)
            )
    return jnp.stack(terms).reshape(3, 3, padded.shape[3], channels)


def left_product(left, right):
    return jnp.einsum("ti,to->io", left, right, preferred_element_type=jnp.float32)


def right_back(upstream, weight):
    return jnp.einsum("to,io->ti", upstream, weight, preferred_element_type=jnp.float32)


def column_sum(value):
    return jnp.sum(value.astype(jnp.float32), axis=0)


def body(
    features,
    quarter_turns,
    heights,
    widths,
    frozen_scale,
    frozen_shift,
    first_kernel,
    second_kernel,
    project_weight,
    project_bias,
    query_weight,
    query_bias,
    key_weight,
    value_weight,
    value_bias,
    output_weight,
    output_bias,
    first_gain,
    first_shift,
    expand_weight,
    expand_bias,
    shrink_weight,
    shrink_bias,
    final_gain,
    final_shift,
    cotangent,
):
    pages, rows, side, channels = features.shape
    width = project_weight.shape[1]
    head_size = width // HEADS
    length = rows * side
    strips = lax.axis_size("strip")
    whole = strips * length
    row_start = lax.axis_index("strip") * rows
    factor = head_size ** (-0.5)
    padded_in = pad_columns(with_halo(features, (("strip", 1),), 1))
    first_pre = conv_valid(padded_in, first_kernel) * frozen_scale[0] + frozen_shift[0]
    hidden = gelu_exact(first_pre).astype(jnp.bfloat16)
    padded_hidden = pad_columns(with_halo(hidden, (("strip", 1),), 1))
    second_pre = (
        conv_valid(padded_hidden, second_kernel) * frozen_scale[1]
        + frozen_shift[1]
        + features.astype(jnp.float32)
    )
    block = gelu_exact(second_pre).astype(jnp.bfloat16).reshape(pages * length, channels)
    source = jnp.dot(block, project_weight, preferred_element_type=jnp.float32) + project_bias
    position, valid = sine_positions(quarter_turns, heights, widths, row_start, rows, side, width)
    joint = (source + position.reshape(pages * length, width)).astype(jnp.bfloat16)
    plain = source.astype(jnp.bfloat16)
    queries = (
        jnp.dot(joint, query_weight, preferred_element_type=jnp.float32) + query_bias
    ).astype(jnp.bfloat16)
    queries = queries.reshape(pages, length, HEADS, head_size)
    keys_local = (
        jnp.dot(joint, key_weight, preferred_element_type=jnp.float32)
        .astype(jnp.bfloat16)
        .reshape(pages, length, width)
    )
    values_local = (
        (jnp.dot(plain, value_weight, preferred_element_type=jnp.float32) + value_bias)
        .astype(jnp.bfloat16)
        .reshape(pages, length, width)
    )
    key_bias = jnp.where(valid, 0.0, -10000.0).astype(jnp.bfloat16).reshape(pages, length)
    keys_piece = lax.all_gather(keys_local, "strip", axis=1, tiled=True)
    values_piece = lax.all_gather(values_local, "strip", axis=1, tiled=True)
    bias_piece = lax.all_gather(key_bias, "strip", axis=1, tiled=True)
    count = keys_piece.shape[1]
    partial_scores = jnp.einsum(
        "pqhd,pkhd->phqk",
        queries,
        keys_piece.reshape(pages, count, HEADS, head_size),
        preferred_element_type=jnp.float32,
    )
    partial_scores = partial_scores * factor + bias_piece.astype(jnp.float32)[:, None, None, :]
    peak = jnp.max(partial_scores, axis=-1)
    expd = jnp.exp(partial_scores - peak[..., None])
    denom = jnp.sum(expd, axis=-1)
    logsum = peak + jnp.log(denom)
    low_prob = (expd / denom[..., None]).astype(jnp.bfloat16)
    mixed = jnp.einsum(
        "phqk,pkhd->pqhd",
        low_prob,
        values_piece.reshape(pages, whole, HEADS, head_size),
        preferred_element_type=jnp.float32,
    )
    combined = mixed.reshape(pages * length, width).astype(jnp.bfloat16)
    attended = jnp.dot(combined, output_weight, preferred_element_type=jnp.float32) + output_bias
    first_sum = source + attended
    normed = layer_norm(first_sum, first_gain, first_shift)
    ff_in = normed.astype(jnp.bfloat16)
    expanded = jnp.dot(ff_in, expand_weight, preferred_element_type=jnp.float32) + expand_bias
    activated = gelu_exact(expanded).astype(jnp.bfloat16)
    second_sum = (
        normed + jnp.dot(activated, shrink_weight, preferred_element_type=jnp.float32) + shrink_bias
    )
    result, final_back = jax.vjp(layer_norm, second_sum, final_gain, final_shift)
    encoded = result.astype(jnp.bfloat16).reshape(pages, rows, side, width)
    d_second, final_gain_grad, final_shift_grad = final_back(
        cotangent.astype(jnp.float32).reshape(pages * length, width)
    )
    d_shrunk = d_second.astype(jnp.bfloat16)
    shrink_bias_grad = column_sum(d_shrunk)
    shrink_weight_grad = left_product(activated, d_shrunk)
    d_expanded = gelu_back(expanded, right_back(d_shrunk, shrink_weight)).astype(jnp.bfloat16)
    expand_bias_grad = column_sum(d_expanded)
    expand_weight_grad = left_product(ff_in, d_expanded)
    d_normed = right_back(d_expanded, expand_weight) + d_second
    d_first, first_gain_grad, first_shift_grad = jax.vjp(
        layer_norm, first_sum, first_gain, first_shift
    )[1](d_normed)
    d_attended = d_first.astype(jnp.bfloat16)
    output_bias_grad = column_sum(d_attended)
    output_weight_grad = left_product(combined, d_attended)
    d_combined = (
        right_back(d_attended, output_weight)
        .astype(jnp.bfloat16)
        .reshape(pages, length, HEADS, head_size)
    )
    delta = jnp.sum(d_combined.astype(jnp.float32) * mixed, axis=-1)
    logsum_rows = jnp.transpose(logsum, (0, 2, 1))
    keys_all, values_again, bias_all = (
        lax.all_gather(keys_local, "strip", axis=1, tiled=True),
        lax.all_gather(values_local, "strip", axis=1, tiled=True),
        lax.all_gather(key_bias, "strip", axis=1, tiled=True),
    )
    keys_four = keys_all.reshape(pages, whole, HEADS, head_size)
    values_four = values_again.reshape(pages, whole, HEADS, head_size)
    part_scores = (
        jnp.einsum("pqhd,pkhd->phqk", queries, keys_four, preferred_element_type=jnp.float32)
        * factor
    )
    part_scores = part_scores + bias_all.astype(jnp.float32)[:, None, None, :]
    prob = jnp.exp(part_scores - jnp.transpose(logsum_rows, (0, 2, 1))[..., None])
    d_prob = jnp.einsum(
        "pqhd,pkhd->phqk", d_combined, values_four, preferred_element_type=jnp.float32
    )
    pair_d_scores = (prob * (d_prob - jnp.transpose(delta, (0, 2, 1))[..., None])).astype(
        jnp.bfloat16
    )
    weights_low = prob.astype(jnp.bfloat16)
    d_queries = factor * jnp.einsum(
        "phqk,pkhd->pqhd", pair_d_scores, keys_four, preferred_element_type=jnp.float32
    )
    key_part = factor * jnp.einsum(
        "phqk,pqhd->kphd", pair_d_scores, queries, preferred_element_type=jnp.float32
    )
    value_part = jnp.einsum(
        "phqk,pqhd->kphd", weights_low, d_combined, preferred_element_type=jnp.float32
    )
    summed = lax.psum_scatter(
        jnp.concatenate(
            [
                key_part.reshape(length * lax.axis_size("strip"), pages, width),
                value_part.reshape(length * lax.axis_size("strip"), pages, width),
            ],
            axis=-1,
        ).astype(jnp.bfloat16),
        "strip",
        scatter_dimension=0,
        tiled=True,
    ).astype(jnp.float32)
    d_keys = jnp.transpose(summed[:, :, :width], (1, 0, 2))
    d_values = jnp.transpose(summed[:, :, width:], (1, 0, 2))
    d_queries_low = d_queries.reshape(pages * length, width).astype(jnp.bfloat16)
    d_keys_low = d_keys.reshape(pages * length, width).astype(jnp.bfloat16)
    d_values_low = d_values.reshape(pages * length, width).astype(jnp.bfloat16)
    query_bias_grad = column_sum(d_queries_low)
    query_weight_grad = left_product(joint, d_queries_low)
    key_weight_grad = left_product(joint, d_keys_low)
    value_weight_grad = left_product(plain, d_values_low)
    value_bias_grad = column_sum(d_values_low)
    d_source = (
        d_first
        + right_back(d_queries_low, query_weight)
        + right_back(d_keys_low, key_weight)
        + right_back(d_values_low, value_weight)
    )
    d_source_low = d_source.astype(jnp.bfloat16)
    project_bias_grad = column_sum(d_source_low)
    project_weight_grad = left_product(block, d_source_low)
    d_block = right_back(d_source_low, project_weight).reshape(pages, rows, side, channels)
    d_second_pre = gelu_back(second_pre, d_block)
    d_late = (d_second_pre * frozen_scale[1]).astype(jnp.bfloat16)
    padded_late = pad_columns(with_halo(d_late, (("strip", 1),), 1))
    d_hidden = conv_valid(padded_late, flipped(second_kernel))
    second_kernel_grad = kernel_grad(padded_hidden, d_late)
    d_early = (gelu_back(first_pre, d_hidden) * frozen_scale[0]).astype(jnp.bfloat16)
    padded_early = pad_columns(with_halo(d_early, (("strip", 1),), 1))
    features_grad = conv_valid(padded_early, flipped(first_kernel)) + d_second_pre
    first_kernel_grad = kernel_grad(padded_in, d_early)
    first_part, second_part = (
        lax.psum_scatter(
            first_kernel_grad.astype(jnp.bfloat16), "page", scatter_dimension=2, tiled=True
        ).astype(jnp.float32),
        lax.psum_scatter(
            second_kernel_grad.astype(jnp.bfloat16), "page", scatter_dimension=2, tiled=True
        ).astype(jnp.float32),
    )
    first_part, second_part = (
        lax.psum_scatter(
            first_part.astype(jnp.bfloat16), "strip", scatter_dimension=3, tiled=True
        ).astype(jnp.float32),
        lax.psum_scatter(
            second_part.astype(jnp.bfloat16), "strip", scatter_dimension=3, tiled=True
        ).astype(jnp.float32),
    )
    dense = lax.psum(
        (
            project_weight_grad,
            project_bias_grad,
            query_weight_grad,
            query_bias_grad,
            key_weight_grad,
            value_weight_grad,
            value_bias_grad,
            output_weight_grad,
            output_bias_grad,
            first_gain_grad,
            first_shift_grad,
            expand_weight_grad,
            expand_bias_grad,
            shrink_weight_grad,
            shrink_bias_grad,
            final_gain_grad,
            final_shift_grad,
        ),
        ("page", "strip"),
    )
    return (encoded, features_grad, first_part, second_part) + tuple(dense)


MESH = pl.DeviceIdType.MESH
CORE, X, Y, Z0, Z1 = range(5)
STEPS = {CORE: 1, Y: 2, Z0: 4, Z1: 8}
PLANE, COLUMN = (X, Y), (Z0, Z1)
DENSE = (
    (64, ((CORE,), PLANE, COLUMN)),
    (64, ((CORE,), PLANE, COLUMN)),
    (64, ((CORE,), COLUMN, PLANE)),
    (64, ((CORE,), PLANE, COLUMN)),
    (64, ((CORE,), (X,), (Y,), COLUMN)),
    (32, ((CORE,), (Y,), (X,), COLUMN)),
)
GRADS = (
    ((Y,), (Z0,), (Z1,)),
    ((Z0,), (Y,), (Z1,)),
    ((Y,), (Z0,), (Z1,)),
    ((Y,), (Z0,), (Z1,)),
    ((Z0,), (Y,), (Z1,)),
    ((Y,), (Z0,), (Z1,)),
)
ENDS, MIDDLE = 5, 6
TAPS = 9
LANES = 128
WINDOW = 4.0
DELAY = 2.0
PROJECT, QUERY, VALUE, OUTPUT, FIRST_GAIN, FIRST_SHIFT, SHRINK, FINAL_GAIN, FINAL_SHIFT, EXPAND = range(10)


def own_bits():
    page, strip = lax.axis_index("page"), lax.axis_index("strip")
    bits = {name: (page // step) % 2 for name, step in STEPS.items()}
    bits[X] = strip
    peers = {}
    for names in ((CORE,), (X,), (Y,), (Z0,), (Z1,), COLUMN, PLANE, (CORE, X)):
        there = page
        for name in names:
            if name != X:
                there = there + STEPS[name] - 2 * STEPS[name] * bits[name]
        peers[names] = (there, 1 - strip if X in names else strip)
    return bits, peers


def enter(peers):
    barrier = pltpu.get_barrier_semaphore()
    for peer in peers.values():
        pl.semaphore_signal(barrier, inc=1, device_id=peer, device_id_type=MESH)
    pl.semaphore_wait(barrier, len(peers))


def remote(source, target, sends, recvs, peer):
    return pltpu.make_async_remote_copy(
        source, target, sends, recvs, device_id=peer, device_id_type=MESH
    )


def flat(order):
    return [name for stage in order for name in stage]


def slot_of(names, place):
    slot = 0
    for name in names:
        slot = slot * 2 + place[name]
    return slot


class Reduction:
    def __init__(self, order, group, bits, peers, current, parts, sends, recvs, back, keep):
        self.order, self.bits, self.peers = order, bits, peers
        self.current, self.parts = current, parts
        self.sends, self.recvs = sends, recvs
        self.whole = current if back else None
        self.keep = keep
        self.left = [group * 2 ** len(flat(order[step:])) for step in range(len(order) + 1)]
        self.flights = None

    def toward(self, names):
        for code in range(1, 2 ** len(names)):
            flips = [code >> number & 1 for number in range(len(names))]
            key = tuple(name for name, flip in zip(names, flips) if flip)
            place = {
                name: 1 - self.bits[name] if flip else self.bits[name]
                for name, flip in zip(names, flips)
            }
            yield code - 1, self.peers[key], slot_of(names, place)

    def stage(self, step):
        return self.order[min(step, 2 * len(self.order) - 1 - step)]

    def begin(self, step):
        count = len(self.order)
        level = min(step, 2 * count - 1 - step)
        names = self.stage(step)
        size = self.left[level + 1]
        self.flights = []
        mark = sum(2 ** len(self.stage(before)) - 1 for before in range(step))
        for number, peer, slot in self.toward(names):
            if step < count:
                source = self.current.at[pl.ds(slot * size, size)]
                target = self.parts.at[pl.ds(self.left[0] - self.left[step] + number * size, size)]
            else:
                first = 0
                for depth in range(level + 1):
                    first += slot_of(self.order[depth], self.bits) * self.left[depth + 1]
                source = target = self.whole.at[pl.ds(first, size)]
            flight = remote(
                source, target, self.sends.at[number], self.recvs.at[mark + number], peer
            )
            flight.start()
            self.flights.append(flight)

    def end(self, step):
        count = len(self.order)
        for flight in self.flights:
            flight.wait()
        if step >= count:
            return
        size = self.left[step + 1]
        offset = self.left[0] - self.left[step]
        total = self.current[pl.ds(slot_of(self.order[step], self.bits) * size, size)]
        total = total.astype(jnp.float32)
        for number in range(len(self.flights)):
            total += self.parts[pl.ds(offset + number * size, size)].astype(jnp.float32)
        total = total.astype(jnp.bfloat16)
        if step == count - 1:
            self.keep(total)
            return
        following = self.parts.at[pl.ds(offset, size)]
        following[...] = total
        self.current = following


class Doubling:
    def __init__(self, order, peers, sums, parts, sends, recvs):
        self.order, self.peers = order, peers
        self.sums, self.parts, self.sends, self.recvs = sums, parts, sends, recvs
        self.flight = None

    def begin(self, step):
        self.flight = remote(
            self.sums.at[step],
            self.parts.at[step],
            self.sends.at[step],
            self.recvs.at[step],
            self.peers[(self.order[step],)],
        )
        self.flight.start()

    def end(self, step):
        self.flight.wait()
        self.sums[step + 1] = self.sums[step] + self.parts[step]


def link_plan(units, window):
    events = [(ready, 1, unit, 0) for unit, (ready, _) in enumerate(units)]
    queue, busy, actions = [], {}, []
    while events:
        events.sort()
        now, kind, unit, step = events.pop(0)
        if kind == 0:
            actions.append((now, False, unit, step))
            step += 1
        if step < len(units[unit][1]):
            left = sum(max(cost.values()) + DELAY for cost in units[unit][1][step:])
            queue.append((-left, unit, step))
        queue.sort()
        held, waiting = set(), []
        for left, unit, step in queue:
            cost = units[unit][1][step]
            if any(link in held or busy.get(link, 0.0) - now >= window for link in cost):
                held.update(cost)
                waiting.append((left, unit, step))
                continue
            for link, spent in cost.items():
                busy[link] = max(now, busy.get(link, 0.0)) + spent
            actions.append((now, True, unit, step))
            events.append((max(busy[link] for link in cost) + DELAY, 0, unit, step))
        queue = waiting
    return actions


def link_costs(order, size, back):
    costs = []
    for names in order:
        size = size / 2 ** len(names)
        per_flow = size / 9e4
        if names == (CORE,):
            costs.append({CORE: size / 6e5})
        elif names == PLANE:
            costs.append({X: 4 * per_flow, Y: 4 * per_flow})
        elif names == COLUMN:
            costs.append({MIDDLE: 8 * per_flow, ENDS: 6 * per_flow})
        elif names == (Z0,):
            costs.append({ENDS: 2 * per_flow})
        elif names == (Z1,):
            costs.append({MIDDLE: 4 * per_flow, ENDS: 2 * per_flow})
        else:
            costs.append({names[0]: 2 * per_flow})
    return costs + costs[::-1] if back else costs


def shifted(value):
    side = value.shape[0]
    wide = value.astype(jnp.float32)
    column = lax.broadcasted_iota(jnp.int32, wide.shape, 0)
    later = jnp.where(column < side - 1, pltpu.roll(wide, side - 1, 0), 0.0)
    earlier = jnp.where(column > 0, pltpu.roll(wide, 1, 0), 0.0)
    return later.astype(jnp.bfloat16), earlier.astype(jnp.bfloat16)


def gelu_both(value):
    bell = 0.5 * (1.0 + lax.erf(value * math.sqrt(0.5)))
    density = jnp.exp(-0.5 * value * value) * (1.0 / math.sqrt(2.0 * math.pi))
    return value * bell, bell + value * density


def dot(left, right):
    return jnp.dot(left, right, preferred_element_type=jnp.float32)


def dot_nt(left, right):
    return lax.dot_general(
        left, right, (((1,), (1,)), ((), ())), preferred_element_type=jnp.float32
    )


def low(value):
    return value.astype(jnp.bfloat16)


def row_sum(value):
    return jnp.sum(value.astype(jnp.float32), axis=0, keepdims=True)


def norm_parts(value):
    center = value - jnp.mean(value, axis=-1, keepdims=True)
    spread = jnp.mean(center * center, axis=-1, keepdims=True)
    root = lax.rsqrt(spread + 1e-05)
    return center * root, root


def norm_back(normal, root, gain, upstream):
    weighted = upstream * gain
    return root * (
        weighted
        - jnp.mean(weighted, axis=-1, keepdims=True)
        - normal * jnp.mean(weighted * normal, axis=-1, keepdims=True)
    )


def page_kernel(side, names, *refs):
    r = SimpleNamespace(**dict(zip(names, refs)))
    width = r.w_project.shape[1]
    feat_ext = r.feat_ext
    edge = 2 * side
    length = feat_ext.shape[0] - 2 * edge
    feat = feat_ext.at[pl.ds(edge, length)]
    f32, bf16 = jnp.float32, jnp.bfloat16
    r.loads = (
        (r.features, feat),
        (r.first_kernel, r.w_first),
        (r.frozen_scale, r.v_scale),
        (r.frozen_shift, r.v_shift),
        (r.second_kernel, r.w_second),
        (r.project_weight, r.w_project),
        (r.project_bias, r.v_project),
        (r.query_weight, r.w_query),
        (r.key_weight, r.w_key),
        (r.value_weight, r.w_value),
        (r.query_bias, r.v_query),
        (r.value_bias, r.v_value),
        (r.output_weight, r.w_output),
        (r.expand_weight, r.w_expand),
        (r.shrink_weight, r.w_shrink),
        (r.cotangent, r.cot),
        (r.output_bias, r.v_output),
        (r.first_gain, r.v_first_gain),
        (r.first_shift, r.v_first_shift),
        (r.expand_bias, r.v_expand),
        (r.shrink_bias, r.v_shrink),
        (r.final_gain, r.v_final_gain),
        (r.final_shift, r.v_final_shift),
    )
    channels = feat_ext.shape[1]
    hidden_units = r.w_expand.shape[1]
    head_size = width // HEADS
    rows = length // side
    factor = head_size ** (-0.5)
    bits, peers = own_bits()
    strip, core = bits[X], bits[CORE]
    clock = [0.0]

    loads = {}
    for number, (source, target) in enumerate(r.loads):
        pieces = source.shape[0] if len(source.shape) == 3 else 1
        semaphore = r.load_sems.at[number]
        for piece in range(pieces):
            at = pl.ds(piece, 1) if pieces > 1 else pl.ds(0, source.shape[0])
            pltpu.make_async_copy(source.at[at], target.at[at], semaphore).start()
        loads[number] = pltpu.make_async_copy(source, target, semaphore)
    enter(peers)

    exchanged = [0]

    def exchange(source, target, peer):
        number = exchanged[0]
        exchanged[0] += 1
        copy = remote(source, target, r.pair_sends.at[number], r.pair_recvs.at[number], peer)
        copy.start()
        return copy

    def aligned(start, size, unit=side):
        return pl.ds(pl.multiple_of(start, unit), size)

    own_edge = (1 - strip) * (length - edge)
    feat_halo = exchange(
        r.features.at[aligned(own_edge, edge)],
        r.feat_ext.at[aligned(strip * (length + edge), edge)],
        peers[(X,)],
    )

    turn, height, breadth = r.quarter_turns[0], r.heights[0], r.widths[0]
    odd = turn % 2
    lane = lax.broadcasted_iota(jnp.int32, (side, LANES), 1)
    count = lax.broadcasted_iota(jnp.int32, (side, LANES), 0)
    inverse = jnp.exp((lane // 2).astype(f32) * (-2.0 * math.log(10000.0) / LANES))
    row_place = strip * rows + count
    row_place = jnp.where(row_place >= side, row_place - side, row_place)
    row_flip = ((turn == 1) | (turn == 2)).astype(jnp.int32)
    column_flip = (turn // 2) % 2
    for place, flip, extent, first, table, bias in (
        (
            row_place,
            row_flip,
            height + odd * (breadth - height),
            1 - odd,
            r.table_row,
            r.bias_row,
        ),
        (
            count,
            column_flip,
            breadth + odd * (height - breadth),
            odd,
            r.table_col,
            r.bias_col,
        ),
    ):
        place = place + flip * (side - 1 - 2 * place)
        along = (place + 1).astype(f32) / (jnp.full((side, LANES), extent).astype(f32) + 1e-06)
        phase = along * (2.0 * math.pi) * inverse
        sines = jnp.where(lane % 2 == 0, jnp.sin(phase), jnp.cos(phase))
        share = jnp.full((side, LANES), first).astype(f32)
        table[:, pl.ds(0, LANES)] = sines * share
        table[:, pl.ds(LANES, LANES)] = sines * (1.0 - share)
        bias[...] = jnp.where(place < extent, 0.0, -10000.0)

    pool, dense, owned = r.pool, r.dense, r.owned
    dense_units = len(DENSE)
    reducers, costs = [], []
    ready_dense = [30.0, 30.2, 30.4, 30.6, 43.0, 44.0]
    unit_slots = 24
    begin, marks = 0, 0
    for unit, (slots, order) in enumerate(DENSE):
        group = slots // 32

        def keep_dense(value, begin=begin, group=group, order=order):
            dense[pl.ds(begin + slot_of(flat(order), bits) * group, group)] = value

        reducers.append(
            Reduction(
                order,
                group,
                bits,
                peers,
                dense.at[pl.ds(begin, slots)],
                r.dense_parts.at[pl.ds(begin, slots)],
                r.dense_sends.at[pl.ds(3 * unit, 3)],
                r.dense_recvs.at[pl.ds(14 * unit, 14)],
                True,
                keep_dense,
            )
        )
        costs.append((ready_dense[unit], link_costs(order, slots * 8192, True)))
        begin += slots
    for unit, order in enumerate(GRADS):

        def keep_grad(value, unit=unit):
            half = value.shape[1] // 2
            for across in range(3):
                tap = unit % 3 * 3 + across
                owned[unit // 3, 0, tap] = value[across, :half]
                owned[unit // 3, 1, tap] = value[across, half:]

        reducers.append(
            Reduction(
                order,
                3,
                bits,
                peers,
                pool.at[pl.ds(unit * unit_slots, unit_slots)],
                r.parts.at[unit],
                r.grad_sends.at[pl.ds(unit, 1)],
                r.grad_recvs.at[pl.ds(3 * unit, 3)],
                False,
                keep_grad,
            )
        )
        made = 53.0 + unit if unit < 3 else 61.0 + unit - 3
        costs.append((made, link_costs(order, 393216, False)))
    small_order = (CORE, X, Y, Z0, Z1)
    small = r.small_sums
    reducers.append(
        Doubling(
            small_order, peers, small, r.small_parts, r.small_sends, r.small_recvs
        )
    )
    costs.append((44.0, [{CORE: 0.2}, {X: 0.5}, {Y: 0.5}, {ENDS: 0.5}, {MIDDLE: 1.0, ENDS: 0.5}]))
    agenda = link_plan(costs, WINDOW)

    def work(spent):
        clock[0] += spent
        while agenda and agenda[0][0] <= clock[0]:
            _, begins, unit, step = agenda.pop(0)
            if begins:
                reducers[unit].begin(step)
            else:
                reducers[unit].end(step)

    stores = []

    def store(source, target):
        stores.append(pltpu.make_async_copy(source, target, r.out_sems.at[len(stores)]))
        stores[-1].start()

    def settle(at):
        clock[0] = at
        work(0.0)

    def spread(source, target, first, count):
        def one(row, carry):
            at = aligned(row * side, side)
            value = source[at]
            later, earlier = shifted(value)
            target[0, at] = later
            target[1, at] = value
            target[2, at] = earlier
            return carry

        lax.fori_loop(first, first + count, one, 0)

    def conv(x3, weight, start, count, transposed):
        total = None
        for tap in range(TAPS):
            down, across = tap // 3, tap % 3
            if transposed:
                window = pl.ds(start + side * (2 - down), count)
                term = dot_nt(x3[across, window], weight[tap])
            else:
                window = pl.ds(start + side * down, count)
                term = dot(x3[2 - across, window], weight[tap])
            total = term if total is None else total + term
        return total

    x3 = r.x3
    scale, shift = r.v_scale, r.v_shift

    def vector(ref, piece=0):
        return ref[pl.ds(piece * width, width)].reshape(1, width)


    loads[0].wait()
    feat_ext[aligned(strip * (length + edge), edge)] = jnp.zeros((edge, channels), bf16)
    spread(feat_ext, x3, 2, rows)
    own_lanes = aligned(strip * length, length, length)
    other_lanes = aligned((1 - strip) * length, length, length)

    def share(every, lanes, source_page, target_page, peer):
        return exchange(every.at[source_page, :, lanes], every.at[target_page, :, lanes], peer)

    r.features_all[0, :, own_lanes] = feat[...].T
    feat_copies = [
        share(r.features_all, own_lanes, 0, 0, peers[(X,)]),
        share(r.features_all, own_lanes, 0, 1, peers[(CORE,)]),
    ]
    for number in (1, 2, 3):
        loads[number].wait()
    feat_halo.wait()
    spread(feat_ext, x3, 0, 2)
    spread(feat_ext, x3, rows + 2, 2)
    hidden = r.hidden
    half_rows = (length + edge) // 2
    for part in range(2):
        at = pl.ds(part * half_rows, half_rows)
        pre = conv(x3, r.w_first, part * half_rows, half_rows, False)
        value, slope = gelu_both(pre * scale[0:1] + shift[0:1])
        hidden[at] = low(value)
        r.slope_first[at] = slope * scale[0:1]
    for begin, inside in ((0, strip), (length + side, 1 - strip)):
        at = pl.ds(begin, side)
        keep = jnp.broadcast_to(inside, (side, channels)).astype(f32)
        hidden[at] = low(hidden[at].astype(f32) * keep)
        r.slope_first[at] = r.slope_first[at] * keep
    spread(hidden, x3, 0, rows + 2)
    r.hidden_all[0, :, own_lanes] = hidden[pl.ds(side, length)].T

    for number in (4, 5, 6):
        loads[number].wait()
    block, source, plain = r.block, r.source, r.plain
    half = length // 2
    plain_copies = []
    for part in range(2):
        at = pl.ds(part * half, half)
        pre = conv(x3, r.w_second, part * half, half, False)
        value, slope = gelu_both(pre * scale[1:2] + shift[1:2] + feat[at].astype(f32))
        block[at] = low(value)
        r.direct[at] = slope
        rows_here = dot(block[at], r.w_project[...]) + vector(r.v_project)
        source[at] = rows_here
        plain[at] = low(rows_here)
        plain_copies.append(
            exchange(plain.at[at], plain.at[pl.ds(length + part * half, half)], peers[(X,)])
        )
    for number in range(7, 12):
        loads[number].wait()

    joint, keys, values = r.joint, r.keys, r.values
    keys_t, values_t = r.keys_t, r.values_t
    table_row, table_col = r.table_row, r.table_col
    bias_row, bias_col = r.bias_row, r.bias_col

    def keys_of(which):
        base = which * length
        for row in range(rows):
            at = pl.ds(base + row * side, side)
            index = which * rows + row
            position = table_row[index : index + 1] + table_col[...]
            rows_here = source[pl.ds(row * side, side)] if which == 0 else plain[at].astype(f32)
            joint[at] = low(rows_here + position)
            r.bias[at] = jnp.minimum(bias_row[index : index + 1], bias_col[...])
        at = pl.ds(base, length)
        keys[at] = low(dot(joint[at], r.w_key[...]))
        values[at] = low(dot(plain[at], r.w_value[...]) + vector(r.v_value))
        keys_t[which] = keys[at].T
        values_t[which] = values[at].T

    lane_head = lax.broadcasted_iota(jnp.int32, (1, width), 1) // head_size

    def only(head, value):
        return jnp.where(lane_head == head, value, 0).astype(bf16)

    quarter = length // LANES
    tile = length // 64

    def pool_at(which, head, lane):
        return pl.ds(((which * HEADS + head) * quarter + lane) * tile, tile)

    keys_of(0)
    queries = r.queries
    queries[...] = low(dot(joint[pl.ds(0, length)], r.w_query[...]) + vector(r.v_query))
    stat, mixed_parts = r.stat, r.mixed_parts

    def attend(which):
        def one(head, carry):
            at = pl.ds(which * length, length)
            scores = dot_nt(keys[at], only(head, queries[...])) * factor
            bias = r.bias[at]
            scores = scores + jnp.concatenate([bias] * quarter, axis=1)
            peak = jnp.max(scores, axis=0, keepdims=True)
            powers = jnp.exp(scores - peak)
            stat[head, 2 * which : 2 * which + 1] = peak
            stat[head, 2 * which + 1 : 2 * which + 2] = jnp.sum(powers, axis=0, keepdims=True)
            powers = low(powers)
            for lane in range(quarter):
                pool[pool_at(which, head, lane)] = powers[
                    :, lane * LANES : (lane + 1) * LANES
                ].reshape(tile, 64, LANES)
            channel = aligned(head * head_size, head_size, head_size)
            mixed_parts[which, channel] = dot(values_t[which, channel], powers)
            return carry

        lax.fori_loop(0, HEADS, one, 0)

    attend(0)
    for copy in plain_copies + feat_copies:
        copy.wait()
    hidden_copies = [
        share(r.hidden_all, own_lanes, 0, 0, peers[(X,)]),
        share(r.hidden_all, own_lanes, 0, 1, peers[(CORE,)]),
    ]
    feat_relay = share(r.features_all, other_lanes, 0, 1, peers[(CORE,)])
    keys_of(1)
    attend(1)

    shares_t = r.shares_t
    for head in range(HEADS):
        channel = pl.ds(head * head_size, head_size)
        first_peak, first_sum = stat[head, 0:1], stat[head, 1:2]
        second_peak, second_sum = stat[head, 2:3], stat[head, 3:4]
        peak = jnp.maximum(first_peak, second_peak)
        first_scale, second_scale = jnp.exp(first_peak - peak), jnp.exp(second_peak - peak)
        total = first_scale * first_sum + second_scale * second_sum
        first_scale, second_scale = first_scale / total, second_scale / total
        stat[head, 4:5] = first_scale
        stat[head, 5:6] = second_scale
        shares_t[0, channel] = jnp.broadcast_to(first_scale, (head_size, length))
        shares_t[1, channel] = jnp.broadcast_to(second_scale, (head_size, length))
    mixed = (shares_t[0] * mixed_parts[0] + shares_t[1] * mixed_parts[1]).T
    combined = r.combined
    combined[...] = low(mixed)

    for number in range(12, len(loads)):
        loads[number].wait()
    small[...] = jnp.zeros_like(small)
    activated, d_expanded = r.activated, r.d_expanded
    ff_in, d_shrunk, d_attended, d_first = r.ff_in, r.d_shrunk, r.d_attended, source
    d_combined = r.d_combined
    chunk = 256
    pieces = hidden_units // width

    def tokens(step, carry):
        at = aligned(step * chunk, chunk, chunk)
        first_total = source[at] + dot(combined[at], r.w_output[...]) + vector(r.v_output)
        first_normal, first_root = norm_parts(first_total)
        normed = first_normal * vector(r.v_first_gain) + vector(r.v_first_shift)
        ff = low(normed)
        ff_in[at] = ff
        slopes = []
        shrunk = None
        for piece in range(pieces):
            lane = pl.ds(piece * width, width)
            expanded = dot(ff, r.w_expand[:, lane]) + vector(r.v_expand, piece)
            value, slope = gelu_both(expanded)
            value = low(value)
            activated[at, lane] = value
            slopes.append(slope)
            term = dot(value, r.w_shrink[lane])
            shrunk = term if shrunk is None else shrunk + term
        second_total = normed + shrunk + vector(r.v_shrink)
        second_normal, second_root = norm_parts(second_total)
        r.encoded_here[at] = low(
            second_normal * vector(r.v_final_gain) + vector(r.v_final_shift)
        )
        upstream = r.cot[at].astype(f32)
        small[0, FINAL_GAIN : FINAL_GAIN + 1] += row_sum(upstream * second_normal)
        small[0, FINAL_SHIFT : FINAL_SHIFT + 1] += row_sum(upstream)
        d_second = norm_back(second_normal, second_root, vector(r.v_final_gain), upstream)
        d_low = low(d_second)
        d_shrunk[at] = d_low
        small[0, SHRINK : SHRINK + 1] += row_sum(d_low)
        d_normed = d_second
        for piece in range(pieces):
            lane = pl.ds(piece * width, width)
            d_piece = low(dot_nt(d_low, r.w_shrink[lane]) * slopes[piece])
            d_expanded[at, lane] = d_piece
            small[0, EXPAND + piece : EXPAND + piece + 1] += row_sum(d_piece)
            d_normed = d_normed + dot_nt(d_piece, r.w_expand[:, lane])
        small[0, FIRST_GAIN : FIRST_GAIN + 1] += row_sum(d_normed * first_normal)
        small[0, FIRST_SHIFT : FIRST_SHIFT + 1] += row_sum(d_normed)
        d_total = norm_back(first_normal, first_root, vector(r.v_first_gain), d_normed)
        d_first[at] = d_total
        d_low = low(d_total)
        d_attended[at] = d_low
        small[0, OUTPUT : OUTPUT + 1] += row_sum(d_low)
        d_combined[at] = low(dot_nt(d_low, r.w_output[...]))
        return carry

    lax.fori_loop(0, length // chunk, tokens, 0)

    store(r.encoded_here, r.encoded)

    def put(unit, value):
        dense[pl.ds(unit * 32, 32)] = low(value).reshape(32, 16, width)

    for part in range(hidden_units // 512):
        lane = pl.ds(part * 512, 512)
        put(part, dot(activated[:, lane].T, d_shrunk[...]))
    ff_t = ff_in[...].T
    for part in range(pieces // 2):
        both = dot(ff_t, d_expanded[:, pl.ds(part * 512, 512)])
        put(4 + part, jnp.concatenate([both[:, :width], both[:, width:]], axis=0))
    settle(30.0)

    deltas = r.deltas
    d_scaled = r.d_scaled
    total = None
    for which in range(2):
        scaled = low(d_combined[...].astype(f32) * shares_t[which].T)
        d_scaled[which] = scaled
        term = scaled.T.astype(f32) * mixed_parts[which]
        total = term if total is None else total + term
    for head in range(HEADS):
        delta = jnp.sum(total[head * head_size : (head + 1) * head_size], axis=0, keepdims=True)
        deltas[head, 0:1] = delta * stat[head, 4:5]
        deltas[head, 1:2] = delta * stat[head, 5:6]
    work(0.5)
    d_queries_t = r.d_queries_t
    d_queries_t[...] = jnp.zeros_like(d_queries_t)
    spare_query, spare_scaled = activated, d_expanded
    for head in range(HEADS):
        spare_query[:, pl.ds(head * width, width)] = only(head, queries[...])

    def stacked(which):
        return jnp.concatenate(
            [
                pool[pool_at(which, head, lane)].reshape(length, LANES)
                for head in range(HEADS)
                for lane in range(quarter)
            ],
            axis=1,
        )

    def heads_down(wide):
        return jnp.concatenate(
            [wide[:, pl.ds(head * width, width)] for head in range(HEADS)], axis=0
        )

    def attend_back(which):
        at = pl.ds(which * length, length)
        for head in range(HEADS):
            spare_scaled[:, pl.ds(head * width, width)] = only(head, d_scaled[which])
        d_values = low(dot(stacked(which), heads_down(spare_scaled)))
        work(1.2)
        for head in range(HEADS):
            d_prob = dot_nt(values[at], spare_scaled[:, pl.ds(head * width, width)])
            d_prob = d_prob - deltas[head, which : which + 1]
            pieces_here = []
            for lane in range(quarter):
                powers = pool[pool_at(which, head, lane)].reshape(length, LANES).astype(f32)
                d_tile = low(powers * d_prob[:, lane * LANES : (lane + 1) * LANES])
                pool[pool_at(which, head, lane)] = d_tile.reshape(tile, 64, LANES)
                pieces_here.append(d_tile)
            channel = pl.ds(head * head_size, head_size)
            d_queries_t[channel] += dot(
                keys_t[which, channel], jnp.concatenate(pieces_here, axis=1)
            )
            work(0.3)
        d_keys = low(dot(stacked(which), heads_down(spare_query)) * factor)
        work(1.2)
        d_rows = dot_nt(d_keys, r.w_key[...]) + dot_nt(d_values, r.w_value[...])
        small[0, VALUE : VALUE + 1] += row_sum(d_values)
        return (
            d_rows,
            dot(joint[at].T, d_keys),
            dot(plain[at].T, d_values),
        )

    d_other, key_grad, value_grad = attend_back(1)
    d_combined[...] = low(d_other)
    d_rows_copy = exchange(d_combined, r.d_rows_in, peers[(X,)])
    work(0.3)
    d_own, more_key, more_value = attend_back(0)
    d_queries = low(d_queries_t[...].T * factor)
    small[0, QUERY : QUERY + 1] = row_sum(d_queries)
    joint_t = joint[pl.ds(0, length)].T
    put(
        8,
        jnp.concatenate([dot(joint_t, d_queries), key_grad + more_key], axis=0),
    )
    put(
        9,
        jnp.concatenate([value_grad + more_value, dot(combined[...].T, d_attended[...])], axis=0),
    )
    settle(43.0)
    d_source = d_first[...] + dot_nt(d_queries, r.w_query[...]) + d_own
    d_rows_copy.wait()
    d_source = low(d_source + r.d_rows_in[...].astype(f32))
    small[0, PROJECT : PROJECT + 1] = row_sum(d_source)
    direct = r.direct
    late_ext = r.late_ext
    late = late_ext.at[pl.ds(edge, length)]
    direct[...] = dot_nt(d_source, r.w_project[...]) * r.direct[...]
    late[...] = low(direct[...] * scale[1:2])

    blank = jnp.zeros((edge, channels), bf16)
    halo = exchange(
        late_ext.at[aligned(edge + own_edge, edge)],
        late_ext.at[aligned(strip * (length + edge), edge)],
        peers[(X,)],
    )

    def spread_out(source, first, target):
        copies = []
        there = aligned(side + strip * length, length)
        for peer, page, strip_there, core_there in (
            ((X,), 0, 1 - strip, core),
            ((CORE, X), 1, 1 - strip, 1 - core),
            ((CORE,), 1, strip, 1 - core),
        ):
            lane_here = aligned(strip_there * 2 * LANES + core_there * LANES, LANES, LANES)
            copies.append(
                exchange(
                    source.at[pl.ds(first, length), lane_here], target.at[page, there], peers[peer]
                )
            )
        lane_here = aligned(strip * 2 * LANES + core * LANES, LANES, LANES)
        target[0, there] = source[pl.ds(first, length), lane_here]
        for page in range(2):
            target[page, pl.ds(0, side)] = blank[:side, :LANES]
            target[page, pl.ds(side + 2 * length, side)] = blank[:side, :LANES]
        return copies

    late_copies = spread_out(late_ext, edge, r.late_page)
    late_ext[aligned(strip * (length + edge), edge)] = blank
    spread(late_ext, x3, 2, rows)
    put(10, dot(block[...].T, d_source))
    settle(44.0)
    for copy in hidden_copies:
        copy.wait()
    hidden_relay = share(r.hidden_all, other_lanes, 0, 1, peers[(CORE,)])
    halo.wait()
    spread(late_ext, x3, 0, 2)
    spread(late_ext, x3, rows + 2, 2)
    early = hidden
    for part in range(2):
        at = pl.ds(part * half_rows, half_rows)
        d_hidden = conv(x3, r.w_second, part * half_rows, half_rows, True)
        early[at] = low(d_hidden * r.slope_first[at])
        work(1.5)
    early_copies = spread_out(early, side, r.early_page)
    page3 = r.page3

    def spread_pages(source):
        def one(row, carry):
            at = aligned(row * side, side)
            for page in range(2):
                value = source[page, at]
                later, earlier = shifted(value)
                page3[page, 0, at] = later
                page3[page, 1, at] = value
                page3[page, 2, at] = earlier
            return carry

        lax.fori_loop(0, 2 * rows + 2, one, 0)

    def kernel_grads(left, first_unit):
        for down in range(3):
            window = pl.ds(side * (2 - down), 2 * length)
            product = None
            for page in range(2):
                right = jnp.concatenate([page3[page, across, window] for across in range(3)], axis=1)
                term = dot(left[page], right)
                product = term if product is None else product + term
            product = low(product)
            unit = first_unit + down
            order = reducers[dense_units + unit].order
            size = product.shape[0] // 8
            for chip in range(8):
                place = {Y: chip % 2, Z0: chip // 2 % 2, Z1: chip // 4}
                for across in range(3):
                    pool[unit * unit_slots + slot_of(flat(order), place) * 3 + across] = product[
                        chip * size : (chip + 1) * size, across * LANES : (across + 1) * LANES
                    ]
            work(1.0)

    for copy in late_copies + [hidden_relay, feat_relay]:
        copy.wait()
    spread_pages(r.late_page)
    settle(52.0)
    kernel_grads(r.hidden_all, 0)
    spread(early, x3, 0, rows + 2)
    for part in range(2):
        at = pl.ds(part * half, half)
        direct[at] = conv(x3, r.w_first, part * half, half, True) + direct[at]
        work(1.3)
    store(direct, r.features_grad)
    for copy in early_copies:
        copy.wait()
    spread_pages(r.early_page)
    settle(60.0)
    kernel_grads(r.features_all, 3)
    settle(1e9)
    store(small.at[5], r.small_out)
    store(dense, r.dense_out)
    finals = []
    for which, here, out in (
        (1, r.first_here, r.first_grad),
        (0, r.second_here, r.second_grad),
    ):
        copy = exchange(owned.at[which, 1 - core], r.owned_sib.at[which], peers[(CORE,)])
        finals.append((copy, which, here, out))
    for copy, which, here, out in finals:
        copy.wait()
        here[:, :, aligned(core * LANES, LANES, LANES)] = owned[which, core].astype(f32)
        here[:, :, aligned((1 - core) * LANES, LANES, LANES)] = r.owned_sib[which].astype(f32)
        store(here, out)
    for copy in stores:
        copy.wait()


def page_call(side, inputs):
    f32, bf16 = jnp.float32, jnp.bfloat16
    length, channels = inputs["features"].shape
    width = inputs["project_weight"].shape[1]
    hidden_units = inputs["expand_weight"].shape[1]
    edge = 2 * side
    dense_shape = ((2 * hidden_units + channels + 4 * width) // 16, 16, width)
    hbm = pl.BlockSpec(memory_space=pl.ANY)
    sems = pltpu.SemaphoreType.DMA
    def place(array):
        return smem if array.dtype == jnp.int32 else hbm

    smem = pl.BlockSpec(memory_space=pltpu.SMEM)
    outs = dict(
        encoded=((length, width), bf16),
        features_grad=((length, channels), f32),
        first_grad=((TAPS, channels // 16, channels // 2), f32),
        second_grad=((TAPS, channels // 16, channels // 2), f32),
        dense_out=(dense_shape, bf16),
        small_out=((24, width), f32),
    )
    scratch = dict(
        w_first=((TAPS, channels, channels), bf16),
        w_second=((TAPS, channels, channels), bf16),
        w_project=((channels, width), bf16),
        w_query=((width, width), bf16),
        w_key=((width, width), bf16),
        w_value=((width, width), bf16),
        w_output=((width, width), bf16),
        w_expand=((width, hidden_units), bf16),
        w_shrink=((hidden_units, width), bf16),
        cot=((length, width), bf16),
        v_scale=(inputs["frozen_scale"].shape, f32),
        v_shift=(inputs["frozen_shift"].shape, f32),
        v_project=((width,), f32),
        v_query=((width,), f32),
        v_value=((width,), f32),
        v_output=((width,), f32),
        v_first_gain=((width,), f32),
        v_first_shift=((width,), f32),
        v_expand=((hidden_units,), f32),
        v_shrink=((width,), f32),
        v_final_gain=((width,), f32),
        v_final_shift=((width,), f32),
        encoded_here=((length, width), bf16),
        direct=((length, channels), f32),
        first_here=((TAPS, channels // 16, channels // 2), f32),
        second_here=((TAPS, channels // 16, channels // 2), f32),
        table_row=((side, width), f32),
        table_col=((side, width), f32),
        bias_row=((side, LANES), f32),
        bias_col=((side, LANES), f32),
        feat_ext=((length + 2 * edge, channels), bf16),
        x3=((3, length + 2 * edge, channels), bf16),
        hidden=((length + edge, channels), bf16),
        slope_first=((length + edge, channels), f32),
        features_all=((2, channels, 2 * length), bf16),
        hidden_all=((2, channels, 2 * length), bf16),
        block=((length, channels), bf16),
        source=((length, width), f32),
        plain=((2 * length, width), bf16),
        joint=((2 * length, width), bf16),
        bias=((2 * length, LANES), f32),
        keys=((2 * length, width), bf16),
        values=((2 * length, width), bf16),
        keys_t=((2, width, length), bf16),
        values_t=((2, width, length), bf16),
        queries=((length, width), bf16),
        stat=((HEADS, 8, length), f32),
        deltas=((HEADS, 8, length), f32),
        mixed_parts=((2, width, length), f32),
        shares_t=((2, width, length), f32),
        combined=((length, width), bf16),
        activated=((length, hidden_units), bf16),
        d_expanded=((length, hidden_units), bf16),
        ff_in=((length, width), bf16),
        d_shrunk=((length, width), bf16),
        d_attended=((length, width), bf16),
        d_combined=((length, width), bf16),
        d_scaled=((2, length, width), bf16),
        d_queries_t=((width, length), f32),
        d_rows_in=((length, width), bf16),
        late_ext=((length + 2 * edge, channels), bf16),
        late_page=((2, 2 * length + edge, LANES), bf16),
        early_page=((2, 2 * length + edge, LANES), bf16),
        page3=((2, 3, 2 * length + edge, LANES), bf16),
        pool=((2 * HEADS * (length // LANES) * (length // 64), 64, LANES), bf16),
        parts=((6, 21, 64, LANES), bf16),
        dense=(dense_shape, bf16),
        dense_parts=(dense_shape, bf16),
        small_sums=((6, 24, width), f32),
        small_parts=((5, 24, width), f32),
        owned=((2, 2, TAPS, channels // 16, LANES), bf16),
        owned_sib=((2, TAPS, channels // 16, LANES), bf16),
    )
    sem_shapes = dict(
        load_sems=(23,),
        out_sems=(6,),
        pair_sends=(20,),
        pair_recvs=(20,),
        grad_sends=(6,),
        grad_recvs=(18,),
        dense_sends=(3 * len(DENSE),),
        dense_recvs=(14 * len(DENSE),),
        small_sends=(5,),
        small_recvs=(5,),
    )
    names = list(inputs) + list(outs) + list(scratch) + list(sem_shapes)
    results = pl.pallas_call(
        functools.partial(page_kernel, side, names),
        out_shape=tuple(jax.ShapeDtypeStruct(*spec) for spec in outs.values()),
        in_specs=[place(array) for array in inputs.values()],
        out_specs=tuple([hbm] * len(outs)),
        scratch_shapes=[pltpu.VMEM(*spec) for spec in scratch.values()]
        + [sems(shape) for shape in sem_shapes.values()],
        compiler_params=pltpu.CompilerParams(
            collective_id=0, has_side_effects=True, vmem_limit_bytes=63 * 1024 * 1024
        ),
        name="page_step",
    )(*inputs.values())
    return SimpleNamespace(**dict(zip(outs, results)))


def unpack_kernel(passed, dense_hbm, small_hbm, *refs):
    f32 = jnp.float32
    through, refs = refs[:passed], refs[passed:]
    through_out, refs = refs[:passed], refs[passed:]
    held, refs = refs[len(refs) - passed :], refs[: len(refs) - passed]
    outs, (dense, wide, small, vector, vector_wide, in_sems, out_sems) = refs[:-7], refs[-7:]
    project, project_b, query, query_b, key, value, value_b, output, output_b = outs[:9]
    first_gain, first_shift, expand, expand_b, shrink, shrink_b, final_gain, final_shift = outs[9:]
    width = dense.shape[2]
    copies = []

    def send(source, target):
        copies.append(pltpu.make_async_copy(source, target, out_sems.at[len(copies)]))
        copies[-1].start()

    units = dense.shape[0] // 32
    loads = [pltpu.make_async_copy(small_hbm, small, in_sems.at[0])]
    for unit in range(units):
        at = pl.ds(32 * unit, 32)
        loads.append(
            pltpu.make_async_copy(dense_hbm.at[at], dense.at[at], in_sems.at[len(loads)])
        )
    for source, target in zip(through, held):
        loads.append(pltpu.make_async_copy(source, target, in_sems.at[len(loads)]))
    for load in loads:
        load.start()
    loads[0].wait()
    for number, (row, out) in enumerate(
        (
            (PROJECT, project_b),
            (QUERY, query_b),
            (VALUE, value_b),
            (OUTPUT, output_b),
            (FIRST_GAIN, first_gain),
            (FIRST_SHIFT, first_shift),
            (SHRINK, shrink_b),
            (FINAL_GAIN, final_gain),
            (FINAL_SHIFT, final_shift),
        )
    ):
        vector[pl.ds(number * width, width)] = small[row]
        send(vector.at[pl.ds(number * width, width)], out)
    for piece in range(expand_b.shape[0] // width):
        vector_wide[pl.ds(piece * width, width)] = small[EXPAND + piece]
    send(vector_wide, expand_b)

    def widen(unit):
        loads[1 + unit].wait()
        wide[unit] = dense[pl.ds(32 * unit, 32)].reshape(512, width).astype(f32)
        return wide.at[unit]

    for part in range(4):
        send(widen(part), shrink.at[pl.ds(part * 512, 512)])
        both = widen(4 + part)
        send(both.at[pl.ds(0, width)], expand.at[:, pl.ds(part * 512, width)])
        send(both.at[pl.ds(width, width)], expand.at[:, pl.ds(part * 512 + width, width)])
    both = widen(8)
    send(both.at[pl.ds(0, width)], query)
    send(both.at[pl.ds(width, width)], key)
    both = widen(9)
    send(both.at[pl.ds(0, width)], value)
    send(both.at[pl.ds(width, width)], output)
    send(widen(10), project)
    for load, source, target in zip(loads[1 + units :], held, through_out):
        load.wait()
        send(source, target)
    for copy in copies:
        copy.wait()


def paired_body(
    features,
    quarter_turns,
    heights,
    widths,
    frozen_scale,
    frozen_shift,
    first_kernel,
    second_kernel,
    project_weight,
    project_bias,
    query_weight,
    query_bias,
    key_weight,
    value_weight,
    value_bias,
    output_weight,
    output_bias,
    first_gain,
    first_shift,
    expand_weight,
    expand_bias,
    shrink_weight,
    shrink_bias,
    final_gain,
    final_shift,
    cotangent,
):
    pages, rows, side, channels = features.shape
    width = project_weight.shape[1]
    hidden_units = expand_weight.shape[1]
    length = rows * side
    got = page_call(
        side,
        dict(
            features=features.reshape(length, channels),
            first_kernel=first_kernel.reshape(TAPS, channels, channels),
            second_kernel=second_kernel.reshape(TAPS, channels, channels),
            project_weight=project_weight,
            query_weight=query_weight,
            key_weight=key_weight,
            value_weight=value_weight,
            output_weight=output_weight,
            expand_weight=expand_weight,
            shrink_weight=shrink_weight,
            cotangent=cotangent.reshape(length, width),
            frozen_scale=frozen_scale,
            frozen_shift=frozen_shift,
            project_bias=project_bias,
            query_bias=query_bias,
            value_bias=value_bias,
            output_bias=output_bias,
            first_gain=first_gain,
            first_shift=first_shift,
            expand_bias=expand_bias,
            shrink_bias=shrink_bias,
            final_gain=final_gain,
            final_shift=final_shift,
            quarter_turns=quarter_turns,
            heights=heights,
            widths=widths,
        ),
    )
    f32 = jnp.float32
    square, vector = (width, width), (width,)
    shapes = [
        (channels, width),
        vector,
        square,
        vector,
        square,
        square,
        vector,
        square,
        vector,
        vector,
        vector,
        (width, hidden_units),
        (hidden_units,),
        (hidden_units, width),
        vector,
        vector,
        vector,
    ]
    hbm = pl.BlockSpec(memory_space=pl.ANY)
    passed = (got.encoded, got.features_grad, got.first_grad, got.second_grad)
    dense = got.dense_out
    results = pl.pallas_call(
        functools.partial(unpack_kernel, len(passed)),
        out_shape=tuple(jax.ShapeDtypeStruct(value.shape, value.dtype) for value in passed)
        + tuple(jax.ShapeDtypeStruct(shape, f32) for shape in shapes),
        in_specs=[hbm] * (2 + len(passed)),
        out_specs=tuple([hbm] * (len(passed) + len(shapes))),
        scratch_shapes=[
            pltpu.VMEM(dense.shape, jnp.bfloat16),
            pltpu.VMEM((dense.shape[0] // 32, 512, width), f32),
            pltpu.VMEM(got.small_out.shape, f32),
            pltpu.VMEM((9 * width,), f32),
            pltpu.VMEM((hidden_units,), f32),
            pltpu.SemaphoreType.DMA((1 + dense.shape[0] // 32 + len(passed),)),
            pltpu.SemaphoreType.DMA((32,)),
        ]
        + [pltpu.VMEM(value.shape, value.dtype) for value in passed],
        compiler_params=pltpu.CompilerParams(vmem_limit_bytes=63 * 1024 * 1024),
        name="unpack",
    )(dense, got.small_out, *passed)
    part_shape = (3, 3, channels // 16, channels // 2)
    return (
        results[0].reshape(pages, rows, side, width),
        results[1].reshape(pages, rows, side, channels),
        results[2].reshape(part_shape),
        results[3].reshape(part_shape),
    ) + tuple(results[len(passed) :])


def solution(mesh):
    paired = mesh.shape["strip"] == 2 and mesh.shape["page"] == 16
    return jax.shard_map(
        paired_body if paired else body,
        mesh=mesh,
        in_specs=(
            P("page", "strip", None, None),
            P("page"),
            P("page"),
            P("page"),
            P(),
            P(),
            P(),
            P(),
            P(),
            P(),
            P(),
            P(),
            P(),
            P(),
            P(),
            P(),
            P(),
            P(),
            P(),
            P(),
            P(),
            P(),
            P(),
            P(),
            P(),
            P("page", "strip", None, None),
        ),
        out_specs=(
            P("page", "strip", None, None),
            P("page", "strip", None, None),
            P(None, None, "page", "strip"),
            P(None, None, "page", "strip"),
            P(),
            P(),
            P(),
            P(),
            P(),
            P(),
            P(),
            P(),
            P(),
            P(),
            P(),
            P(),
            P(),
            P(),
            P(),
            P(),
            P(),
        ),
        check_vma=False,
    )
```

```python
import functools
import math
from types import SimpleNamespace

import jax
import jax.numpy as jnp
from jax import lax
from jax.experimental import pallas as pl
from jax.experimental.pallas import tpu as pltpu
from jax.sharding import PartitionSpec as P

HEADS = 8


def with_halo(block, sides, width):
    for axis, dim in sides:
        count = lax.axis_size(axis)
        forward = [(i, i + 1) for i in range(count - 1)]
        backward = [(target, source) for source, target in forward]
        low = lax.ppermute(
            lax.slice_in_dim(block, block.shape[dim] - width, None, axis=dim), axis, forward
        )
        high = lax.ppermute(lax.slice_in_dim(block, 0, width, axis=dim), axis, backward)
        block = jnp.concatenate([low, block, high], axis=dim)
    return block


def gelu_exact(value):
    return jax.nn.gelu(value, approximate=False)


def gelu_back(value, upstream):
    return jax.vjp(gelu_exact, value)[1](upstream)[0]


def layer_norm(value, gain, shift):
    center = value - jnp.mean(value, axis=-1, keepdims=True)
    spread = jnp.mean(center * center, axis=-1, keepdims=True)
    return center * lax.rsqrt(spread + 1e-05) * gain + shift


def sine_positions(turns, heights, widths, row_start, rows, side, width):
    row = row_start + jnp.arange(rows, dtype=jnp.int32)[None, :, None]
    column = jnp.arange(side, dtype=jnp.int32)[None, None, :]
    turn = turns[:, None, None]
    upright_y = jnp.where(
        turn == 0,
        row,
        jnp.where(turn == 1, column, jnp.where(turn == 2, side - 1 - row, side - 1 - column)),
    )
    upright_x = jnp.where(
        turn == 0,
        column,
        jnp.where(turn == 1, side - 1 - row, jnp.where(turn == 2, side - 1 - column, row)),
    )
    valid = (upright_y < heights[:, None, None]) & (upright_x < widths[:, None, None])
    half = width // 2
    index = jnp.arange(half, dtype=jnp.int32)
    period = 10000.0 ** (2.0 * (index // 2).astype(jnp.float32) / half)
    even = index % 2 == 0
    along_y = (
        (upright_y + 1).astype(jnp.float32)
        / (heights[:, None, None].astype(jnp.float32) + 1e-06)
        * (2.0 * math.pi)
    )
    along_x = (
        (upright_x + 1).astype(jnp.float32)
        / (widths[:, None, None].astype(jnp.float32) + 1e-06)
        * (2.0 * math.pi)
    )
    phase_y = along_y[..., None] / period
    phase_x = along_x[..., None] / period
    pos_y = jnp.where(even, jnp.sin(phase_y), jnp.cos(phase_y))
    pos_x = jnp.where(even, jnp.sin(phase_x), jnp.cos(phase_x))
    return (jnp.concatenate([pos_y, pos_x], axis=-1), valid)


def pad_columns(value):
    return jnp.pad(value, ((0, 0), (0, 0), (1, 1), (0, 0)))


def conv_valid(padded, kernel):
    return lax.conv_general_dilated(
        padded,
        kernel,
        (1, 1),
        "VALID",
        dimension_numbers=("NHWC", "HWIO", "NHWC"),
        preferred_element_type=jnp.float32,
    )


def flipped(kernel):
    return jnp.transpose(kernel[::-1, ::-1], (0, 1, 3, 2))


def kernel_grad(padded, upstream):
    rows, side, channels = (upstream.shape[1], upstream.shape[2], upstream.shape[3])
    terms = []
    for down in range(3):
        for across in range(3):
            window = padded[:, down : down + rows, across : across + side, :]
            terms.append(
                jnp.einsum("prci,prco->io", window, upstream, preferred_element_type=jnp.float32)
            )
    return jnp.stack(terms).reshape(3, 3, padded.shape[3], channels)


def left_product(left, right):
    return jnp.einsum("ti,to->io", left, right, preferred_element_type=jnp.float32)


def right_back(upstream, weight):
    return jnp.einsum("to,io->ti", upstream, weight, preferred_element_type=jnp.float32)


def column_sum(value):
    return jnp.sum(value.astype(jnp.float32), axis=0)


def body(
    features,
    quarter_turns,
    heights,
    widths,
    frozen_scale,
    frozen_shift,
    first_kernel,
    second_kernel,
    project_weight,
    project_bias,
    query_weight,
    query_bias,
    key_weight,
    value_weight,
    value_bias,
    output_weight,
    output_bias,
    first_gain,
    first_shift,
    expand_weight,
    expand_bias,
    shrink_weight,
    shrink_bias,
    final_gain,
    final_shift,
    cotangent,
):
    pages, rows, side, channels = features.shape
    width = project_weight.shape[1]
    head_size = width // HEADS
    length = rows * side
    strips = lax.axis_size("strip")
    whole = strips * length
    row_start = lax.axis_index("strip") * rows
    factor = head_size ** (-0.5)
    padded_in = pad_columns(with_halo(features, (("strip", 1),), 1))
    first_pre = conv_valid(padded_in, first_kernel) * frozen_scale[0] + frozen_shift[0]
    hidden = gelu_exact(first_pre).astype(jnp.bfloat16)
    padded_hidden = pad_columns(with_halo(hidden, (("strip", 1),), 1))
    second_pre = (
        conv_valid(padded_hidden, second_kernel) * frozen_scale[1]
        + frozen_shift[1]
        + features.astype(jnp.float32)
    )
    block = gelu_exact(second_pre).astype(jnp.bfloat16).reshape(pages * length, channels)
    source = jnp.dot(block, project_weight, preferred_element_type=jnp.float32) + project_bias
    position, valid = sine_positions(quarter_turns, heights, widths, row_start, rows, side, width)
    joint = (source + position.reshape(pages * length, width)).astype(jnp.bfloat16)
    plain = source.astype(jnp.bfloat16)
    queries = (
        jnp.dot(joint, query_weight, preferred_element_type=jnp.float32) + query_bias
    ).astype(jnp.bfloat16)
    queries = queries.reshape(pages, length, HEADS, head_size)
    keys_local = (
        jnp.dot(joint, key_weight, preferred_element_type=jnp.float32)
        .astype(jnp.bfloat16)
        .reshape(pages, length, width)
    )
    values_local = (
        (jnp.dot(plain, value_weight, preferred_element_type=jnp.float32) + value_bias)
        .astype(jnp.bfloat16)
        .reshape(pages, length, width)
    )
    key_bias = jnp.where(valid, 0.0, -10000.0).astype(jnp.bfloat16).reshape(pages, length)
    keys_piece = lax.all_gather(keys_local, "strip", axis=1, tiled=True)
    values_piece = lax.all_gather(values_local, "strip", axis=1, tiled=True)
    bias_piece = lax.all_gather(key_bias, "strip", axis=1, tiled=True)
    count = keys_piece.shape[1]
    partial_scores = jnp.einsum(
        "pqhd,pkhd->phqk",
        queries,
        keys_piece.reshape(pages, count, HEADS, head_size),
        preferred_element_type=jnp.float32,
    )
    partial_scores = partial_scores * factor + bias_piece.astype(jnp.float32)[:, None, None, :]
    peak = jnp.max(partial_scores, axis=-1)
    expd = jnp.exp(partial_scores - peak[..., None])
    denom = jnp.sum(expd, axis=-1)
    logsum = peak + jnp.log(denom)
    low_prob = (expd / denom[..., None]).astype(jnp.bfloat16)
    mixed = jnp.einsum(
        "phqk,pkhd->pqhd",
        low_prob,
        values_piece.reshape(pages, whole, HEADS, head_size),
        preferred_element_type=jnp.float32,
    )
    combined = mixed.reshape(pages * length, width).astype(jnp.bfloat16)
    attended = jnp.dot(combined, output_weight, preferred_element_type=jnp.float32) + output_bias
    first_sum = source + attended
    normed = layer_norm(first_sum, first_gain, first_shift)
    ff_in = normed.astype(jnp.bfloat16)
    expanded = jnp.dot(ff_in, expand_weight, preferred_element_type=jnp.float32) + expand_bias
    activated = gelu_exact(expanded).astype(jnp.bfloat16)
    second_sum = (
        normed + jnp.dot(activated, shrink_weight, preferred_element_type=jnp.float32) + shrink_bias
    )
    result, final_back = jax.vjp(layer_norm, second_sum, final_gain, final_shift)
    encoded = result.astype(jnp.bfloat16).reshape(pages, rows, side, width)
    d_second, final_gain_grad, final_shift_grad = final_back(
        cotangent.astype(jnp.float32).reshape(pages * length, width)
    )
    d_shrunk = d_second.astype(jnp.bfloat16)
    shrink_bias_grad = column_sum(d_shrunk)
    shrink_weight_grad = left_product(activated, d_shrunk)
    d_expanded = gelu_back(expanded, right_back(d_shrunk, shrink_weight)).astype(jnp.bfloat16)
    expand_bias_grad = column_sum(d_expanded)
    expand_weight_grad = left_product(ff_in, d_expanded)
    d_normed = right_back(d_expanded, expand_weight) + d_second
    d_first, first_gain_grad, first_shift_grad = jax.vjp(
        layer_norm, first_sum, first_gain, first_shift
    )[1](d_normed)
    d_attended = d_first.astype(jnp.bfloat16)
    output_bias_grad = column_sum(d_attended)
    output_weight_grad = left_product(combined, d_attended)
    d_combined = (
        right_back(d_attended, output_weight)
        .astype(jnp.bfloat16)
        .reshape(pages, length, HEADS, head_size)
    )
    delta = jnp.sum(d_combined.astype(jnp.float32) * mixed, axis=-1)
    logsum_rows = jnp.transpose(logsum, (0, 2, 1))
    keys_all, values_again, bias_all = (
        lax.all_gather(keys_local, "strip", axis=1, tiled=True),
        lax.all_gather(values_local, "strip", axis=1, tiled=True),
        lax.all_gather(key_bias, "strip", axis=1, tiled=True),
    )
    keys_four = keys_all.reshape(pages, whole, HEADS, head_size)
    values_four = values_again.reshape(pages, whole, HEADS, head_size)
    part_scores = (
        jnp.einsum("pqhd,pkhd->phqk", queries, keys_four, preferred_element_type=jnp.float32)
        * factor
    )
    part_scores = part_scores + bias_all.astype(jnp.float32)[:, None, None, :]
    prob = jnp.exp(part_scores - jnp.transpose(logsum_rows, (0, 2, 1))[..., None])
    d_prob = jnp.einsum(
        "pqhd,pkhd->phqk", d_combined, values_four, preferred_element_type=jnp.float32
    )
    pair_d_scores = (prob * (d_prob - jnp.transpose(delta, (0, 2, 1))[..., None])).astype(
        jnp.bfloat16
    )
    weights_low = prob.astype(jnp.bfloat16)
    d_queries = factor * jnp.einsum(
        "phqk,pkhd->pqhd", pair_d_scores, keys_four, preferred_element_type=jnp.float32
    )
    key_part = factor * jnp.einsum(
        "phqk,pqhd->kphd", pair_d_scores, queries, preferred_element_type=jnp.float32
    )
    value_part = jnp.einsum(
        "phqk,pqhd->kphd", weights_low, d_combined, preferred_element_type=jnp.float32
    )
    summed = lax.psum_scatter(
        jnp.concatenate(
            [
                key_part.reshape(length * lax.axis_size("strip"), pages, width),
                value_part.reshape(length * lax.axis_size("strip"), pages, width),
            ],
            axis=-1,
        ).astype(jnp.bfloat16),
        "strip",
        scatter_dimension=0,
        tiled=True,
    ).astype(jnp.float32)
    d_keys = jnp.transpose(summed[:, :, :width], (1, 0, 2))
    d_values = jnp.transpose(summed[:, :, width:], (1, 0, 2))
    d_queries_low = d_queries.reshape(pages * length, width).astype(jnp.bfloat16)
    d_keys_low = d_keys.reshape(pages * length, width).astype(jnp.bfloat16)
    d_values_low = d_values.reshape(pages * length, width).astype(jnp.bfloat16)
    query_bias_grad = column_sum(d_queries_low)
    query_weight_grad = left_product(joint, d_queries_low)
    key_weight_grad = left_product(joint, d_keys_low)
    value_weight_grad = left_product(plain, d_values_low)
    value_bias_grad = column_sum(d_values_low)
    d_source = (
        d_first
        + right_back(d_queries_low, query_weight)
        + right_back(d_keys_low, key_weight)
        + right_back(d_values_low, value_weight)
    )
    d_source_low = d_source.astype(jnp.bfloat16)
    project_bias_grad = column_sum(d_source_low)
    project_weight_grad = left_product(block, d_source_low)
    d_block = right_back(d_source_low, project_weight).reshape(pages, rows, side, channels)
    d_second_pre = gelu_back(second_pre, d_block)
    d_late = (d_second_pre * frozen_scale[1]).astype(jnp.bfloat16)
    padded_late = pad_columns(with_halo(d_late, (("strip", 1),), 1))
    d_hidden = conv_valid(padded_late, flipped(second_kernel))
    second_kernel_grad = kernel_grad(padded_hidden, d_late)
    d_early = (gelu_back(first_pre, d_hidden) * frozen_scale[0]).astype(jnp.bfloat16)
    padded_early = pad_columns(with_halo(d_early, (("strip", 1),), 1))
    features_grad = conv_valid(padded_early, flipped(first_kernel)) + d_second_pre
    first_kernel_grad = kernel_grad(padded_in, d_early)
    first_part, second_part = (
        lax.psum_scatter(
            first_kernel_grad.astype(jnp.bfloat16), "page", scatter_dimension=2, tiled=True
        ).astype(jnp.float32),
        lax.psum_scatter(
            second_kernel_grad.astype(jnp.bfloat16), "page", scatter_dimension=2, tiled=True
        ).astype(jnp.float32),
    )
    first_part, second_part = (
        lax.psum_scatter(
            first_part.astype(jnp.bfloat16), "strip", scatter_dimension=3, tiled=True
        ).astype(jnp.float32),
        lax.psum_scatter(
            second_part.astype(jnp.bfloat16), "strip", scatter_dimension=3, tiled=True
        ).astype(jnp.float32),
    )
    dense = lax.psum(
        (
            project_weight_grad,
            project_bias_grad,
            query_weight_grad,
            query_bias_grad,
            key_weight_grad,
            value_weight_grad,
            value_bias_grad,
            output_weight_grad,
            output_bias_grad,
            first_gain_grad,
            first_shift_grad,
            expand_weight_grad,
            expand_bias_grad,
            shrink_weight_grad,
            shrink_bias_grad,
            final_gain_grad,
            final_shift_grad,
        ),
        ("page", "strip"),
    )
    return (encoded, features_grad, first_part, second_part) + tuple(dense)


MESH = pl.DeviceIdType.MESH
CORE, X, Y, Z0, Z1 = range(5)
STEPS = {CORE: 1, Y: 2, Z0: 4, Z1: 8}
PLANE, COLUMN = (X, Y), (Z0, Z1)
X_FIRST, X_LAST = ((CORE,), (X,), (Y,), COLUMN), ((CORE,), (Y,), COLUMN, (X,))
DENSE = (
    (64, X_LAST, 0.22, 0.21),
    (64, X_FIRST, 0.56, 0.07),
    (64, X_FIRST, 0.14, 0.44),
    (64, X_LAST, 0.21, 0.08),
    (64, X_LAST, 0.49, 0.95),
    (32, X_LAST, 0.90, 0.45),
)
GRADS = (
    (((Y,), COLUMN), 0.88),
    (((Z0,), (Y,), (Z1,)), 0.66),
    (((Y,), COLUMN), 0.23),
    (((Y,), (Z0,), (Z1,)), 0.69),
    (((Z0,), (Y,), (Z1,)), 0.56),
    (((Y,), (Z0,), (Z1,)), 0.97),
)
ENDS, MIDDLE = 5, 6
TAPS = 9
LANES = 128
WINDOW = 10.0
DELAY = 2.0
CHORE = 0.15
T_DENSE, T_LATE, T_HALO, T_HIDDEN, T_SECOND, T_THIRD, T_FIRST = 31.0, 43.9, 46.0, 47.1, 53.0, 56.7, 60.7
TICK = 0.55
X_TRAFFIC = ((3.0, 10.5), (11.0, 5.0), (19.0, 10.5), (36.5, 6.5), (44.0, 12.5))
PROJECT, QUERY, VALUE, OUTPUT, FIRST_GAIN, FIRST_SHIFT, SHRINK, FINAL_GAIN, FINAL_SHIFT, EXPAND = range(10)


def own_bits():
    page, strip = lax.axis_index("page"), lax.axis_index("strip")
    bits = {name: (page // step) % 2 for name, step in STEPS.items()}
    bits[X] = strip
    peers = {}
    for names in ((CORE,), (X,), (Y,), (Z0,), (Z1,), COLUMN, PLANE, (CORE, X)):
        there = page
        for name in names:
            if name != X:
                there = there + STEPS[name] - 2 * STEPS[name] * bits[name]
        peers[names] = (there, 1 - strip if X in names else strip)
    return bits, peers


def enter(peers):
    barrier = pltpu.get_barrier_semaphore()
    for peer in peers.values():
        pl.semaphore_signal(barrier, inc=1, device_id=peer, device_id_type=MESH)
    pl.semaphore_wait(barrier, len(peers))


def remote(source, target, sends, recvs, peer):
    return pltpu.make_async_remote_copy(
        source, target, sends, recvs, device_id=peer, device_id_type=MESH
    )


def flat(order):
    return [name for stage in order for name in stage]


def slot_of(names, place):
    slot = 0
    for name in names:
        slot = slot * 2 + place[name]
    return slot


class Reduction:
    def __init__(self, order, group, bits, peers, current, parts, sends, recvs, back, keep):
        self.order, self.bits, self.peers = order, bits, peers
        self.current, self.parts = current, parts
        self.sends, self.recvs = sends, recvs
        self.whole = current if back else None
        self.keep = keep
        self.left = [group * 2 ** len(flat(order[step:])) for step in range(len(order) + 1)]
        self.flights = None

    def toward(self, names):
        for code in range(1, 2 ** len(names)):
            flips = [code >> number & 1 for number in range(len(names))]
            key = tuple(name for name, flip in zip(names, flips) if flip)
            place = {
                name: 1 - self.bits[name] if flip else self.bits[name]
                for name, flip in zip(names, flips)
            }
            yield code - 1, self.peers[key], slot_of(names, place)

    def stage(self, step):
        return self.order[min(step, 2 * len(self.order) - 1 - step)]

    def begin(self, step):
        count = len(self.order)
        level = min(step, 2 * count - 1 - step)
        names = self.stage(step)
        size = self.left[level + 1]
        self.flights = []
        mark = sum(2 ** len(self.stage(before)) - 1 for before in range(step))
        for number, peer, slot in self.toward(names):
            if step < count:
                source = self.current.at[pl.ds(slot * size, size)]
                target = self.parts.at[pl.ds(self.left[0] - self.left[step] + number * size, size)]
            else:
                first = 0
                for depth in range(level + 1):
                    first += slot_of(self.order[depth], self.bits) * self.left[depth + 1]
                source = target = self.whole.at[pl.ds(first, size)]
            flight = remote(
                source, target, self.sends.at[number], self.recvs.at[mark + number], peer
            )
            flight.start()
            self.flights.append(flight)

    def end(self, step):
        count = len(self.order)
        for flight in self.flights:
            flight.wait()
        if step >= count:
            return
        size = self.left[step + 1]
        offset = self.left[0] - self.left[step]
        total = self.current[pl.ds(slot_of(self.order[step], self.bits) * size, size)]
        if len(self.flights) == 1:
            total = total + self.parts[pl.ds(offset, size)]
        else:
            total = total.astype(jnp.float32)
            for number in range(len(self.flights)):
                total += self.parts[pl.ds(offset + number * size, size)].astype(jnp.float32)
            total = total.astype(jnp.bfloat16)
        if step == count - 1:
            self.keep(total)
            return
        following = self.parts.at[pl.ds(offset, size)]
        following[...] = total
        self.current = following


class Doubling:
    def __init__(self, order, peers, sums, parts, sends, recvs):
        self.order, self.peers = order, peers
        self.sums, self.parts, self.sends, self.recvs = sums, parts, sends, recvs
        self.flight = None

    def begin(self, step):
        self.flight = remote(
            self.sums.at[step],
            self.parts.at[step],
            self.sends.at[step],
            self.recvs.at[step],
            self.peers[(self.order[step],)],
        )
        self.flight.start()

    def end(self, step):
        self.flight.wait()
        self.sums[step + 1] = self.sums[step] + self.parts[step]


def poll_times():
    half = [1.3] + [0.42] * HEADS + [1.3]
    times = [T_DENSE]
    for spent in [0.5] + half + [0.4] + half:
        times.append(times[-1] + spent)
    for start, count in ((T_HALO, 1), (T_HIDDEN, 7), (T_SECOND, 7), (T_THIRD, 7), (T_FIRST, 7)):
        times += [start + TICK * number for number in range(count)]
    return sorted(times + [T_LATE])


def link_plan(units):
    polls = poll_times()

    def poll(time):
        return min([at for at in polls if at >= time], default=time)

    events = [(poll(ready), 1, unit, 0) for unit, (ready, _, _) in enumerate(units)]
    events += [(time, 0, -1, spent) for time, spent in X_TRAFFIC]
    queue, busy, actions, free = [], {}, [], 0.0
    while events:
        events.sort()
        now, kind, unit, step = events.pop(0)
        if unit < 0:
            busy[X] = max(now, busy.get(X, 0.0)) + step
            continue
        if now >= polls[-1]:
            now = max(now, free)
            free = now + CHORE
        if kind == 0:
            actions.append((now, False, unit, step))
            step += 1
        if step < len(units[unit][1]):
            queue.append((units[unit][2][step], unit, step))
        queue.sort()
        held, waiting = set(), []
        for rank, unit, step in queue:
            cost = units[unit][1][step]
            if any(
                link in held or busy.get(link, 0.0) - now >= (0.01 if link == X else WINDOW)
                for link in cost
            ):
                held.update(cost)
                waiting.append((rank, unit, step))
                continue
            for link, spent in cost.items():
                busy[link] = max(now, busy.get(link, 0.0)) + spent
            actions.append((now, True, unit, step))
            events.append((poll(max(busy[link] for link in cost) + DELAY), 0, unit, step))
        queue = waiting
    return actions


def link_costs(order, size, back):
    costs = []
    for names in order:
        size = size / 2 ** len(names)
        per_flow = size / 9e4
        if names == (CORE,):
            costs.append({CORE: size / 6e5})
        elif names == PLANE:
            costs.append({X: 4 * per_flow, Y: 4 * per_flow})
        elif names == COLUMN:
            costs.append({MIDDLE: 8 * per_flow, ENDS: 6 * per_flow})
        elif names == (Z0,):
            costs.append({ENDS: 2 * per_flow})
        elif names == (Z1,):
            costs.append({MIDDLE: 4 * per_flow, ENDS: 2 * per_flow})
        else:
            costs.append({names[0]: 2 * per_flow})
    return costs + costs[::-1] if back else costs


def shifted(value):
    side = value.shape[0]
    wide = value.astype(jnp.float32)
    column = lax.broadcasted_iota(jnp.int32, wide.shape, 0)
    later = jnp.where(column < side - 1, pltpu.roll(wide, side - 1, 0), 0.0)
    earlier = jnp.where(column > 0, pltpu.roll(wide, 1, 0), 0.0)
    return later.astype(jnp.bfloat16), earlier.astype(jnp.bfloat16)


def gelu_both(value):
    bell = 0.5 * (1.0 + lax.erf(value * math.sqrt(0.5)))
    density = jnp.exp(-0.5 * value * value) * (1.0 / math.sqrt(2.0 * math.pi))
    return value * bell, bell + value * density


def dot(left, right):
    return jnp.dot(left, right, preferred_element_type=jnp.float32)


def dot_nt(left, right):
    return lax.dot_general(
        left, right, (((1,), (1,)), ((), ())), preferred_element_type=jnp.float32
    )


def low(value):
    return value.astype(jnp.bfloat16)


def row_sum(value):
    return jnp.sum(value.astype(jnp.float32), axis=0, keepdims=True)


def norm_parts(value):
    center = value - jnp.mean(value, axis=-1, keepdims=True)
    spread = jnp.mean(center * center, axis=-1, keepdims=True)
    root = lax.rsqrt(spread + 1e-05)
    return center * root, root


def norm_back(normal, root, gain, upstream):
    weighted = upstream * gain
    return root * (
        weighted
        - jnp.mean(weighted, axis=-1, keepdims=True)
        - normal * jnp.mean(weighted * normal, axis=-1, keepdims=True)
    )


def page_kernel(side, names, *refs):
    r = SimpleNamespace(**dict(zip(names, refs)))
    width = r.w_project.shape[1]
    feat_ext = r.feat_ext
    edge = 2 * side
    length = feat_ext.shape[0] - 2 * edge
    feat = feat_ext.at[pl.ds(edge, length)]
    f32, bf16 = jnp.float32, jnp.bfloat16
    r.loads = (
        (r.features, feat),
        (r.first_kernel, r.w_first),
        (r.frozen_scale, r.v_scale),
        (r.frozen_shift, r.v_shift),
        (r.second_kernel, r.w_second),
        (r.project_weight, r.w_project),
        (r.project_bias, r.v_project),
        (r.query_weight, r.w_query),
        (r.key_weight, r.w_key),
        (r.value_weight, r.w_value),
        (r.query_bias, r.v_query),
        (r.value_bias, r.v_value),
        (r.output_weight, r.w_output),
        (r.expand_weight, r.w_expand),
        (r.shrink_weight, r.w_shrink),
        (r.cotangent, r.cot),
        (r.output_bias, r.v_output),
        (r.first_gain, r.v_first_gain),
        (r.first_shift, r.v_first_shift),
        (r.expand_bias, r.v_expand),
        (r.shrink_bias, r.v_shrink),
        (r.final_gain, r.v_final_gain),
        (r.final_shift, r.v_final_shift),
    )
    channels = feat_ext.shape[1]
    hidden_units = r.w_expand.shape[1]
    head_size = width // HEADS
    rows = length // side
    factor = head_size ** (-0.5)
    bits, peers = own_bits()
    strip, core = bits[X], bits[CORE]
    clock = [0.0]

    loads = {}
    for number, (source, target) in enumerate(r.loads):
        pieces = source.shape[0] if len(source.shape) == 3 else 1
        semaphore = r.load_sems.at[number]
        for piece in range(pieces):
            at = pl.ds(piece, 1) if pieces > 1 else pl.ds(0, source.shape[0])
            pltpu.make_async_copy(source.at[at], target.at[at], semaphore).start()
        loads[number] = pltpu.make_async_copy(source, target, semaphore)
    enter(peers)

    exchanged = [0]

    def exchange(source, target, peer):
        number = exchanged[0]
        exchanged[0] += 1
        copy = remote(source, target, r.pair_sends.at[number], r.pair_recvs.at[number], peer)
        copy.start()
        return copy

    def aligned(start, size, unit=side):
        return pl.ds(pl.multiple_of(start, unit), size)

    own_edge = (1 - strip) * (length - edge)
    feat_halo = exchange(
        r.features.at[aligned(own_edge, edge)],
        r.feat_ext.at[aligned(strip * (length + edge), edge)],
        peers[(X,)],
    )

    turn, height, breadth = r.quarter_turns[0], r.heights[0], r.widths[0]
    odd = turn % 2
    lane = lax.broadcasted_iota(jnp.int32, (side, LANES), 1)
    count = lax.broadcasted_iota(jnp.int32, (side, LANES), 0)
    inverse = jnp.exp((lane // 2).astype(f32) * (-2.0 * math.log(10000.0) / LANES))
    row_place = strip * rows + count
    row_place = jnp.where(row_place >= side, row_place - side, row_place)
    row_flip = ((turn == 1) | (turn == 2)).astype(jnp.int32)
    column_flip = (turn // 2) % 2
    for place, flip, extent, first, table, bias in (
        (
            row_place,
            row_flip,
            height + odd * (breadth - height),
            1 - odd,
            r.table_row,
            r.bias_row,
        ),
        (
            count,
            column_flip,
            breadth + odd * (height - breadth),
            odd,
            r.table_col,
            r.bias_col,
        ),
    ):
        place = place + flip * (side - 1 - 2 * place)
        along = (place + 1).astype(f32) / (jnp.full((side, LANES), extent).astype(f32) + 1e-06)
        phase = along * (2.0 * math.pi) * inverse
        sines = jnp.where(lane % 2 == 0, jnp.sin(phase), jnp.cos(phase))
        share = jnp.full((side, LANES), first).astype(f32)
        table[:, pl.ds(0, LANES)] = sines * share
        table[:, pl.ds(LANES, LANES)] = sines * (1.0 - share)
        bias[...] = jnp.where(place < extent, 0.0, -10000.0)

    pool, dense, owned = r.pool, r.dense, r.owned
    dense_units = len(DENSE)
    reducers, costs = [], []
    unit_slots = 24
    begin, marks = 0, 0
    for unit, (slots, order, rank, back_rank) in enumerate(DENSE):
        group = slots // 32

        def keep_dense(value, begin=begin, group=group, order=order):
            dense[pl.ds(begin + slot_of(flat(order), bits) * group, group)] = value

        reducers.append(
            Reduction(
                order,
                group,
                bits,
                peers,
                dense.at[pl.ds(begin, slots)],
                r.dense_parts.at[pl.ds(begin, slots)],
                r.dense_sends.at[pl.ds(3 * unit, 3)],
                r.dense_recvs.at[pl.ds(12 * unit, 12)],
                True,
                keep_dense,
            )
        )
        ready = T_DENSE if unit < 4 else T_LATE if unit == 4 else T_HALO
        ranks = [rank] * len(order) + [back_rank] * len(order)
        costs.append((ready, link_costs(order, slots * 8192, True), ranks))
        begin += slots
    for unit, (order, rank) in enumerate(GRADS):

        def keep_grad(value, unit=unit):
            half = value.shape[1] // 2
            for across in range(3):
                tap = unit % 3 * 3 + across
                owned[unit // 3, 0, tap] = value[across, :half]
                owned[unit // 3, 1, tap] = value[across, half:]

        reducers.append(
            Reduction(
                order,
                3,
                bits,
                peers,
                pool.at[pl.ds(unit * unit_slots, unit_slots)],
                r.parts.at[unit],
                r.grad_sends.at[pl.ds(3 * unit, 3)],
                r.grad_recvs.at[pl.ds(4 * unit, 4)],
                False,
                keep_grad,
            )
        )
        made = (T_SECOND if unit < 3 else T_FIRST) + 2 * TICK * (unit % 3 + 1) - 0.01
        costs.append((made, link_costs(order, 393216, False), [rank] * len(order)))
    small_order = (CORE, X, Y, Z0, Z1)
    small = r.small_sums
    reducers.append(
        Doubling(
            small_order, peers, small, r.small_parts, r.small_sends, r.small_recvs
        )
    )
    small_costs = [{CORE: 0.2}, {X: 0.5}, {Y: 0.5}, {ENDS: 0.5}, {MIDDLE: 1.0, ENDS: 0.5}]
    costs.append((T_HALO, small_costs, [0.0] * 5))
    agenda = link_plan(costs)

    def work(spent):
        clock[0] += spent
        while agenda and agenda[0][0] <= clock[0]:
            _, begins, unit, step = agenda.pop(0)
            if begins:
                reducers[unit].begin(step)
            else:
                reducers[unit].end(step)

    stores = []

    def store(source, target):
        stores.append(pltpu.make_async_copy(source, target, r.out_sems.at[len(stores)]))
        stores[-1].start()

    def settle(at):
        clock[0] = at
        work(0.0)

    def spread(source, target, first, count):
        def one(row, carry):
            at = aligned(row * side, side)
            value = source[at]
            later, earlier = shifted(value)
            target[0, at] = later
            target[1, at] = value
            target[2, at] = earlier
            return carry

        lax.fori_loop(first, first + count, one, 0)

    def conv(x3, weight, start, count, transposed):
        total = None
        for tap in range(TAPS):
            down, across = tap // 3, tap % 3
            if transposed:
                window = pl.ds(start + side * (2 - down), count)
                term = dot_nt(x3[across, window], weight[tap])
            else:
                window = pl.ds(start + side * down, count)
                term = dot(x3[2 - across, window], weight[tap])
            total = term if total is None else total + term
            if transposed and across == 2:
                work(TICK)
        return total

    x3 = r.x3
    scale, shift = r.v_scale, r.v_shift

    def vector(ref, piece=0):
        return ref[pl.ds(piece * width, width)].reshape(1, width)


    loads[0].wait()
    feat_ext[aligned(strip * (length + edge), edge)] = jnp.zeros((edge, channels), bf16)
    spread(feat_ext, x3, 2, rows)
    own_lanes = aligned(strip * length, length, length)
    other_lanes = aligned((1 - strip) * length, length, length)

    def share(every, lanes, source_page, target_page, peer):
        return exchange(every.at[source_page, :, lanes], every.at[target_page, :, lanes], peer)

    r.features_all[0, :, own_lanes] = feat[...].T
    feat_copies = [
        share(r.features_all, own_lanes, 0, 0, peers[(X,)]),
        share(r.features_all, own_lanes, 0, 1, peers[(CORE,)]),
    ]
    for number in (1, 2, 3):
        loads[number].wait()
    feat_halo.wait()
    spread(feat_ext, x3, 0, 2)
    spread(feat_ext, x3, rows + 2, 2)
    hidden = r.hidden
    half_rows = (length + edge) // 2
    for part in range(2):
        at = pl.ds(part * half_rows, half_rows)
        pre = conv(x3, r.w_first, part * half_rows, half_rows, False)
        value, slope = gelu_both(pre * scale[0:1] + shift[0:1])
        hidden[at] = low(value)
        r.slope_first[at] = slope * scale[0:1]
    for begin, inside in ((0, strip), (length + side, 1 - strip)):
        at = pl.ds(begin, side)
        keep = jnp.broadcast_to(inside, (side, channels)).astype(f32)
        hidden[at] = low(hidden[at].astype(f32) * keep)
        r.slope_first[at] = r.slope_first[at] * keep
    spread(hidden, x3, 0, rows + 2)
    r.hidden_all[0, :, own_lanes] = hidden[pl.ds(side, length)].T

    for number in (4, 5, 6):
        loads[number].wait()
    block, source, plain = r.block, r.source, r.plain
    half = length // 2
    plain_copies = []
    for part in range(2):
        at = pl.ds(part * half, half)
        pre = conv(x3, r.w_second, part * half, half, False)
        value, slope = gelu_both(pre * scale[1:2] + shift[1:2] + feat[at].astype(f32))
        block[at] = low(value)
        r.direct[at] = slope
        rows_here = dot(block[at], r.w_project[...]) + vector(r.v_project)
        source[at] = rows_here
        plain[at] = low(rows_here)
        plain_copies.append(
            exchange(plain.at[at], plain.at[pl.ds(length + part * half, half)], peers[(X,)])
        )
    for number in range(7, 12):
        loads[number].wait()

    joint, keys, values = r.joint, r.keys, r.values
    keys_t, values_t = r.keys_t, r.values_t
    table_row, table_col = r.table_row, r.table_col
    bias_row, bias_col = r.bias_row, r.bias_col

    def keys_of(which):
        base = which * length
        for row in range(rows):
            at = pl.ds(base + row * side, side)
            index = which * rows + row
            position = table_row[index : index + 1] + table_col[...]
            rows_here = source[pl.ds(row * side, side)] if which == 0 else plain[at].astype(f32)
            joint[at] = low(rows_here + position)
            r.bias[at] = jnp.minimum(bias_row[index : index + 1], bias_col[...])
        at = pl.ds(base, length)
        keys[at] = low(dot(joint[at], r.w_key[...]))
        values[at] = low(dot(plain[at], r.w_value[...]) + vector(r.v_value))
        keys_t[which] = keys[at].T
        values_t[which] = values[at].T

    lane_head = lax.broadcasted_iota(jnp.int32, (1, width), 1) // head_size

    def only(head, value):
        return jnp.where(lane_head == head, value, 0).astype(bf16)

    quarter = length // LANES
    tile = length // 64

    def pool_at(which, head, lane):
        return pl.ds(((which * HEADS + head) * quarter + lane) * tile, tile)

    keys_of(0)
    queries = r.queries
    queries[...] = low(dot(joint[pl.ds(0, length)], r.w_query[...]) + vector(r.v_query))
    stat, mixed_parts = r.stat, r.mixed_parts

    def attend(which):
        def one(head, carry):
            at = pl.ds(which * length, length)
            scores = dot_nt(keys[at], only(head, queries[...])) * factor
            bias = r.bias[at]
            scores = scores + jnp.concatenate([bias] * quarter, axis=1)
            peak = jnp.max(scores, axis=0, keepdims=True)
            powers = jnp.exp(scores - peak)
            stat[head, 2 * which : 2 * which + 1] = peak
            stat[head, 2 * which + 1 : 2 * which + 2] = jnp.sum(powers, axis=0, keepdims=True)
            powers = low(powers)
            for lane in range(quarter):
                pool[pool_at(which, head, lane)] = powers[
                    :, lane * LANES : (lane + 1) * LANES
                ].reshape(tile, 64, LANES)
            channel = aligned(head * head_size, head_size, head_size)
            mixed_parts[which, channel] = dot(values_t[which, channel], powers)
            return carry

        lax.fori_loop(0, HEADS, one, 0)

    attend(0)
    for copy in plain_copies + feat_copies:
        copy.wait()
    hidden_copies = [
        share(r.hidden_all, own_lanes, 0, 0, peers[(X,)]),
        share(r.hidden_all, own_lanes, 0, 1, peers[(CORE,)]),
    ]
    feat_relay = share(r.features_all, other_lanes, 0, 1, peers[(CORE,)])
    keys_of(1)
    attend(1)

    for head in range(HEADS):
        first_peak, first_sum = stat[head, 0:1], stat[head, 1:2]
        second_peak, second_sum = stat[head, 2:3], stat[head, 3:4]
        peak = jnp.maximum(first_peak, second_peak)
        first_scale, second_scale = jnp.exp(first_peak - peak), jnp.exp(second_peak - peak)
        total = first_scale * first_sum + second_scale * second_sum
        stat[head, 4:5] = first_scale / total
        stat[head, 5:6] = second_scale / total

    def shares_t(which):
        return jnp.concatenate(
            [
                jnp.broadcast_to(stat[head, 4 + which : 5 + which], (head_size, length))
                for head in range(HEADS)
            ],
            axis=0,
        )

    mixed = (shares_t(0) * mixed_parts[0] + shares_t(1) * mixed_parts[1]).T
    combined = r.combined
    combined[...] = low(mixed)

    for number in range(12, len(loads)):
        loads[number].wait()
    small[...] = jnp.zeros_like(small)
    activated, d_expanded = r.activated, r.d_expanded
    ff_in, d_shrunk, d_attended, d_first = r.ff_in, r.d_shrunk, r.d_attended, source
    d_combined = r.d_combined
    chunk = 256
    pieces = hidden_units // width

    def tokens(step, carry):
        at = aligned(step * chunk, chunk, chunk)
        first_total = source[at] + dot(combined[at], r.w_output[...]) + vector(r.v_output)
        first_normal, first_root = norm_parts(first_total)
        normed = first_normal * vector(r.v_first_gain) + vector(r.v_first_shift)
        ff = low(normed)
        ff_in[at] = ff
        slopes = []
        shrunk = None
        for piece in range(pieces):
            lane = pl.ds(piece * width, width)
            expanded = dot(ff, r.w_expand[:, lane]) + vector(r.v_expand, piece)
            value, slope = gelu_both(expanded)
            value = low(value)
            activated[at, lane] = value
            slopes.append(slope)
            term = dot(value, r.w_shrink[lane])
            shrunk = term if shrunk is None else shrunk + term
        second_total = normed + shrunk + vector(r.v_shrink)
        second_normal, second_root = norm_parts(second_total)
        r.encoded_here[at] = low(
            second_normal * vector(r.v_final_gain) + vector(r.v_final_shift)
        )
        upstream = r.cot[at].astype(f32)
        small[0, FINAL_GAIN : FINAL_GAIN + 1] += row_sum(upstream * second_normal)
        small[0, FINAL_SHIFT : FINAL_SHIFT + 1] += row_sum(upstream)
        d_second = norm_back(second_normal, second_root, vector(r.v_final_gain), upstream)
        d_low = low(d_second)
        d_shrunk[at] = d_low
        small[0, SHRINK : SHRINK + 1] += row_sum(d_low)
        d_normed = d_second
        for piece in range(pieces):
            lane = pl.ds(piece * width, width)
            d_piece = low(dot_nt(d_low, r.w_shrink[lane]) * slopes[piece])
            d_expanded[at, lane] = d_piece
            small[0, EXPAND + piece : EXPAND + piece + 1] += row_sum(d_piece)
            d_normed = d_normed + dot_nt(d_piece, r.w_expand[:, lane])
        small[0, FIRST_GAIN : FIRST_GAIN + 1] += row_sum(d_normed * first_normal)
        small[0, FIRST_SHIFT : FIRST_SHIFT + 1] += row_sum(d_normed)
        d_total = norm_back(first_normal, first_root, vector(r.v_first_gain), d_normed)
        d_first[at] = d_total
        d_low = low(d_total)
        d_attended[at] = d_low
        small[0, OUTPUT : OUTPUT + 1] += row_sum(d_low)
        d_combined[at] = low(dot_nt(d_low, r.w_output[...]))
        return carry

    lax.fori_loop(0, length // chunk, tokens, 0)

    store(r.encoded_here, r.encoded)

    def put(unit, value):
        dense[pl.ds(unit * 32, 32)] = low(value).reshape(32, 16, width)

    for part in range(hidden_units // 512):
        lane = pl.ds(part * 512, 512)
        put(part, dot(activated[:, lane].T, d_shrunk[...]))
    ff_t = ff_in[...].T
    for part in range(pieces // 2):
        both = dot(ff_t, d_expanded[:, pl.ds(part * 512, 512)])
        put(4 + part, jnp.concatenate([both[:, :width], both[:, width:]], axis=0))
    settle(T_DENSE)

    deltas = r.deltas
    d_scaled = r.d_scaled
    total = None
    for which in range(2):
        scaled = low(d_combined[...].astype(f32) * shares_t(which).T)
        d_scaled[which] = scaled
        term = scaled.T.astype(f32) * mixed_parts[which]
        total = term if total is None else total + term
    for head in range(HEADS):
        delta = jnp.sum(total[head * head_size : (head + 1) * head_size], axis=0, keepdims=True)
        deltas[head, 0:1] = delta * stat[head, 4:5]
        deltas[head, 1:2] = delta * stat[head, 5:6]
    work(0.5)
    d_queries_t = r.d_queries_t
    d_queries_t[...] = jnp.zeros_like(d_queries_t)
    spare_query, spare_scaled = activated, d_expanded
    for head in range(HEADS):
        spare_query[:, pl.ds(head * width, width)] = only(head, queries[...])

    def stacked(which):
        return jnp.concatenate(
            [
                pool[pool_at(which, head, lane)].reshape(length, LANES)
                for head in range(HEADS)
                for lane in range(quarter)
            ],
            axis=1,
        )

    def heads_down(wide):
        return jnp.concatenate(
            [wide[:, pl.ds(head * width, width)] for head in range(HEADS)], axis=0
        )

    def attend_back(which):
        at = pl.ds(which * length, length)
        for head in range(HEADS):
            spare_scaled[:, pl.ds(head * width, width)] = only(head, d_scaled[which])
        d_values = low(dot(stacked(which), heads_down(spare_scaled)))
        work(1.3)
        for head in range(HEADS):
            d_prob = dot_nt(values[at], spare_scaled[:, pl.ds(head * width, width)])
            d_prob = d_prob - deltas[head, which : which + 1]
            pieces_here = []
            for lane in range(quarter):
                powers = pool[pool_at(which, head, lane)].reshape(length, LANES).astype(f32)
                d_tile = low(powers * d_prob[:, lane * LANES : (lane + 1) * LANES])
                pool[pool_at(which, head, lane)] = d_tile.reshape(tile, 64, LANES)
                pieces_here.append(d_tile)
            channel = pl.ds(head * head_size, head_size)
            d_queries_t[channel] += dot(
                keys_t[which, channel], jnp.concatenate(pieces_here, axis=1)
            )
            work(0.42)
        d_keys = low(dot(stacked(which), heads_down(spare_query)) * factor)
        work(1.3)
        d_rows = dot_nt(d_keys, r.w_key[...]) + dot_nt(d_values, r.w_value[...])
        small[0, VALUE : VALUE + 1] += row_sum(d_values)
        return (
            d_rows,
            dot(joint[at].T, d_keys),
            dot(plain[at].T, d_values),
        )

    d_other, key_grad, value_grad = attend_back(1)
    d_combined[...] = low(d_other)
    d_rows_copy = exchange(d_combined, r.d_rows_in, peers[(X,)])
    work(0.4)
    d_own, more_key, more_value = attend_back(0)
    d_queries = low(d_queries_t[...].T * factor)
    small[0, QUERY : QUERY + 1] = row_sum(d_queries)
    joint_t = joint[pl.ds(0, length)].T
    put(
        8,
        jnp.concatenate([dot(joint_t, d_queries), key_grad + more_key], axis=0),
    )
    put(
        9,
        jnp.concatenate([value_grad + more_value, dot(combined[...].T, d_attended[...])], axis=0),
    )
    settle(T_LATE)
    d_source = d_first[...] + dot_nt(d_queries, r.w_query[...]) + d_own
    d_rows_copy.wait()
    d_source = low(d_source + r.d_rows_in[...].astype(f32))
    small[0, PROJECT : PROJECT + 1] = row_sum(d_source)
    direct = r.direct
    late_ext = r.late_ext
    late = late_ext.at[pl.ds(edge, length)]
    direct[...] = dot_nt(d_source, r.w_project[...]) * r.direct[...]
    late[...] = low(direct[...] * scale[1:2])

    blank = jnp.zeros((edge, channels), bf16)
    halo = exchange(
        late_ext.at[aligned(edge + own_edge, edge)],
        late_ext.at[aligned(strip * (length + edge), edge)],
        peers[(X,)],
    )

    def spread_out(source, first, target):
        copies = []
        there = aligned(side + strip * length, length)
        for peer, page, strip_there, core_there in (
            ((X,), 0, 1 - strip, core),
            ((CORE, X), 1, 1 - strip, 1 - core),
            ((CORE,), 1, strip, 1 - core),
        ):
            lane_here = aligned(strip_there * 2 * LANES + core_there * LANES, LANES, LANES)
            copies.append(
                exchange(
                    source.at[pl.ds(first, length), lane_here], target.at[page, there], peers[peer]
                )
            )
        lane_here = aligned(strip * 2 * LANES + core * LANES, LANES, LANES)
        target[0, there] = source[pl.ds(first, length), lane_here]
        for page in range(2):
            target[page, pl.ds(0, side)] = blank[:side, :LANES]
            target[page, pl.ds(side + 2 * length, side)] = blank[:side, :LANES]
        return copies

    late_copies = spread_out(late_ext, edge, r.late_page)
    late_ext[aligned(strip * (length + edge), edge)] = blank
    spread(late_ext, x3, 2, rows)
    put(10, dot(block[...].T, d_source))
    settle(T_HALO)
    for copy in hidden_copies:
        copy.wait()
    hidden_relay = share(r.hidden_all, other_lanes, 0, 1, peers[(CORE,)])
    halo.wait()
    spread(late_ext, x3, 0, 2)
    spread(late_ext, x3, rows + 2, 2)
    early = hidden
    settle(T_HIDDEN)
    for part in range(2):
        at = pl.ds(part * half_rows, half_rows)
        d_hidden = conv(x3, r.w_second, part * half_rows, half_rows, True)
        early[at] = low(d_hidden * r.slope_first[at])
    early_copies = spread_out(early, side, r.early_page)
    page3 = r.page3

    def spread_pages(source):
        def one(row, carry):
            at = aligned(row * side, side)
            for page in range(2):
                value = source[page, at]
                later, earlier = shifted(value)
                page3[page, 0, at] = later
                page3[page, 1, at] = value
                page3[page, 2, at] = earlier
            return carry

        lax.fori_loop(0, 2 * rows + 2, one, 0)

    def kernel_grads(left, first_unit):
        for down in range(3):
            window = pl.ds(side * (2 - down), 2 * length)
            product = None
            for page in range(2):
                right = jnp.concatenate([page3[page, across, window] for across in range(3)], axis=1)
                term = dot(left[page], right)
                product = term if product is None else product + term
                if page == 0:
                    work(TICK)
            product = low(product)
            unit = first_unit + down
            order = reducers[dense_units + unit].order
            size = product.shape[0] // 8
            for chip in range(8):
                place = {Y: chip % 2, Z0: chip // 2 % 2, Z1: chip // 4}
                for across in range(3):
                    pool[unit * unit_slots + slot_of(flat(order), place) * 3 + across] = product[
                        chip * size : (chip + 1) * size, across * LANES : (across + 1) * LANES
                    ]
            work(TICK)

    for copy in late_copies + [hidden_relay, feat_relay]:
        copy.wait()
    spread_pages(r.late_page)
    settle(T_SECOND)
    kernel_grads(r.hidden_all, 0)
    spread(early, x3, 0, rows + 2)
    settle(T_THIRD)
    for part in range(2):
        at = pl.ds(part * half, half)
        direct[at] = conv(x3, r.w_first, part * half, half, True) + direct[at]
    store(direct, r.features_grad)
    for copy in early_copies:
        copy.wait()
    spread_pages(r.early_page)
    settle(T_FIRST)
    kernel_grads(r.features_all, 3)
    settle(1e9)
    store(small.at[5], r.small_out)
    store(dense, r.dense_out)
    finals = []
    for which, here, out in (
        (1, r.first_here, r.first_grad),
        (0, r.second_here, r.second_grad),
    ):
        copy = exchange(owned.at[which, 1 - core], r.owned_sib.at[which], peers[(CORE,)])
        finals.append((copy, which, here, out))
    for copy, which, here, out in finals:
        copy.wait()
        here[:, :, aligned(core * LANES, LANES, LANES)] = owned[which, core]
        here[:, :, aligned((1 - core) * LANES, LANES, LANES)] = r.owned_sib[which]
        store(here, out)
    for copy in stores:
        copy.wait()


def page_call(side, inputs):
    f32, bf16 = jnp.float32, jnp.bfloat16
    length, channels = inputs["features"].shape
    width = inputs["project_weight"].shape[1]
    hidden_units = inputs["expand_weight"].shape[1]
    edge = 2 * side
    dense_shape = ((2 * hidden_units + channels + 4 * width) // 16, 16, width)
    hbm = pl.BlockSpec(memory_space=pl.ANY)
    sems = pltpu.SemaphoreType.DMA
    def place(array):
        return smem if array.dtype == jnp.int32 else hbm

    smem = pl.BlockSpec(memory_space=pltpu.SMEM)
    outs = dict(
        encoded=((length, width), bf16),
        features_grad=((length, channels), f32),
        first_grad=((TAPS, channels // 16, channels // 2), bf16),
        second_grad=((TAPS, channels // 16, channels // 2), bf16),
        dense_out=(dense_shape, bf16),
        small_out=((24, width), f32),
    )
    scratch = dict(
        w_first=((TAPS, channels, channels), bf16),
        w_second=((TAPS, channels, channels), bf16),
        w_project=((channels, width), bf16),
        w_query=((width, width), bf16),
        w_key=((width, width), bf16),
        w_value=((width, width), bf16),
        w_output=((width, width), bf16),
        w_expand=((width, hidden_units), bf16),
        w_shrink=((hidden_units, width), bf16),
        cot=((length, width), bf16),
        v_scale=(inputs["frozen_scale"].shape, f32),
        v_shift=(inputs["frozen_shift"].shape, f32),
        v_project=((width,), f32),
        v_query=((width,), f32),
        v_value=((width,), f32),
        v_output=((width,), f32),
        v_first_gain=((width,), f32),
        v_first_shift=((width,), f32),
        v_expand=((hidden_units,), f32),
        v_shrink=((width,), f32),
        v_final_gain=((width,), f32),
        v_final_shift=((width,), f32),
        encoded_here=((length, width), bf16),
        direct=((length, channels), f32),
        first_here=((TAPS, channels // 16, channels // 2), bf16),
        second_here=((TAPS, channels // 16, channels // 2), bf16),
        table_row=((side, width), f32),
        table_col=((side, width), f32),
        bias_row=((side, LANES), f32),
        bias_col=((side, LANES), f32),
        feat_ext=((length + 2 * edge, channels), bf16),
        x3=((3, length + 2 * edge, channels), bf16),
        hidden=((length + edge, channels), bf16),
        slope_first=((length + edge, channels), f32),
        features_all=((2, channels, 2 * length), bf16),
        hidden_all=((2, channels, 2 * length), bf16),
        block=((length, channels), bf16),
        source=((length, width), f32),
        plain=((2 * length, width), bf16),
        joint=((2 * length, width), bf16),
        bias=((2 * length, LANES), f32),
        keys=((2 * length, width), bf16),
        values=((2 * length, width), bf16),
        keys_t=((2, width, length), bf16),
        values_t=((2, width, length), bf16),
        queries=((length, width), bf16),
        stat=((HEADS, 8, length), f32),
        deltas=((HEADS, 8, length), f32),
        mixed_parts=((2, width, length), f32),
        combined=((length, width), bf16),
        activated=((length, hidden_units), bf16),
        d_expanded=((length, hidden_units), bf16),
        ff_in=((length, width), bf16),
        d_shrunk=((length, width), bf16),
        d_attended=((length, width), bf16),
        d_combined=((length, width), bf16),
        d_scaled=((2, length, width), bf16),
        d_queries_t=((width, length), f32),
        d_rows_in=((length, width), bf16),
        late_ext=((length + 2 * edge, channels), bf16),
        late_page=((2, 2 * length + edge, LANES), bf16),
        early_page=((2, 2 * length + edge, LANES), bf16),
        page3=((2, 3, 2 * length + edge, LANES), bf16),
        pool=((2 * HEADS * (length // LANES) * (length // 64), 64, LANES), bf16),
        parts=((6, 21, 64, LANES), bf16),
        dense=(dense_shape, bf16),
        dense_parts=(dense_shape, bf16),
        small_sums=((6, 24, width), f32),
        small_parts=((5, 24, width), f32),
        owned=((2, 2, TAPS, channels // 16, LANES), bf16),
        owned_sib=((2, TAPS, channels // 16, LANES), bf16),
    )
    sem_shapes = dict(
        load_sems=(23,),
        out_sems=(6,),
        pair_sends=(20,),
        pair_recvs=(20,),
        grad_sends=(3 * len(GRADS),),
        grad_recvs=(4 * len(GRADS),),
        dense_sends=(3 * len(DENSE),),
        dense_recvs=(12 * len(DENSE),),
        small_sends=(5,),
        small_recvs=(5,),
    )
    names = list(inputs) + list(outs) + list(scratch) + list(sem_shapes)
    results = pl.pallas_call(
        functools.partial(page_kernel, side, names),
        out_shape=tuple(jax.ShapeDtypeStruct(*spec) for spec in outs.values()),
        in_specs=[place(array) for array in inputs.values()],
        out_specs=tuple([hbm] * len(outs)),
        scratch_shapes=[pltpu.VMEM(*spec) for spec in scratch.values()]
        + [sems(shape) for shape in sem_shapes.values()],
        compiler_params=pltpu.CompilerParams(
            collective_id=0, has_side_effects=True, vmem_limit_bytes=63 * 1024 * 1024
        ),
        name="page_step",
    )(*inputs.values())
    return SimpleNamespace(**dict(zip(outs, results)))


def unpack_kernel(passed, dense_hbm, small_hbm, *refs):
    f32 = jnp.float32
    through, refs = refs[:passed], refs[passed:]
    through_out, refs = refs[:passed], refs[passed:]
    held, refs = refs[len(refs) - passed :], refs[: len(refs) - passed]
    outs, (dense, wide, small, vector, vector_wide, wide_grads, in_sems, out_sems) = (
        refs[:-8],
        refs[-8:],
    )
    project, project_b, query, query_b, key, value, value_b, output, output_b = outs[:9]
    first_gain, first_shift, expand, expand_b, shrink, shrink_b, final_gain, final_shift = outs[9:]
    width = dense.shape[2]
    copies = []

    def send(source, target):
        copies.append(pltpu.make_async_copy(source, target, out_sems.at[len(copies)]))
        copies[-1].start()

    units = dense.shape[0] // 32
    loads = [pltpu.make_async_copy(small_hbm, small, in_sems.at[0])]
    for unit in range(units):
        at = pl.ds(32 * unit, 32)
        loads.append(
            pltpu.make_async_copy(dense_hbm.at[at], dense.at[at], in_sems.at[len(loads)])
        )
    for source, target in zip(through, held):
        loads.append(pltpu.make_async_copy(source, target, in_sems.at[len(loads)]))
    for load in loads:
        load.start()
    loads[0].wait()
    for number, (row, out) in enumerate(
        (
            (PROJECT, project_b),
            (QUERY, query_b),
            (VALUE, value_b),
            (OUTPUT, output_b),
            (FIRST_GAIN, first_gain),
            (FIRST_SHIFT, first_shift),
            (SHRINK, shrink_b),
            (FINAL_GAIN, final_gain),
            (FINAL_SHIFT, final_shift),
        )
    ):
        vector[pl.ds(number * width, width)] = small[row]
        send(vector.at[pl.ds(number * width, width)], out)
    for piece in range(expand_b.shape[0] // width):
        vector_wide[pl.ds(piece * width, width)] = small[EXPAND + piece]
    send(vector_wide, expand_b)

    def widen(unit):
        loads[1 + unit].wait()
        wide[unit] = dense[pl.ds(32 * unit, 32)].reshape(512, width).astype(f32)
        return wide.at[unit]

    for part in range(4):
        send(widen(part), shrink.at[pl.ds(part * 512, 512)])
        both = widen(4 + part)
        send(both.at[pl.ds(0, width)], expand.at[:, pl.ds(part * 512, width)])
        send(both.at[pl.ds(width, width)], expand.at[:, pl.ds(part * 512 + width, width)])
    both = widen(8)
    send(both.at[pl.ds(0, width)], query)
    send(both.at[pl.ds(width, width)], key)
    both = widen(9)
    send(both.at[pl.ds(0, width)], value)
    send(both.at[pl.ds(width, width)], output)
    send(widen(10), project)
    for number, (load, source, target) in enumerate(zip(loads[1 + units :], held, through_out)):
        load.wait()
        if source.dtype != target.dtype:
            wide_grads[number % 2] = source[...].astype(f32)
            source = wide_grads.at[number % 2]
        send(source, target)
    for copy in copies:
        copy.wait()


def paired_body(
    features,
    quarter_turns,
    heights,
    widths,
    frozen_scale,
    frozen_shift,
    first_kernel,
    second_kernel,
    project_weight,
    project_bias,
    query_weight,
    query_bias,
    key_weight,
    value_weight,
    value_bias,
    output_weight,
    output_bias,
    first_gain,
    first_shift,
    expand_weight,
    expand_bias,
    shrink_weight,
    shrink_bias,
    final_gain,
    final_shift,
    cotangent,
):
    pages, rows, side, channels = features.shape
    width = project_weight.shape[1]
    hidden_units = expand_weight.shape[1]
    length = rows * side
    got = page_call(
        side,
        dict(
            features=features.reshape(length, channels),
            first_kernel=first_kernel.reshape(TAPS, channels, channels),
            second_kernel=second_kernel.reshape(TAPS, channels, channels),
            project_weight=project_weight,
            query_weight=query_weight,
            key_weight=key_weight,
            value_weight=value_weight,
            output_weight=output_weight,
            expand_weight=expand_weight,
            shrink_weight=shrink_weight,
            cotangent=cotangent.reshape(length, width),
            frozen_scale=frozen_scale,
            frozen_shift=frozen_shift,
            project_bias=project_bias,
            query_bias=query_bias,
            value_bias=value_bias,
            output_bias=output_bias,
            first_gain=first_gain,
            first_shift=first_shift,
            expand_bias=expand_bias,
            shrink_bias=shrink_bias,
            final_gain=final_gain,
            final_shift=final_shift,
            quarter_turns=quarter_turns,
            heights=heights,
            widths=widths,
        ),
    )
    f32 = jnp.float32
    square, vector = (width, width), (width,)
    shapes = [
        (channels, width),
        vector,
        square,
        vector,
        square,
        square,
        vector,
        square,
        vector,
        vector,
        vector,
        (width, hidden_units),
        (hidden_units,),
        (hidden_units, width),
        vector,
        vector,
        vector,
    ]
    hbm = pl.BlockSpec(memory_space=pl.ANY)
    passed = (got.encoded, got.features_grad, got.first_grad, got.second_grad)
    dense = got.dense_out
    results = pl.pallas_call(
        functools.partial(unpack_kernel, len(passed)),
        out_shape=tuple(jax.ShapeDtypeStruct(value.shape, f32 if value.ndim == 3 else value.dtype)
            for value in passed)
        + tuple(jax.ShapeDtypeStruct(shape, f32) for shape in shapes),
        in_specs=[hbm] * (2 + len(passed)),
        out_specs=tuple([hbm] * (len(passed) + len(shapes))),
        scratch_shapes=[
            pltpu.VMEM(dense.shape, jnp.bfloat16),
            pltpu.VMEM((dense.shape[0] // 32, 512, width), f32),
            pltpu.VMEM(got.small_out.shape, f32),
            pltpu.VMEM((9 * width,), f32),
            pltpu.VMEM((hidden_units,), f32),
            pltpu.VMEM((2,) + got.first_grad.shape, f32),
            pltpu.SemaphoreType.DMA((1 + dense.shape[0] // 32 + len(passed),)),
            pltpu.SemaphoreType.DMA((32,)),
        ]
        + [pltpu.VMEM(value.shape, value.dtype) for value in passed],
        compiler_params=pltpu.CompilerParams(vmem_limit_bytes=63 * 1024 * 1024),
        name="unpack",
    )(dense, got.small_out, *passed)
    part_shape = (3, 3, channels // 16, channels // 2)
    return (
        results[0].reshape(pages, rows, side, width),
        results[1].reshape(pages, rows, side, channels),
        results[2].reshape(part_shape),
        results[3].reshape(part_shape),
    ) + tuple(results[len(passed) :])


def solution(mesh):
    paired = mesh.shape["strip"] == 2 and mesh.shape["page"] == 16
    return jax.shard_map(
        paired_body if paired else body,
        mesh=mesh,
        in_specs=(
            P("page", "strip", None, None),
            P("page"),
            P("page"),
            P("page"),
            P(),
            P(),
            P(),
            P(),
            P(),
            P(),
            P(),
            P(),
            P(),
            P(),
            P(),
            P(),
            P(),
            P(),
            P(),
            P(),
            P(),
            P(),
            P(),
            P(),
            P(),
            P("page", "strip", None, None),
        ),
        out_specs=(
            P("page", "strip", None, None),
            P("page", "strip", None, None),
            P(None, None, "page", "strip"),
            P(None, None, "page", "strip"),
            P(),
            P(),
            P(),
            P(),
            P(),
            P(),
            P(),
            P(),
            P(),
            P(),
            P(),
            P(),
            P(),
            P(),
            P(),
            P(),
            P(),
        ),
        check_vma=False,
    )
```

```python
import functools
import math
from types import SimpleNamespace

import jax
import jax.numpy as jnp
from jax import lax
from jax.experimental import pallas as pl
from jax.experimental.pallas import tpu as pltpu
from jax.sharding import PartitionSpec as P

HEADS = 8


def with_halo(block, sides, width):
    for axis, dim in sides:
        count = lax.axis_size(axis)
        forward = [(i, i + 1) for i in range(count - 1)]
        backward = [(target, source) for source, target in forward]
        low = lax.ppermute(
            lax.slice_in_dim(block, block.shape[dim] - width, None, axis=dim), axis, forward
        )
        high = lax.ppermute(lax.slice_in_dim(block, 0, width, axis=dim), axis, backward)
        block = jnp.concatenate([low, block, high], axis=dim)
    return block


def gelu_exact(value):
    return jax.nn.gelu(value, approximate=False)


def gelu_back(value, upstream):
    return jax.vjp(gelu_exact, value)[1](upstream)[0]


def layer_norm(value, gain, shift):
    center = value - jnp.mean(value, axis=-1, keepdims=True)
    spread = jnp.mean(center * center, axis=-1, keepdims=True)
    return center * lax.rsqrt(spread + 1e-05) * gain + shift


def sine_positions(turns, heights, widths, row_start, rows, side, width):
    row = row_start + jnp.arange(rows, dtype=jnp.int32)[None, :, None]
    column = jnp.arange(side, dtype=jnp.int32)[None, None, :]
    turn = turns[:, None, None]
    upright_y = jnp.where(
        turn == 0,
        row,
        jnp.where(turn == 1, column, jnp.where(turn == 2, side - 1 - row, side - 1 - column)),
    )
    upright_x = jnp.where(
        turn == 0,
        column,
        jnp.where(turn == 1, side - 1 - row, jnp.where(turn == 2, side - 1 - column, row)),
    )
    valid = (upright_y < heights[:, None, None]) & (upright_x < widths[:, None, None])
    half = width // 2
    index = jnp.arange(half, dtype=jnp.int32)
    period = 10000.0 ** (2.0 * (index // 2).astype(jnp.float32) / half)
    even = index % 2 == 0
    along_y = (
        (upright_y + 1).astype(jnp.float32)
        / (heights[:, None, None].astype(jnp.float32) + 1e-06)
        * (2.0 * math.pi)
    )
    along_x = (
        (upright_x + 1).astype(jnp.float32)
        / (widths[:, None, None].astype(jnp.float32) + 1e-06)
        * (2.0 * math.pi)
    )
    phase_y = along_y[..., None] / period
    phase_x = along_x[..., None] / period
    pos_y = jnp.where(even, jnp.sin(phase_y), jnp.cos(phase_y))
    pos_x = jnp.where(even, jnp.sin(phase_x), jnp.cos(phase_x))
    return (jnp.concatenate([pos_y, pos_x], axis=-1), valid)


def pad_columns(value):
    return jnp.pad(value, ((0, 0), (0, 0), (1, 1), (0, 0)))


def conv_valid(padded, kernel):
    return lax.conv_general_dilated(
        padded,
        kernel,
        (1, 1),
        "VALID",
        dimension_numbers=("NHWC", "HWIO", "NHWC"),
        preferred_element_type=jnp.float32,
    )


def flipped(kernel):
    return jnp.transpose(kernel[::-1, ::-1], (0, 1, 3, 2))


def kernel_grad(padded, upstream):
    rows, side, channels = (upstream.shape[1], upstream.shape[2], upstream.shape[3])
    terms = []
    for down in range(3):
        for across in range(3):
            window = padded[:, down : down + rows, across : across + side, :]
            terms.append(
                jnp.einsum("prci,prco->io", window, upstream, preferred_element_type=jnp.float32)
            )
    return jnp.stack(terms).reshape(3, 3, padded.shape[3], channels)


def left_product(left, right):
    return jnp.einsum("ti,to->io", left, right, preferred_element_type=jnp.float32)


def right_back(upstream, weight):
    return jnp.einsum("to,io->ti", upstream, weight, preferred_element_type=jnp.float32)


def column_sum(value):
    return jnp.sum(value.astype(jnp.float32), axis=0)


def body(
    features,
    quarter_turns,
    heights,
    widths,
    frozen_scale,
    frozen_shift,
    first_kernel,
    second_kernel,
    project_weight,
    project_bias,
    query_weight,
    query_bias,
    key_weight,
    value_weight,
    value_bias,
    output_weight,
    output_bias,
    first_gain,
    first_shift,
    expand_weight,
    expand_bias,
    shrink_weight,
    shrink_bias,
    final_gain,
    final_shift,
    cotangent,
):
    pages, rows, side, channels = features.shape
    width = project_weight.shape[1]
    head_size = width // HEADS
    length = rows * side
    strips = lax.axis_size("strip")
    whole = strips * length
    row_start = lax.axis_index("strip") * rows
    factor = head_size ** (-0.5)
    padded_in = pad_columns(with_halo(features, (("strip", 1),), 1))
    first_pre = conv_valid(padded_in, first_kernel) * frozen_scale[0] + frozen_shift[0]
    hidden = gelu_exact(first_pre).astype(jnp.bfloat16)
    padded_hidden = pad_columns(with_halo(hidden, (("strip", 1),), 1))
    second_pre = (
        conv_valid(padded_hidden, second_kernel) * frozen_scale[1]
        + frozen_shift[1]
        + features.astype(jnp.float32)
    )
    block = gelu_exact(second_pre).astype(jnp.bfloat16).reshape(pages * length, channels)
    source = jnp.dot(block, project_weight, preferred_element_type=jnp.float32) + project_bias
    position, valid = sine_positions(quarter_turns, heights, widths, row_start, rows, side, width)
    joint = (source + position.reshape(pages * length, width)).astype(jnp.bfloat16)
    plain = source.astype(jnp.bfloat16)
    queries = (
        jnp.dot(joint, query_weight, preferred_element_type=jnp.float32) + query_bias
    ).astype(jnp.bfloat16)
    queries = queries.reshape(pages, length, HEADS, head_size)
    keys_local = (
        jnp.dot(joint, key_weight, preferred_element_type=jnp.float32)
        .astype(jnp.bfloat16)
        .reshape(pages, length, width)
    )
    values_local = (
        (jnp.dot(plain, value_weight, preferred_element_type=jnp.float32) + value_bias)
        .astype(jnp.bfloat16)
        .reshape(pages, length, width)
    )
    key_bias = jnp.where(valid, 0.0, -10000.0).astype(jnp.bfloat16).reshape(pages, length)
    keys_piece = lax.all_gather(keys_local, "strip", axis=1, tiled=True)
    values_piece = lax.all_gather(values_local, "strip", axis=1, tiled=True)
    bias_piece = lax.all_gather(key_bias, "strip", axis=1, tiled=True)
    count = keys_piece.shape[1]
    partial_scores = jnp.einsum(
        "pqhd,pkhd->phqk",
        queries,
        keys_piece.reshape(pages, count, HEADS, head_size),
        preferred_element_type=jnp.float32,
    )
    partial_scores = partial_scores * factor + bias_piece.astype(jnp.float32)[:, None, None, :]
    peak = jnp.max(partial_scores, axis=-1)
    expd = jnp.exp(partial_scores - peak[..., None])
    denom = jnp.sum(expd, axis=-1)
    logsum = peak + jnp.log(denom)
    low_prob = (expd / denom[..., None]).astype(jnp.bfloat16)
    mixed = jnp.einsum(
        "phqk,pkhd->pqhd",
        low_prob,
        values_piece.reshape(pages, whole, HEADS, head_size),
        preferred_element_type=jnp.float32,
    )
    combined = mixed.reshape(pages * length, width).astype(jnp.bfloat16)
    attended = jnp.dot(combined, output_weight, preferred_element_type=jnp.float32) + output_bias
    first_sum = source + attended
    normed = layer_norm(first_sum, first_gain, first_shift)
    ff_in = normed.astype(jnp.bfloat16)
    expanded = jnp.dot(ff_in, expand_weight, preferred_element_type=jnp.float32) + expand_bias
    activated = gelu_exact(expanded).astype(jnp.bfloat16)
    second_sum = (
        normed + jnp.dot(activated, shrink_weight, preferred_element_type=jnp.float32) + shrink_bias
    )
    result, final_back = jax.vjp(layer_norm, second_sum, final_gain, final_shift)
    encoded = result.astype(jnp.bfloat16).reshape(pages, rows, side, width)
    d_second, final_gain_grad, final_shift_grad = final_back(
        cotangent.astype(jnp.float32).reshape(pages * length, width)
    )
    d_shrunk = d_second.astype(jnp.bfloat16)
    shrink_bias_grad = column_sum(d_shrunk)
    shrink_weight_grad = left_product(activated, d_shrunk)
    d_expanded = gelu_back(expanded, right_back(d_shrunk, shrink_weight)).astype(jnp.bfloat16)
    expand_bias_grad = column_sum(d_expanded)
    expand_weight_grad = left_product(ff_in, d_expanded)
    d_normed = right_back(d_expanded, expand_weight) + d_second
    d_first, first_gain_grad, first_shift_grad = jax.vjp(
        layer_norm, first_sum, first_gain, first_shift
    )[1](d_normed)
    d_attended = d_first.astype(jnp.bfloat16)
    output_bias_grad = column_sum(d_attended)
    output_weight_grad = left_product(combined, d_attended)
    d_combined = (
        right_back(d_attended, output_weight)
        .astype(jnp.bfloat16)
        .reshape(pages, length, HEADS, head_size)
    )
    delta = jnp.sum(d_combined.astype(jnp.float32) * mixed, axis=-1)
    logsum_rows = jnp.transpose(logsum, (0, 2, 1))
    keys_all, values_again, bias_all = (
        lax.all_gather(keys_local, "strip", axis=1, tiled=True),
        lax.all_gather(values_local, "strip", axis=1, tiled=True),
        lax.all_gather(key_bias, "strip", axis=1, tiled=True),
    )
    keys_four = keys_all.reshape(pages, whole, HEADS, head_size)
    values_four = values_again.reshape(pages, whole, HEADS, head_size)
    part_scores = (
        jnp.einsum("pqhd,pkhd->phqk", queries, keys_four, preferred_element_type=jnp.float32)
        * factor
    )
    part_scores = part_scores + bias_all.astype(jnp.float32)[:, None, None, :]
    prob = jnp.exp(part_scores - jnp.transpose(logsum_rows, (0, 2, 1))[..., None])
    d_prob = jnp.einsum(
        "pqhd,pkhd->phqk", d_combined, values_four, preferred_element_type=jnp.float32
    )
    pair_d_scores = (prob * (d_prob - jnp.transpose(delta, (0, 2, 1))[..., None])).astype(
        jnp.bfloat16
    )
    weights_low = prob.astype(jnp.bfloat16)
    d_queries = factor * jnp.einsum(
        "phqk,pkhd->pqhd", pair_d_scores, keys_four, preferred_element_type=jnp.float32
    )
    key_part = factor * jnp.einsum(
        "phqk,pqhd->kphd", pair_d_scores, queries, preferred_element_type=jnp.float32
    )
    value_part = jnp.einsum(
        "phqk,pqhd->kphd", weights_low, d_combined, preferred_element_type=jnp.float32
    )
    summed = lax.psum_scatter(
        jnp.concatenate(
            [
                key_part.reshape(length * lax.axis_size("strip"), pages, width),
                value_part.reshape(length * lax.axis_size("strip"), pages, width),
            ],
            axis=-1,
        ).astype(jnp.bfloat16),
        "strip",
        scatter_dimension=0,
        tiled=True,
    ).astype(jnp.float32)
    d_keys = jnp.transpose(summed[:, :, :width], (1, 0, 2))
    d_values = jnp.transpose(summed[:, :, width:], (1, 0, 2))
    d_queries_low = d_queries.reshape(pages * length, width).astype(jnp.bfloat16)
    d_keys_low = d_keys.reshape(pages * length, width).astype(jnp.bfloat16)
    d_values_low = d_values.reshape(pages * length, width).astype(jnp.bfloat16)
    query_bias_grad = column_sum(d_queries_low)
    query_weight_grad = left_product(joint, d_queries_low)
    key_weight_grad = left_product(joint, d_keys_low)
    value_weight_grad = left_product(plain, d_values_low)
    value_bias_grad = column_sum(d_values_low)
    d_source = (
        d_first
        + right_back(d_queries_low, query_weight)
        + right_back(d_keys_low, key_weight)
        + right_back(d_values_low, value_weight)
    )
    d_source_low = d_source.astype(jnp.bfloat16)
    project_bias_grad = column_sum(d_source_low)
    project_weight_grad = left_product(block, d_source_low)
    d_block = right_back(d_source_low, project_weight).reshape(pages, rows, side, channels)
    d_second_pre = gelu_back(second_pre, d_block)
    d_late = (d_second_pre * frozen_scale[1]).astype(jnp.bfloat16)
    padded_late = pad_columns(with_halo(d_late, (("strip", 1),), 1))
    d_hidden = conv_valid(padded_late, flipped(second_kernel))
    second_kernel_grad = kernel_grad(padded_hidden, d_late)
    d_early = (gelu_back(first_pre, d_hidden) * frozen_scale[0]).astype(jnp.bfloat16)
    padded_early = pad_columns(with_halo(d_early, (("strip", 1),), 1))
    features_grad = conv_valid(padded_early, flipped(first_kernel)) + d_second_pre
    first_kernel_grad = kernel_grad(padded_in, d_early)
    first_part, second_part = (
        lax.psum_scatter(
            first_kernel_grad.astype(jnp.bfloat16), "page", scatter_dimension=2, tiled=True
        ).astype(jnp.float32),
        lax.psum_scatter(
            second_kernel_grad.astype(jnp.bfloat16), "page", scatter_dimension=2, tiled=True
        ).astype(jnp.float32),
    )
    first_part, second_part = (
        lax.psum_scatter(
            first_part.astype(jnp.bfloat16), "strip", scatter_dimension=3, tiled=True
        ).astype(jnp.float32),
        lax.psum_scatter(
            second_part.astype(jnp.bfloat16), "strip", scatter_dimension=3, tiled=True
        ).astype(jnp.float32),
    )
    dense = lax.psum(
        (
            project_weight_grad,
            project_bias_grad,
            query_weight_grad,
            query_bias_grad,
            key_weight_grad,
            value_weight_grad,
            value_bias_grad,
            output_weight_grad,
            output_bias_grad,
            first_gain_grad,
            first_shift_grad,
            expand_weight_grad,
            expand_bias_grad,
            shrink_weight_grad,
            shrink_bias_grad,
            final_gain_grad,
            final_shift_grad,
        ),
        ("page", "strip"),
    )
    return (encoded, features_grad, first_part, second_part) + tuple(dense)


MESH = pl.DeviceIdType.MESH
CORE, X, Y, Z0, Z1 = range(5)
STEPS = {CORE: 1, Y: 2, Z0: 4, Z1: 8}
PLANE, COLUMN = (X, Y), (Z0, Z1)
X_FIRST, X_LAST = ((CORE,), (X,), (Y,), COLUMN), ((CORE,), (Y,), COLUMN, (X,))
DENSE = (
    (64, X_LAST, 0.22, 0.21),
    (64, X_FIRST, 0.56, 0.07),
    (64, X_FIRST, 0.14, 0.44),
    (64, X_LAST, 0.21, 0.08),
    (64, X_LAST, 0.49, 0.95),
    (32, X_LAST, 0.90, 0.45),
)
GRADS = (
    (((Y,), COLUMN), 0.88),
    (((Z0,), (Y,), (Z1,)), 0.66),
    (((Y,), COLUMN), 0.23),
    (((Y,), (Z0,), (Z1,)), 0.69),
    (((Z0,), (Y,), (Z1,)), 0.56),
    (((Y,), (Z0,), (Z1,)), 0.97),
)
ENDS, MIDDLE = 5, 6
TAPS = 9
LANES = 128
WINDOW = 10.0
DELAY = 2.0
CHORE = 0.15
T_DENSE, T_LATE, T_HALO, T_HIDDEN, T_SECOND, T_THIRD, T_FIRST = 31.0, 43.9, 46.0, 47.1, 53.0, 56.7, 60.7
TICK = 0.55
X_TRAFFIC = ((3.0, 10.5), (11.0, 5.0), (19.0, 10.5), (36.5, 6.5), (44.0, 12.5))
PROJECT, QUERY, VALUE, OUTPUT, FIRST_GAIN, FIRST_SHIFT, SHRINK, FINAL_GAIN, FINAL_SHIFT, EXPAND = range(10)


def own_bits():
    page, strip = lax.axis_index("page"), lax.axis_index("strip")
    bits = {name: (page // step) % 2 for name, step in STEPS.items()}
    bits[X] = strip
    peers = {}
    for names in ((CORE,), (X,), (Y,), (Z0,), (Z1,), COLUMN, PLANE, (CORE, X)):
        there = page
        for name in names:
            if name != X:
                there = there + STEPS[name] - 2 * STEPS[name] * bits[name]
        peers[names] = (there, 1 - strip if X in names else strip)
    return bits, peers


def enter(peers):
    barrier = pltpu.get_barrier_semaphore()
    for peer in peers.values():
        pl.semaphore_signal(barrier, inc=1, device_id=peer, device_id_type=MESH)
    pl.semaphore_wait(barrier, len(peers))


def remote(source, target, sends, recvs, peer):
    return pltpu.make_async_remote_copy(
        source, target, sends, recvs, device_id=peer, device_id_type=MESH
    )


def flat(order):
    return [name for stage in order for name in stage]


def slot_of(names, place):
    slot = 0
    for name in names:
        slot = slot * 2 + place[name]
    return slot


class Reduction:
    def __init__(self, order, group, bits, peers, current, parts, sends, recvs, back, keep):
        self.order, self.bits, self.peers = order, bits, peers
        self.current, self.parts = current, parts
        self.sends, self.recvs = sends, recvs
        self.whole = current if back else None
        self.keep = keep
        self.left = [group * 2 ** len(flat(order[step:])) for step in range(len(order) + 1)]
        self.flights = None

    def toward(self, names):
        for code in range(1, 2 ** len(names)):
            flips = [code >> number & 1 for number in range(len(names))]
            key = tuple(name for name, flip in zip(names, flips) if flip)
            place = {
                name: 1 - self.bits[name] if flip else self.bits[name]
                for name, flip in zip(names, flips)
            }
            yield code - 1, self.peers[key], slot_of(names, place)

    def stage(self, step):
        return self.order[min(step, 2 * len(self.order) - 1 - step)]

    def begin(self, step):
        count = len(self.order)
        level = min(step, 2 * count - 1 - step)
        names = self.stage(step)
        size = self.left[level + 1]
        self.flights = []
        mark = sum(2 ** len(self.stage(before)) - 1 for before in range(step))
        for number, peer, slot in self.toward(names):
            if step < count:
                source = self.current.at[pl.ds(slot * size, size)]
                target = self.parts.at[pl.ds(self.left[0] - self.left[step] + number * size, size)]
            else:
                first = 0
                for depth in range(level + 1):
                    first += slot_of(self.order[depth], self.bits) * self.left[depth + 1]
                source = target = self.whole.at[pl.ds(first, size)]
            flight = remote(
                source, target, self.sends.at[number], self.recvs.at[mark + number], peer
            )
            flight.start()
            self.flights.append(flight)

    def end(self, step):
        count = len(self.order)
        for flight in self.flights:
            flight.wait()
        if step >= count:
            return
        size = self.left[step + 1]
        offset = self.left[0] - self.left[step]
        total = self.current[pl.ds(slot_of(self.order[step], self.bits) * size, size)]
        if len(self.flights) == 1:
            total = total + self.parts[pl.ds(offset, size)]
        else:
            total = total.astype(jnp.float32)
            for number in range(len(self.flights)):
                total += self.parts[pl.ds(offset + number * size, size)].astype(jnp.float32)
            total = total.astype(jnp.bfloat16)
        if step == count - 1:
            self.keep(total)
            return
        following = self.parts.at[pl.ds(offset, size)]
        following[...] = total
        self.current = following


class Doubling:
    def __init__(self, order, peers, sums, parts, sends, recvs):
        self.order, self.peers = order, peers
        self.sums, self.parts, self.sends, self.recvs = sums, parts, sends, recvs
        self.flight = None

    def begin(self, step):
        self.flight = remote(
            self.sums.at[step],
            self.parts.at[step],
            self.sends.at[step],
            self.recvs.at[step],
            self.peers[(self.order[step],)],
        )
        self.flight.start()

    def end(self, step):
        self.flight.wait()
        self.sums[step + 1] = self.sums[step] + self.parts[step]


def poll_times():
    half = [1.3] + [0.42] * HEADS + [1.3]
    times = [T_DENSE]
    for spent in [0.5] + half + [0.4] + half:
        times.append(times[-1] + spent)
    for start, count in ((T_HALO, 1), (T_HIDDEN, 7), (T_SECOND, 7), (T_THIRD, 7), (T_FIRST, 7)):
        times += [start + TICK * number for number in range(count)]
    return sorted(times + [T_LATE])


def link_plan(units):
    polls = poll_times()

    def poll(time):
        return min([at for at in polls if at >= time], default=time)

    events = [(poll(ready), 1, unit, 0) for unit, (ready, _, _) in enumerate(units)]
    events += [(time, 0, -1, spent) for time, spent in X_TRAFFIC]
    queue, busy, actions, free = [], {}, [], 0.0
    while events:
        events.sort()
        now, kind, unit, step = events.pop(0)
        if unit < 0:
            busy[X] = max(now, busy.get(X, 0.0)) + step
            continue
        if now >= polls[-1]:
            now = max(now, free)
            free = now + CHORE
        if kind == 0:
            actions.append((now, False, unit, step))
            step += 1
        if step < len(units[unit][1]):
            queue.append((units[unit][2][step], unit, step))
        queue.sort()
        held, waiting = set(), []
        for rank, unit, step in queue:
            cost = units[unit][1][step]
            if any(
                link in held or busy.get(link, 0.0) - now >= (0.01 if link == X else WINDOW)
                for link in cost
            ):
                held.update(cost)
                waiting.append((rank, unit, step))
                continue
            for link, spent in cost.items():
                busy[link] = max(now, busy.get(link, 0.0)) + spent
            actions.append((now, True, unit, step))
            events.append((poll(max(busy[link] for link in cost) + DELAY), 0, unit, step))
        queue = waiting
    return actions


def link_costs(order, size, back):
    costs = []
    for names in order:
        size = size / 2 ** len(names)
        per_flow = size / 9e4
        if names == (CORE,):
            costs.append({CORE: size / 6e5})
        elif names == PLANE:
            costs.append({X: 4 * per_flow, Y: 4 * per_flow})
        elif names == COLUMN:
            costs.append({MIDDLE: 8 * per_flow, ENDS: 6 * per_flow})
        elif names == (Z0,):
            costs.append({ENDS: 2 * per_flow})
        elif names == (Z1,):
            costs.append({MIDDLE: 4 * per_flow, ENDS: 2 * per_flow})
        else:
            costs.append({names[0]: 2 * per_flow})
    return costs + costs[::-1] if back else costs


def shifted(value):
    side = value.shape[0]
    wide = value.astype(jnp.float32)
    column = lax.broadcasted_iota(jnp.int32, wide.shape, 0)
    later = jnp.where(column < side - 1, pltpu.roll(wide, side - 1, 0), 0.0)
    earlier = jnp.where(column > 0, pltpu.roll(wide, 1, 0), 0.0)
    return later.astype(jnp.bfloat16), earlier.astype(jnp.bfloat16)


def gelu_both(value):
    bell = 0.5 * (1.0 + lax.erf(value * math.sqrt(0.5)))
    density = jnp.exp(-0.5 * value * value) * (1.0 / math.sqrt(2.0 * math.pi))
    return value * bell, bell + value * density


def dot(left, right):
    return jnp.dot(left, right, preferred_element_type=jnp.float32)


def dot_nt(left, right):
    return lax.dot_general(
        left, right, (((1,), (1,)), ((), ())), preferred_element_type=jnp.float32
    )


def low(value):
    return value.astype(jnp.bfloat16)


def row_sum(value):
    return jnp.sum(value.astype(jnp.float32), axis=0, keepdims=True)


def norm_parts(value):
    center = value - jnp.mean(value, axis=-1, keepdims=True)
    spread = jnp.mean(center * center, axis=-1, keepdims=True)
    root = lax.rsqrt(spread + 1e-05)
    return center * root, root


def norm_back(normal, root, gain, upstream):
    weighted = upstream * gain
    return root * (
        weighted
        - jnp.mean(weighted, axis=-1, keepdims=True)
        - normal * jnp.mean(weighted * normal, axis=-1, keepdims=True)
    )


def page_kernel(side, names, *refs):
    r = SimpleNamespace(**dict(zip(names, refs)))
    width = r.w_project.shape[1]
    feat_ext = r.feat_ext
    edge = 2 * side
    length = feat_ext.shape[0] - 2 * edge
    feat = feat_ext.at[pl.ds(edge, length)]
    f32, bf16 = jnp.float32, jnp.bfloat16
    r.loads = (
        (r.features, feat),
        (r.first_kernel, r.w_first),
        (r.frozen_scale, r.v_scale),
        (r.frozen_shift, r.v_shift),
        (r.second_kernel, r.w_second),
        (r.project_weight, r.w_project),
        (r.project_bias, r.v_project),
        (r.query_weight, r.w_query),
        (r.key_weight, r.w_key),
        (r.value_weight, r.w_value),
        (r.query_bias, r.v_query),
        (r.value_bias, r.v_value),
        (r.output_weight, r.w_output),
        (r.expand_weight, r.w_expand),
        (r.shrink_weight, r.w_shrink),
        (r.cotangent, r.cot),
        (r.output_bias, r.v_output),
        (r.first_gain, r.v_first_gain),
        (r.first_shift, r.v_first_shift),
        (r.expand_bias, r.v_expand),
        (r.shrink_bias, r.v_shrink),
        (r.final_gain, r.v_final_gain),
        (r.final_shift, r.v_final_shift),
    )
    channels = feat_ext.shape[1]
    hidden_units = r.w_expand.shape[1]
    head_size = width // HEADS
    rows = length // side
    factor = head_size ** (-0.5)
    bits, peers = own_bits()
    strip, core = bits[X], bits[CORE]
    clock = [0.0]

    loads = {}
    for number, (source, target) in enumerate(r.loads):
        pieces = source.shape[0] if len(source.shape) == 3 else 1
        semaphore = r.load_sems.at[number]
        for piece in range(pieces):
            at = pl.ds(piece, 1) if pieces > 1 else pl.ds(0, source.shape[0])
            pltpu.make_async_copy(source.at[at], target.at[at], semaphore).start()
        loads[number] = pltpu.make_async_copy(source, target, semaphore)
    enter(peers)

    exchanged = [0]

    def exchange(source, target, peer):
        number = exchanged[0]
        exchanged[0] += 1
        copy = remote(source, target, r.pair_sends.at[number], r.pair_recvs.at[number], peer)
        copy.start()
        return copy

    def aligned(start, size, unit=side):
        return pl.ds(pl.multiple_of(start, unit), size)

    own_edge = (1 - strip) * (length - edge)
    feat_halo = exchange(
        r.features.at[aligned(own_edge, edge)],
        r.feat_ext.at[aligned(strip * (length + edge), edge)],
        peers[(X,)],
    )

    turn, height, breadth = r.quarter_turns[0], r.heights[0], r.widths[0]
    odd = turn % 2
    lane = lax.broadcasted_iota(jnp.int32, (side, LANES), 1)
    count = lax.broadcasted_iota(jnp.int32, (side, LANES), 0)
    inverse = jnp.exp((lane // 2).astype(f32) * (-2.0 * math.log(10000.0) / LANES))
    row_place = strip * rows + count
    row_place = jnp.where(row_place >= side, row_place - side, row_place)
    row_flip = ((turn == 1) | (turn == 2)).astype(jnp.int32)
    column_flip = (turn // 2) % 2
    for place, flip, extent, first, table, bias in (
        (
            row_place,
            row_flip,
            height + odd * (breadth - height),
            1 - odd,
            r.table_row,
            r.bias_row,
        ),
        (
            count,
            column_flip,
            breadth + odd * (height - breadth),
            odd,
            r.table_col,
            r.bias_col,
        ),
    ):
        place = place + flip * (side - 1 - 2 * place)
        along = (place + 1).astype(f32) / (jnp.full((side, LANES), extent).astype(f32) + 1e-06)
        phase = along * (2.0 * math.pi) * inverse
        sines = jnp.where(lane % 2 == 0, jnp.sin(phase), jnp.cos(phase))
        share = jnp.full((side, LANES), first).astype(f32)
        table[:, pl.ds(0, LANES)] = sines * share
        table[:, pl.ds(LANES, LANES)] = sines * (1.0 - share)
        bias[...] = jnp.where(place < extent, 0.0, -10000.0)

    pool, dense, owned = r.pool, r.dense, r.owned
    dense_units = len(DENSE)
    reducers, costs = [], []
    unit_slots = 24
    begin, marks = 0, 0
    for unit, (slots, order, rank, back_rank) in enumerate(DENSE):
        group = slots // 32

        def keep_dense(value, begin=begin, group=group, order=order):
            dense[pl.ds(begin + slot_of(flat(order), bits) * group, group)] = value

        reducers.append(
            Reduction(
                order,
                group,
                bits,
                peers,
                dense.at[pl.ds(begin, slots)],
                r.dense_parts.at[pl.ds(begin, slots)],
                r.dense_sends.at[pl.ds(3 * unit, 3)],
                r.dense_recvs.at[pl.ds(12 * unit, 12)],
                True,
                keep_dense,
            )
        )
        ready = T_DENSE if unit < 4 else T_LATE if unit == 4 else T_HALO
        ranks = [rank] * len(order) + [back_rank] * len(order)
        costs.append((ready, link_costs(order, slots * 8192, True), ranks))
        begin += slots
    for unit, (order, rank) in enumerate(GRADS):

        def keep_grad(value, unit=unit):
            half = value.shape[1] // 2
            for across in range(3):
                tap = unit % 3 * 3 + across
                owned[unit // 3, 0, tap] = value[across, :half]
                owned[unit // 3, 1, tap] = value[across, half:]

        reducers.append(
            Reduction(
                order,
                3,
                bits,
                peers,
                pool.at[pl.ds(unit * unit_slots, unit_slots)],
                r.parts.at[unit],
                r.grad_sends.at[pl.ds(3 * unit, 3)],
                r.grad_recvs.at[pl.ds(4 * unit, 4)],
                False,
                keep_grad,
            )
        )
        made = (T_SECOND if unit < 3 else T_FIRST) + 2 * TICK * (unit % 3 + 1) - 0.01
        costs.append((made, link_costs(order, 393216, False), [rank] * len(order)))
    small_order = (CORE, X, Y, Z0, Z1)
    small = r.small_sums
    reducers.append(
        Doubling(
            small_order, peers, small, r.small_parts, r.small_sends, r.small_recvs
        )
    )
    small_costs = [{CORE: 0.2}, {X: 0.5}, {Y: 0.5}, {ENDS: 0.5}, {MIDDLE: 1.0, ENDS: 0.5}]
    costs.append((T_HALO, small_costs, [0.0] * 5))
    agenda = link_plan(costs)

    def work(spent):
        clock[0] += spent
        while agenda and agenda[0][0] <= clock[0]:
            _, begins, unit, step = agenda.pop(0)
            if begins:
                reducers[unit].begin(step)
            else:
                reducers[unit].end(step)
                if unit < dense_units and step + 1 == len(costs[unit][1]):
                    first = sum(slots for slots, _, _, _ in DENSE[:unit])
                    at = pl.ds(first, DENSE[unit][0])
                    store(dense.at[at], r.dense_out.at[at])

    stores = []

    def store(source, target):
        stores.append(pltpu.make_async_copy(source, target, r.out_sems.at[len(stores)]))
        stores[-1].start()

    def settle(at):
        clock[0] = at
        work(0.0)

    def spread(source, target, first, count):
        def one(row, carry):
            at = aligned(row * side, side)
            value = source[at]
            later, earlier = shifted(value)
            target[0, at] = later
            target[1, at] = value
            target[2, at] = earlier
            return carry

        lax.fori_loop(first, first + count, one, 0)

    def conv(x3, weight, start, count, transposed):
        total = None
        for tap in range(TAPS):
            down, across = tap // 3, tap % 3
            if transposed:
                window = pl.ds(start + side * (2 - down), count)
                term = dot_nt(x3[across, window], weight[tap])
            else:
                window = pl.ds(start + side * down, count)
                term = dot(x3[2 - across, window], weight[tap])
            total = term if total is None else total + term
            if transposed and across == 2:
                work(TICK)
        return total

    x3 = r.x3
    scale, shift = r.v_scale, r.v_shift

    def vector(ref, piece=0):
        return ref[pl.ds(piece * width, width)].reshape(1, width)


    loads[0].wait()
    feat_ext[aligned(strip * (length + edge), edge)] = jnp.zeros((edge, channels), bf16)
    spread(feat_ext, x3, 2, rows)
    own_lanes = aligned(strip * length, length, length)
    other_lanes = aligned((1 - strip) * length, length, length)

    def share(every, lanes, source_page, target_page, peer):
        return exchange(every.at[source_page, :, lanes], every.at[target_page, :, lanes], peer)

    r.features_all[0, :, own_lanes] = feat[...].T
    feat_copies = [
        share(r.features_all, own_lanes, 0, 0, peers[(X,)]),
        share(r.features_all, own_lanes, 0, 1, peers[(CORE,)]),
    ]
    for number in (1, 2, 3):
        loads[number].wait()
    feat_halo.wait()
    spread(feat_ext, x3, 0, 2)
    spread(feat_ext, x3, rows + 2, 2)
    hidden = r.hidden
    half_rows = (length + edge) // 2
    for part in range(2):
        at = pl.ds(part * half_rows, half_rows)
        pre = conv(x3, r.w_first, part * half_rows, half_rows, False)
        value, slope = gelu_both(pre * scale[0:1] + shift[0:1])
        hidden[at] = low(value)
        r.slope_first[at] = slope * scale[0:1]
    for begin, inside in ((0, strip), (length + side, 1 - strip)):
        at = pl.ds(begin, side)
        keep = jnp.broadcast_to(inside, (side, channels)).astype(f32)
        hidden[at] = low(hidden[at].astype(f32) * keep)
        r.slope_first[at] = r.slope_first[at] * keep
    spread(hidden, x3, 0, rows + 2)
    r.hidden_all[0, :, own_lanes] = hidden[pl.ds(side, length)].T

    for number in (4, 5, 6):
        loads[number].wait()
    block, source, plain = r.block, r.source, r.plain
    half = length // 2
    plain_copies = []
    for part in range(2):
        at = pl.ds(part * half, half)
        pre = conv(x3, r.w_second, part * half, half, False)
        value, slope = gelu_both(pre * scale[1:2] + shift[1:2] + feat[at].astype(f32))
        block[at] = low(value)
        r.direct[at] = slope
        rows_here = dot(block[at], r.w_project[...]) + vector(r.v_project)
        source[at] = rows_here
        plain[at] = low(rows_here)
        plain_copies.append(
            exchange(plain.at[at], plain.at[pl.ds(length + part * half, half)], peers[(X,)])
        )
    for number in range(7, 12):
        loads[number].wait()

    joint, keys, values = r.joint, r.keys, r.values
    keys_t, values_t = r.keys_t, r.values_t
    table_row, table_col = r.table_row, r.table_col
    bias_row, bias_col = r.bias_row, r.bias_col

    def keys_of(which):
        base = which * length
        for row in range(rows):
            at = pl.ds(base + row * side, side)
            index = which * rows + row
            position = table_row[index : index + 1] + table_col[...]
            rows_here = source[pl.ds(row * side, side)] if which == 0 else plain[at].astype(f32)
            joint[at] = low(rows_here + position)
            r.bias[at] = jnp.minimum(bias_row[index : index + 1], bias_col[...])
        at = pl.ds(base, length)
        keys[at] = low(dot(joint[at], r.w_key[...]))
        values[at] = low(dot(plain[at], r.w_value[...]) + vector(r.v_value))
        keys_t[which] = keys[at].T
        values_t[which] = values[at].T

    lane_head = lax.broadcasted_iota(jnp.int32, (1, width), 1) // head_size

    def only(head, value):
        return jnp.where(lane_head == head, value, 0).astype(bf16)

    quarter = length // LANES
    tile = length // 64

    def pool_at(which, head, lane):
        return pl.ds(((which * HEADS + head) * quarter + lane) * tile, tile)

    keys_of(0)
    queries = r.queries
    queries[...] = low(dot(joint[pl.ds(0, length)], r.w_query[...]) + vector(r.v_query))
    stat, mixed_parts = r.stat, r.mixed_parts

    def attend(which):
        def one(head, carry):
            at = pl.ds(which * length, length)
            scores = dot_nt(keys[at], only(head, queries[...])) * factor
            bias = r.bias[at]
            scores = scores + jnp.concatenate([bias] * quarter, axis=1)
            peak = jnp.max(scores, axis=0, keepdims=True)
            powers = jnp.exp(scores - peak)
            stat[head, 2 * which : 2 * which + 1] = peak
            stat[head, 2 * which + 1 : 2 * which + 2] = jnp.sum(powers, axis=0, keepdims=True)
            powers = low(powers)
            for lane in range(quarter):
                pool[pool_at(which, head, lane)] = powers[
                    :, lane * LANES : (lane + 1) * LANES
                ].reshape(tile, 64, LANES)
            channel = aligned(head * head_size, head_size, head_size)
            mixed_parts[which, channel] = dot(values_t[which, channel], powers)
            return carry

        lax.fori_loop(0, HEADS, one, 0)

    attend(0)
    for copy in plain_copies + feat_copies:
        copy.wait()
    hidden_copies = [
        share(r.hidden_all, own_lanes, 0, 0, peers[(X,)]),
        share(r.hidden_all, own_lanes, 0, 1, peers[(CORE,)]),
    ]
    feat_relay = share(r.features_all, other_lanes, 0, 1, peers[(CORE,)])
    keys_of(1)
    attend(1)

    for head in range(HEADS):
        first_peak, first_sum = stat[head, 0:1], stat[head, 1:2]
        second_peak, second_sum = stat[head, 2:3], stat[head, 3:4]
        peak = jnp.maximum(first_peak, second_peak)
        first_scale, second_scale = jnp.exp(first_peak - peak), jnp.exp(second_peak - peak)
        total = first_scale * first_sum + second_scale * second_sum
        stat[head, 4:5] = first_scale / total
        stat[head, 5:6] = second_scale / total

    def shares_t(which):
        return jnp.concatenate(
            [
                jnp.broadcast_to(stat[head, 4 + which : 5 + which], (head_size, length))
                for head in range(HEADS)
            ],
            axis=0,
        )

    mixed = (shares_t(0) * mixed_parts[0] + shares_t(1) * mixed_parts[1]).T
    combined = r.combined
    combined[...] = low(mixed)

    for number in range(12, len(loads)):
        loads[number].wait()
    small[...] = jnp.zeros_like(small)
    activated, d_expanded = r.activated, r.d_expanded
    ff_in, d_shrunk, d_attended, d_first = r.ff_in, r.d_shrunk, r.d_attended, source
    d_combined = r.d_combined
    chunk = 256
    pieces = hidden_units // width

    def tokens(step, carry):
        at = aligned(step * chunk, chunk, chunk)
        first_total = source[at] + dot(combined[at], r.w_output[...]) + vector(r.v_output)
        first_normal, first_root = norm_parts(first_total)
        normed = first_normal * vector(r.v_first_gain) + vector(r.v_first_shift)
        ff = low(normed)
        ff_in[at] = ff
        slopes = []
        shrunk = None
        for piece in range(pieces):
            lane = pl.ds(piece * width, width)
            expanded = dot(ff, r.w_expand[:, lane]) + vector(r.v_expand, piece)
            value, slope = gelu_both(expanded)
            value = low(value)
            activated[at, lane] = value
            slopes.append(slope)
            term = dot(value, r.w_shrink[lane])
            shrunk = term if shrunk is None else shrunk + term
        second_total = normed + shrunk + vector(r.v_shrink)
        second_normal, second_root = norm_parts(second_total)
        r.encoded_here[at] = low(
            second_normal * vector(r.v_final_gain) + vector(r.v_final_shift)
        )
        upstream = r.cot[at].astype(f32)
        small[0, FINAL_GAIN : FINAL_GAIN + 1] += row_sum(upstream * second_normal)
        small[0, FINAL_SHIFT : FINAL_SHIFT + 1] += row_sum(upstream)
        d_second = norm_back(second_normal, second_root, vector(r.v_final_gain), upstream)
        d_low = low(d_second)
        d_shrunk[at] = d_low
        small[0, SHRINK : SHRINK + 1] += row_sum(d_low)
        d_normed = d_second
        for piece in range(pieces):
            lane = pl.ds(piece * width, width)
            d_piece = low(dot_nt(d_low, r.w_shrink[lane]) * slopes[piece])
            d_expanded[at, lane] = d_piece
            small[0, EXPAND + piece : EXPAND + piece + 1] += row_sum(d_piece)
            d_normed = d_normed + dot_nt(d_piece, r.w_expand[:, lane])
        small[0, FIRST_GAIN : FIRST_GAIN + 1] += row_sum(d_normed * first_normal)
        small[0, FIRST_SHIFT : FIRST_SHIFT + 1] += row_sum(d_normed)
        d_total = norm_back(first_normal, first_root, vector(r.v_first_gain), d_normed)
        d_first[at] = d_total
        d_low = low(d_total)
        d_attended[at] = d_low
        small[0, OUTPUT : OUTPUT + 1] += row_sum(d_low)
        d_combined[at] = low(dot_nt(d_low, r.w_output[...]))
        return carry

    lax.fori_loop(0, length // chunk, tokens, 0)

    store(r.encoded_here, r.encoded)

    def put(unit, value):
        dense[pl.ds(unit * 32, 32)] = low(value).reshape(32, 16, width)

    for part in range(hidden_units // 512):
        lane = pl.ds(part * 512, 512)
        put(part, dot(activated[:, lane].T, d_shrunk[...]))
    ff_t = ff_in[...].T
    for part in range(pieces // 2):
        both = dot(ff_t, d_expanded[:, pl.ds(part * 512, 512)])
        put(4 + part, jnp.concatenate([both[:, :width], both[:, width:]], axis=0))
    settle(T_DENSE)

    deltas = r.deltas
    d_scaled = r.d_scaled
    total = None
    for which in range(2):
        scaled = low(d_combined[...].astype(f32) * shares_t(which).T)
        d_scaled[which] = scaled
        term = scaled.T.astype(f32) * mixed_parts[which]
        total = term if total is None else total + term
    for head in range(HEADS):
        delta = jnp.sum(total[head * head_size : (head + 1) * head_size], axis=0, keepdims=True)
        deltas[head, 0:1] = delta * stat[head, 4:5]
        deltas[head, 1:2] = delta * stat[head, 5:6]
    work(0.5)
    d_queries_t = r.d_queries_t
    d_queries_t[...] = jnp.zeros_like(d_queries_t)
    spare_query, spare_scaled = activated, d_expanded
    for head in range(HEADS):
        spare_query[:, pl.ds(head * width, width)] = only(head, queries[...])

    def stacked(which):
        return jnp.concatenate(
            [
                pool[pool_at(which, head, lane)].reshape(length, LANES)
                for head in range(HEADS)
                for lane in range(quarter)
            ],
            axis=1,
        )

    def heads_down(wide):
        return jnp.concatenate(
            [wide[:, pl.ds(head * width, width)] for head in range(HEADS)], axis=0
        )

    def attend_back(which):
        at = pl.ds(which * length, length)
        for head in range(HEADS):
            spare_scaled[:, pl.ds(head * width, width)] = only(head, d_scaled[which])
        d_values = low(dot(stacked(which), heads_down(spare_scaled)))
        work(1.3)
        for head in range(HEADS):
            d_prob = dot_nt(values[at], spare_scaled[:, pl.ds(head * width, width)])
            d_prob = d_prob - deltas[head, which : which + 1]
            pieces_here = []
            for lane in range(quarter):
                powers = pool[pool_at(which, head, lane)].reshape(length, LANES).astype(f32)
                d_tile = low(powers * d_prob[:, lane * LANES : (lane + 1) * LANES])
                pool[pool_at(which, head, lane)] = d_tile.reshape(tile, 64, LANES)
                pieces_here.append(d_tile)
            channel = pl.ds(head * head_size, head_size)
            d_queries_t[channel] += dot(
                keys_t[which, channel], jnp.concatenate(pieces_here, axis=1)
            )
            work(0.42)
        d_keys = low(dot(stacked(which), heads_down(spare_query)) * factor)
        work(1.3)
        d_rows = dot_nt(d_keys, r.w_key[...]) + dot_nt(d_values, r.w_value[...])
        small[0, VALUE : VALUE + 1] += row_sum(d_values)
        return (
            d_rows,
            dot(joint[at].T, d_keys),
            dot(plain[at].T, d_values),
        )

    d_other, key_grad, value_grad = attend_back(1)
    d_combined[...] = low(d_other)
    d_rows_copy = exchange(d_combined, r.d_rows_in, peers[(X,)])
    work(0.4)
    d_own, more_key, more_value = attend_back(0)
    d_queries = low(d_queries_t[...].T * factor)
    small[0, QUERY : QUERY + 1] = row_sum(d_queries)
    joint_t = joint[pl.ds(0, length)].T
    put(
        8,
        jnp.concatenate([dot(joint_t, d_queries), key_grad + more_key], axis=0),
    )
    put(
        9,
        jnp.concatenate([value_grad + more_value, dot(combined[...].T, d_attended[...])], axis=0),
    )
    settle(T_LATE)
    d_source = d_first[...] + dot_nt(d_queries, r.w_query[...]) + d_own
    d_rows_copy.wait()
    d_source = low(d_source + r.d_rows_in[...].astype(f32))
    small[0, PROJECT : PROJECT + 1] = row_sum(d_source)
    direct = r.direct
    late_ext = r.late_ext
    late = late_ext.at[pl.ds(edge, length)]
    direct[...] = dot_nt(d_source, r.w_project[...]) * r.direct[...]
    late[...] = low(direct[...] * scale[1:2])

    blank = jnp.zeros((edge, channels), bf16)
    halo = exchange(
        late_ext.at[aligned(edge + own_edge, edge)],
        late_ext.at[aligned(strip * (length + edge), edge)],
        peers[(X,)],
    )

    def spread_out(source, first, target):
        copies = []
        there = aligned(side + strip * length, length)
        for peer, page, strip_there, core_there in (
            ((X,), 0, 1 - strip, core),
            ((CORE, X), 1, 1 - strip, 1 - core),
            ((CORE,), 1, strip, 1 - core),
        ):
            lane_here = aligned(strip_there * 2 * LANES + core_there * LANES, LANES, LANES)
            copies.append(
                exchange(
                    source.at[pl.ds(first, length), lane_here], target.at[page, there], peers[peer]
                )
            )
        lane_here = aligned(strip * 2 * LANES + core * LANES, LANES, LANES)
        target[0, there] = source[pl.ds(first, length), lane_here]
        for page in range(2):
            target[page, pl.ds(0, side)] = blank[:side, :LANES]
            target[page, pl.ds(side + 2 * length, side)] = blank[:side, :LANES]
        return copies

    late_copies = spread_out(late_ext, edge, r.late_page)
    late_ext[aligned(strip * (length + edge), edge)] = blank
    spread(late_ext, x3, 2, rows)
    put(10, dot(block[...].T, d_source))
    settle(T_HALO)
    for copy in hidden_copies:
        copy.wait()
    hidden_relay = share(r.hidden_all, other_lanes, 0, 1, peers[(CORE,)])
    halo.wait()
    spread(late_ext, x3, 0, 2)
    spread(late_ext, x3, rows + 2, 2)
    early = hidden
    settle(T_HIDDEN)
    for part in range(2):
        at = pl.ds(part * half_rows, half_rows)
        d_hidden = conv(x3, r.w_second, part * half_rows, half_rows, True)
        early[at] = low(d_hidden * r.slope_first[at])
    early_copies = spread_out(early, side, r.early_page)
    page3 = r.page3

    def spread_pages(source):
        def one(row, carry):
            at = aligned(row * side, side)
            for page in range(2):
                value = source[page, at]
                later, earlier = shifted(value)
                page3[page, 0, at] = later
                page3[page, 1, at] = value
                page3[page, 2, at] = earlier
            return carry

        lax.fori_loop(0, 2 * rows + 2, one, 0)

    def kernel_grads(left, first_unit):
        for down in range(3):
            window = pl.ds(side * (2 - down), 2 * length)
            product = None
            for page in range(2):
                right = jnp.concatenate([page3[page, across, window] for across in range(3)], axis=1)
                term = dot(left[page], right)
                product = term if product is None else product + term
                if page == 0:
                    work(TICK)
            product = low(product)
            unit = first_unit + down
            order = reducers[dense_units + unit].order
            size = product.shape[0] // 8
            for chip in range(8):
                place = {Y: chip % 2, Z0: chip // 2 % 2, Z1: chip // 4}
                for across in range(3):
                    pool[unit * unit_slots + slot_of(flat(order), place) * 3 + across] = product[
                        chip * size : (chip + 1) * size, across * LANES : (across + 1) * LANES
                    ]
            work(TICK)

    for copy in late_copies + [hidden_relay, feat_relay]:
        copy.wait()
    spread_pages(r.late_page)
    settle(T_SECOND)
    kernel_grads(r.hidden_all, 0)
    spread(early, x3, 0, rows + 2)
    settle(T_THIRD)
    for part in range(2):
        at = pl.ds(part * half, half)
        direct[at] = conv(x3, r.w_first, part * half, half, True) + direct[at]
    store(direct, r.features_grad)
    for copy in early_copies:
        copy.wait()
    spread_pages(r.early_page)
    settle(T_FIRST)
    kernel_grads(r.features_all, 3)
    settle(1e9)
    store(small.at[5], r.small_out)
    finals = []
    for which, here, out in (
        (1, r.first_here, r.first_grad),
        (0, r.second_here, r.second_grad),
    ):
        copy = exchange(owned.at[which, 1 - core], r.owned_sib.at[which], peers[(CORE,)])
        finals.append((copy, which, here, out))
    for copy, which, here, out in finals:
        copy.wait()
        here[:, :, aligned(core * LANES, LANES, LANES)] = owned[which, core]
        here[:, :, aligned((1 - core) * LANES, LANES, LANES)] = r.owned_sib[which]
        store(here, out)
    for copy in stores:
        copy.wait()


def page_call(side, inputs):
    f32, bf16 = jnp.float32, jnp.bfloat16
    length, channels = inputs["features"].shape
    width = inputs["project_weight"].shape[1]
    hidden_units = inputs["expand_weight"].shape[1]
    edge = 2 * side
    dense_shape = ((2 * hidden_units + channels + 4 * width) // 16, 16, width)
    hbm = pl.BlockSpec(memory_space=pl.ANY)
    sems = pltpu.SemaphoreType.DMA
    def place(array):
        return smem if array.dtype == jnp.int32 else hbm

    smem = pl.BlockSpec(memory_space=pltpu.SMEM)
    outs = dict(
        encoded=((length, width), bf16),
        features_grad=((length, channels), f32),
        first_grad=((TAPS, channels // 16, channels // 2), bf16),
        second_grad=((TAPS, channels // 16, channels // 2), bf16),
        dense_out=(dense_shape, bf16),
        small_out=((24, width), f32),
    )
    scratch = dict(
        w_first=((TAPS, channels, channels), bf16),
        w_second=((TAPS, channels, channels), bf16),
        w_project=((channels, width), bf16),
        w_query=((width, width), bf16),
        w_key=((width, width), bf16),
        w_value=((width, width), bf16),
        w_output=((width, width), bf16),
        w_expand=((width, hidden_units), bf16),
        w_shrink=((hidden_units, width), bf16),
        cot=((length, width), bf16),
        v_scale=(inputs["frozen_scale"].shape, f32),
        v_shift=(inputs["frozen_shift"].shape, f32),
        v_project=((width,), f32),
        v_query=((width,), f32),
        v_value=((width,), f32),
        v_output=((width,), f32),
        v_first_gain=((width,), f32),
        v_first_shift=((width,), f32),
        v_expand=((hidden_units,), f32),
        v_shrink=((width,), f32),
        v_final_gain=((width,), f32),
        v_final_shift=((width,), f32),
        encoded_here=((length, width), bf16),
        direct=((length, channels), f32),
        first_here=((TAPS, channels // 16, channels // 2), bf16),
        second_here=((TAPS, channels // 16, channels // 2), bf16),
        table_row=((side, width), f32),
        table_col=((side, width), f32),
        bias_row=((side, LANES), f32),
        bias_col=((side, LANES), f32),
        feat_ext=((length + 2 * edge, channels), bf16),
        x3=((3, length + 2 * edge, channels), bf16),
        hidden=((length + edge, channels), bf16),
        slope_first=((length + edge, channels), f32),
        features_all=((2, channels, 2 * length), bf16),
        hidden_all=((2, channels, 2 * length), bf16),
        block=((length, channels), bf16),
        source=((length, width), f32),
        plain=((2 * length, width), bf16),
        joint=((2 * length, width), bf16),
        bias=((2 * length, LANES), f32),
        keys=((2 * length, width), bf16),
        values=((2 * length, width), bf16),
        keys_t=((2, width, length), bf16),
        values_t=((2, width, length), bf16),
        queries=((length, width), bf16),
        stat=((HEADS, 8, length), f32),
        deltas=((HEADS, 8, length), f32),
        mixed_parts=((2, width, length), f32),
        combined=((length, width), bf16),
        activated=((length, hidden_units), bf16),
        d_expanded=((length, hidden_units), bf16),
        ff_in=((length, width), bf16),
        d_shrunk=((length, width), bf16),
        d_attended=((length, width), bf16),
        d_combined=((length, width), bf16),
        d_scaled=((2, length, width), bf16),
        d_queries_t=((width, length), f32),
        d_rows_in=((length, width), bf16),
        late_ext=((length + 2 * edge, channels), bf16),
        late_page=((2, 2 * length + edge, LANES), bf16),
        early_page=((2, 2 * length + edge, LANES), bf16),
        page3=((2, 3, 2 * length + edge, LANES), bf16),
        pool=((2 * HEADS * (length // LANES) * (length // 64), 64, LANES), bf16),
        parts=((6, 21, 64, LANES), bf16),
        dense=(dense_shape, bf16),
        dense_parts=(dense_shape, bf16),
        small_sums=((6, 24, width), f32),
        small_parts=((5, 24, width), f32),
        owned=((2, 2, TAPS, channels // 16, LANES), bf16),
        owned_sib=((2, TAPS, channels // 16, LANES), bf16),
    )
    sem_shapes = dict(
        load_sems=(23,),
        out_sems=(5 + len(DENSE),),
        pair_sends=(20,),
        pair_recvs=(20,),
        grad_sends=(3 * len(GRADS),),
        grad_recvs=(4 * len(GRADS),),
        dense_sends=(3 * len(DENSE),),
        dense_recvs=(12 * len(DENSE),),
        small_sends=(5,),
        small_recvs=(5,),
    )
    names = list(inputs) + list(outs) + list(scratch) + list(sem_shapes)
    results = pl.pallas_call(
        functools.partial(page_kernel, side, names),
        out_shape=tuple(jax.ShapeDtypeStruct(*spec) for spec in outs.values()),
        in_specs=[place(array) for array in inputs.values()],
        out_specs=tuple([hbm] * len(outs)),
        scratch_shapes=[pltpu.VMEM(*spec) for spec in scratch.values()]
        + [sems(shape) for shape in sem_shapes.values()],
        compiler_params=pltpu.CompilerParams(
            collective_id=0, has_side_effects=True, vmem_limit_bytes=63 * 1024 * 1024
        ),
        name="page_step",
    )(*inputs.values())
    return SimpleNamespace(**dict(zip(outs, results)))


def unpack_kernel(passed, dense_hbm, small_hbm, *refs):
    f32 = jnp.float32
    through, refs = refs[:passed], refs[passed:]
    through_out, refs = refs[:passed], refs[passed:]
    held, refs = refs[len(refs) - passed :], refs[: len(refs) - passed]
    outs, (dense, wide, small, vector, vector_wide, wide_grads, in_sems, out_sems) = (
        refs[:-8],
        refs[-8:],
    )
    project, project_b, query, query_b, key, value, value_b, output, output_b = outs[:9]
    first_gain, first_shift, expand, expand_b, shrink, shrink_b, final_gain, final_shift = outs[9:]
    width = dense.shape[2]
    copies = []

    def send(source, target):
        copies.append(pltpu.make_async_copy(source, target, out_sems.at[len(copies)]))
        copies[-1].start()

    units = dense.shape[0] // 32
    loads = [pltpu.make_async_copy(small_hbm, small, in_sems.at[0])]
    for unit in range(units):
        at = pl.ds(32 * unit, 32)
        loads.append(
            pltpu.make_async_copy(dense_hbm.at[at], dense.at[at], in_sems.at[len(loads)])
        )
    for source, target in zip(through, held):
        loads.append(pltpu.make_async_copy(source, target, in_sems.at[len(loads)]))
    for load in loads:
        load.start()
    loads[0].wait()
    for number, (row, out) in enumerate(
        (
            (PROJECT, project_b),
            (QUERY, query_b),
            (VALUE, value_b),
            (OUTPUT, output_b),
            (FIRST_GAIN, first_gain),
            (FIRST_SHIFT, first_shift),
            (SHRINK, shrink_b),
            (FINAL_GAIN, final_gain),
            (FINAL_SHIFT, final_shift),
        )
    ):
        vector[pl.ds(number * width, width)] = small[row]
        send(vector.at[pl.ds(number * width, width)], out)
    for piece in range(expand_b.shape[0] // width):
        vector_wide[pl.ds(piece * width, width)] = small[EXPAND + piece]
    send(vector_wide, expand_b)

    def widen(unit):
        loads[1 + unit].wait()
        wide[unit] = dense[pl.ds(32 * unit, 32)].reshape(512, width).astype(f32)
        return wide.at[unit]

    for part in range(4):
        send(widen(part), shrink.at[pl.ds(part * 512, 512)])
        both = widen(4 + part)
        send(both.at[pl.ds(0, width)], expand.at[:, pl.ds(part * 512, width)])
        send(both.at[pl.ds(width, width)], expand.at[:, pl.ds(part * 512 + width, width)])
    for number, (load, source, target) in enumerate(zip(loads[1 + units :], held, through_out)):
        load.wait()
        if source.dtype != target.dtype:
            wide_grads[number % 2] = source[...].astype(f32)
            source = wide_grads.at[number % 2]
        send(source, target)
    both = widen(8)
    send(both.at[pl.ds(0, width)], query)
    send(both.at[pl.ds(width, width)], key)
    both = widen(9)
    send(both.at[pl.ds(0, width)], value)
    send(both.at[pl.ds(width, width)], output)
    send(widen(10), project)
    for copy in copies:
        copy.wait()


def paired_body(
    features,
    quarter_turns,
    heights,
    widths,
    frozen_scale,
    frozen_shift,
    first_kernel,
    second_kernel,
    project_weight,
    project_bias,
    query_weight,
    query_bias,
    key_weight,
    value_weight,
    value_bias,
    output_weight,
    output_bias,
    first_gain,
    first_shift,
    expand_weight,
    expand_bias,
    shrink_weight,
    shrink_bias,
    final_gain,
    final_shift,
    cotangent,
):
    pages, rows, side, channels = features.shape
    width = project_weight.shape[1]
    hidden_units = expand_weight.shape[1]
    length = rows * side
    got = page_call(
        side,
        dict(
            features=features.reshape(length, channels),
            first_kernel=first_kernel.reshape(TAPS, channels, channels),
            second_kernel=second_kernel.reshape(TAPS, channels, channels),
            project_weight=project_weight,
            query_weight=query_weight,
            key_weight=key_weight,
            value_weight=value_weight,
            output_weight=output_weight,
            expand_weight=expand_weight,
            shrink_weight=shrink_weight,
            cotangent=cotangent.reshape(length, width),
            frozen_scale=frozen_scale,
            frozen_shift=frozen_shift,
            project_bias=project_bias,
            query_bias=query_bias,
            value_bias=value_bias,
            output_bias=output_bias,
            first_gain=first_gain,
            first_shift=first_shift,
            expand_bias=expand_bias,
            shrink_bias=shrink_bias,
            final_gain=final_gain,
            final_shift=final_shift,
            quarter_turns=quarter_turns,
            heights=heights,
            widths=widths,
        ),
    )
    f32 = jnp.float32
    square, vector = (width, width), (width,)
    shapes = [
        (channels, width),
        vector,
        square,
        vector,
        square,
        square,
        vector,
        square,
        vector,
        vector,
        vector,
        (width, hidden_units),
        (hidden_units,),
        (hidden_units, width),
        vector,
        vector,
        vector,
    ]
    hbm = pl.BlockSpec(memory_space=pl.ANY)
    passed = (got.encoded, got.features_grad, got.first_grad, got.second_grad)
    dense = got.dense_out
    results = pl.pallas_call(
        functools.partial(unpack_kernel, len(passed)),
        out_shape=tuple(jax.ShapeDtypeStruct(value.shape, f32 if value.ndim == 3 else value.dtype)
            for value in passed)
        + tuple(jax.ShapeDtypeStruct(shape, f32) for shape in shapes),
        in_specs=[hbm] * (2 + len(passed)),
        out_specs=tuple([hbm] * (len(passed) + len(shapes))),
        scratch_shapes=[
            pltpu.VMEM(dense.shape, jnp.bfloat16),
            pltpu.VMEM((dense.shape[0] // 32, 512, width), f32),
            pltpu.VMEM(got.small_out.shape, f32),
            pltpu.VMEM((9 * width,), f32),
            pltpu.VMEM((hidden_units,), f32),
            pltpu.VMEM((2,) + got.first_grad.shape, f32),
            pltpu.SemaphoreType.DMA((1 + dense.shape[0] // 32 + len(passed),)),
            pltpu.SemaphoreType.DMA((32,)),
        ]
        + [pltpu.VMEM(value.shape, value.dtype) for value in passed],
        compiler_params=pltpu.CompilerParams(vmem_limit_bytes=63 * 1024 * 1024),
        name="unpack",
    )(dense, got.small_out, *passed)
    part_shape = (3, 3, channels // 16, channels // 2)
    return (
        results[0].reshape(pages, rows, side, width),
        results[1].reshape(pages, rows, side, channels),
        results[2].reshape(part_shape),
        results[3].reshape(part_shape),
    ) + tuple(results[len(passed) :])


def solution(mesh):
    paired = mesh.shape["strip"] == 2 and mesh.shape["page"] == 16
    return jax.shard_map(
        paired_body if paired else body,
        mesh=mesh,
        in_specs=(
            P("page", "strip", None, None),
            P("page"),
            P("page"),
            P("page"),
            P(),
            P(),
            P(),
            P(),
            P(),
            P(),
            P(),
            P(),
            P(),
            P(),
            P(),
            P(),
            P(),
            P(),
            P(),
            P(),
            P(),
            P(),
            P(),
            P(),
            P(),
            P("page", "strip", None, None),
        ),
        out_specs=(
            P("page", "strip", None, None),
            P("page", "strip", None, None),
            P(None, None, "page", "strip"),
            P(None, None, "page", "strip"),
            P(),
            P(),
            P(),
            P(),
            P(),
            P(),
            P(),
            P(),
            P(),
            P(),
            P(),
            P(),
            P(),
            P(),
            P(),
            P(),
            P(),
        ),
        check_vma=False,
    )
```
